32 devices in a mesh: seq: 16 (over z, x, core), tp: 2 (over y).
Axes of the slice: x: 2, y: 2, z: 4, core: 2. Of those that a mesh axis runs over, the one named last changes fastest.
Arguments:
- stream_x: bfloat16 [2048, 4096], P('seq', 'tp'), may hold values from -6 to 6
- norm_gain: float32 [4096], replicated, may hold values from 0.1 to 1.9
- w_qkv: bfloat16 [4096, 6144], P('seq', 'tp'), may hold values from -0.09375 to 0.09375
- cache_kv: bfloat16 [2, 1024, 1024], P(None, 'seq', 'tp'), may hold values from -400 to 400
- recomp_hidden: bfloat16 [128, 4096], P('seq', 'tp'), may hold values from -6 to 6
- recomp_index: int32 [128], P('seq'), may hold values from 0 to 1023, as said below
- prefix_len: int32 [1], replicated, may hold values from 512 to 1024
Outputs:
- attended: bfloat16 [2048, 4096], P('seq', 'tp')
The draws below stay inside these ranges and needn't reach their ends.
Inputs may be any that keep to these rules, and one draw needn't show every extreme that they name: `recomp_index`: the entries held by index s of seq name distinct cache rows of s * 64 to s * 64 + 63.
All inputs are finite; a program needn't handle non-finite values.
Results may differ from the reference program's by a relative error of at most 0.015.
The reference program's roundings to bfloat16 on the way count: a program that leaves them out, or rounds other values in their place, can miss the bound.
Values may be sent and summed in bfloat16 or wider, within the bound.
No kernel may reach another device: no remote copies, remote signals or barrier semaphores. Data moves between devices by JAX's collectives and lax.ppermute only.
A program may use at most 64 MiB of HBM per device.

```python
import math
import jax
import jax.numpy as jnp
from jax import lax

D = 4096
HEADS = 32
KVH = 8
HD = 128
GROUP = 4
CACHE_DEV = 64
RECOMP_DEV = 8
STREAM = 2048
CACHE = 1024
RECOMP = 128


def draw_recomp_index(key, part):
    blocks = CACHE // CACHE_DEV
    subkeys = jax.random.split(jax.random.fold_in(key, 11), blocks)
    offsets = jax.vmap(lambda k: jax.random.permutation(k, CACHE_DEV)[:RECOMP_DEV])(subkeys)
    base = jnp.arange(blocks, dtype=jnp.int32)[:, None] * CACHE_DEV
    return (offsets.astype(jnp.int32) + base).reshape(-1).astype(jnp.int32)


def draw_cache_kv(key, part):
    base = jax.random.normal(jax.random.fold_in(key, 21), (2, CACHE, KVH * HD), jnp.float32)
    base = jnp.clip(base, -6.0, 6.0)
    return base.astype(jnp.bfloat16)


def shard_levels(own_key, extent, cuts, least, largest):
    factor_of = 1.0
    for dim, parts in cuts:
        steps = jax.random.uniform(jax.random.fold_in(jax.random.fold_in(own_key, 6), dim), (parts,), jnp.float32, least / len(cuts), largest / len(cuts))
        factor_of = factor_of * jnp.repeat(jnp.exp(steps), extent[dim] // parts).reshape((-1,) + (1,) * (len(extent) - 1 - dim))
    return factor_of


def gaussian(key, shape, scale, most, shards=(), kind=jnp.bfloat16):
    level = shard_levels(key, shape, shards, -0.22, 0.18) if shards else 1.0
    values = jax.random.normal(key, shape, jnp.float32) * scale * level
    return jnp.minimum(jnp.maximum(values, -most), most).astype(kind)


def setup_inputs(seed: int = 0) -> dict:
    seeds = jax.random.split(jax.random.key(seed), 8)
    return {
        "stream_x": gaussian(seeds[0], (STREAM, D), 1.0, 6.0, ((0, 16), (1, 2))),
        "norm_gain": jnp.clip(1.0 + 0.18 * jax.random.normal(seeds[1], (D,), jnp.float32), 0.1, 1.9),
        "w_qkv": gaussian(seeds[2], (D, (GROUP + 2) * HD * KVH), D ** -0.5, 0.09375, ((0, 16), (1, 2))),
        "cache_kv": draw_cache_kv(jax.random.fold_in(seeds[7], 71), 0),
        "recomp_hidden": gaussian(seeds[4], (RECOMP, D), 1.0, 6.0, ((0, 16), (1, 2))),
        "recomp_index": draw_recomp_index(jax.random.fold_in(seeds[7], 71), 0),
        "prefix_len": jax.random.randint(seeds[6], (1,), CACHE // 2, CACHE + 1).astype(jnp.int32),
    }


def normed(rows, gain):
    values = rows.astype(jnp.float32)
    spread = lax.optimization_barrier(jnp.mean(values * values, axis=-1, keepdims=True))
    return (values * lax.rsqrt(spread + 1e-05) * gain.astype(jnp.float32)).astype(jnp.bfloat16)

def rotate(values, places):
    half = values.shape[-1] // 2
    freq = jnp.exp(-math.log(1000000.0) * jnp.arange(half, dtype=jnp.float32) * 2.0 / (2 * half))
    angle = places[:, None] * freq[None, :]
    shape = (angle.shape[0],) + (1,) * (values.ndim - 2) + (half,)
    cosine = jnp.cos(angle).reshape(shape)
    sine = jnp.sin(angle).reshape(shape)
    first = values[..., :half]
    second = values[..., half:]
    return jnp.concatenate([first * cosine - second * sine, first * sine + second * cosine], -1)

def reference(stream_x, norm_gain, w_qkv, cache_kv, recomp_hidden, recomp_index, prefix_len):
    group = HEADS // KVH
    normed_x = normed(stream_x, norm_gain)
    normed_h = normed(recomp_hidden, norm_gain)
    proj = jnp.dot(normed_x, w_qkv, preferred_element_type=jnp.float32).reshape(STREAM, KVH, group + 2, HD)
    proj_h = jnp.dot(normed_h, w_qkv, preferred_element_type=jnp.float32).reshape(RECOMP, KVH, group + 2, HD)
    begin = prefix_len[0]
    token_ids = jnp.arange(STREAM, dtype=jnp.int32)
    places = (token_ids + begin).astype(jnp.float32)
    query = rotate(proj[:, :, :group], places).astype(jnp.bfloat16)
    new_keys = rotate(proj[:, :, group], places).astype(jnp.bfloat16)
    new_values = proj[:, :, group + 1].astype(jnp.bfloat16)
    redo_keys = rotate(proj_h[:, :, group], recomp_index.astype(jnp.float32)).astype(jnp.bfloat16)
    redo_values = proj_h[:, :, group + 1].astype(jnp.bfloat16)
    keys_c = cache_kv[0].reshape(CACHE, KVH, HD).at[recomp_index].set(redo_keys)
    values_c = cache_kv[1].reshape(CACHE, KVH, HD).at[recomp_index].set(redo_values)
    all_keys = jnp.transpose(jnp.concatenate([keys_c, new_keys], 0), (1, 0, 2))
    all_values = jnp.transpose(jnp.concatenate([values_c, new_values], 0), (1, 0, 2))
    query_heads = jnp.transpose(query, (1, 0, 2, 3))
    cache_ok = jnp.arange(CACHE, dtype=jnp.int32) < begin
    scale = 1.0 / math.sqrt(HD)
    block = math.gcd(STREAM, 512)

    def one_head(items):
        q_all, key_rows, value_rows = items
        key_f = key_rows.astype(jnp.float32)
        value_f = value_rows.astype(jnp.float32)

        def one_block(index):
            first = index * block
            q_blk = lax.dynamic_slice_in_dim(q_all, first, block, 0).astype(jnp.float32)
            score = jnp.einsum('qhd,nd->hqn', q_blk, key_f) * scale
            rows = first + jnp.arange(block, dtype=jnp.int32)
            stream_ok = token_ids[None, :] <= rows[:, None]
            allowed = jnp.concatenate([jnp.broadcast_to(cache_ok[None, :], (block, CACHE)), stream_ok], 1)
            score = jnp.where(allowed[None], score, -1e+30)
            top = lax.optimization_barrier(jnp.max(score, -1, keepdims=True))
            weights = jnp.where(allowed[None], jnp.exp(score - top), 0.0)
            total = lax.optimization_barrier(jnp.sum(weights, -1))
            mixed = jnp.einsum('hqn,nd->hqd', weights.astype(jnp.bfloat16).astype(jnp.float32), value_f)
            mixed = mixed / total[..., None]
            return jnp.transpose(mixed, (1, 0, 2))
        outs = lax.map(one_block, jnp.arange(STREAM // block, dtype=jnp.int32))
        return outs.reshape(STREAM, group, HD)
    result = lax.map(one_head, (query_heads, all_keys, all_values))
    return jnp.transpose(result, (1, 0, 2, 3)).reshape(STREAM, HEADS * HD).astype(jnp.bfloat16)
```

```python
import functools
import math

import jax
import jax.numpy as jnp
from jax import lax
from jax.experimental import pallas as pl
from jax.experimental.pallas import tpu as pltpu
from jax.sharding import PartitionSpec as P

HEADS = 32
KVH = 8
HD = 128
GROUP = HEADS // KVH
WIDTH = (GROUP + 2) * HD
FEATS = 256
FAR = -1e30
VMEM = pl.BlockSpec(memory_space=pltpu.VMEM)
SMEM = pl.BlockSpec(memory_space=pltpu.SMEM)


def swap(value, axis, size, mask):
    return lax.ppermute(value, axis, [(i, i ^ mask) for i in range(size)])


def norm_kernel(count, *refs):
    parts, gains, outs = refs[:count], refs[count : 2 * count], refs[2 * count :]
    values = [part[...].astype(jnp.float32) for part in parts]
    total = sum(jnp.sum(v * v, axis=-1, keepdims=True) for v in values)
    width = sum(v.shape[1] for v in values)
    factor = lax.rsqrt(total / width + 1e-05)
    for value, gain, out in zip(values, gains, outs):
        rows = (value * factor * gain[...]).astype(jnp.bfloat16)
        for block in range(out.shape[0]):
            out[block] = rows[:, block * FEATS : (block + 1) * FEATS]


def norm(parts, gains):
    rows = parts[0].shape[0]
    return pl.pallas_call(
        functools.partial(norm_kernel, len(parts)),
        out_shape=[
            jax.ShapeDtypeStruct((p.shape[1] // FEATS, rows, FEATS), jnp.bfloat16) for p in parts
        ],
        in_specs=[VMEM] * (2 * len(parts)),
        out_specs=[VMEM] * len(parts),
        compiler_params=pltpu.CompilerParams(vmem_limit_bytes=24 * 2**20),
        name="norm",
    )(*parts, *[g.reshape(1, -1) for g in gains])


def project_kernel(n_x, n_w, tok, *refs):
    x_ids, w_ids = refs[0], refs[1]
    x_parts = refs[2 : 2 + n_x]
    w_parts = refs[2 + n_x : 2 + n_x + n_w]
    cosine, sine, cache, pick, q_out, kv_out, held = refs[2 + n_x + n_w :]
    tile = pl.program_id(0)

    @pl.when(tile == 0)
    def _():
        at = 0
        for part in x_parts:
            for block in range(part.shape[0]):
                held[x_ids[at]] = part[block]
                at += 1

    total = None
    at = 0
    for part in w_parts:
        for block in range(part.shape[0]):
            term = jnp.dot(held[w_ids[at]], part[block], preferred_element_type=jnp.float32)
            total = term if total is None else total + term
            at += 1
    cos_rows, sin_rows = cosine[...], sine[...]

    def rotated(value):
        return value * cos_rows + pltpu.roll(value, HD // 2, 1) * sin_rows

    @pl.when(tile > 0)
    def _():
        for head in range(2):
            turned = rotated(total[:, head * HD : (head + 1) * HD])
            q_out[head] = turned[:tok].astype(jnp.bfloat16)

    @pl.when(tile == 0)
    def _():
        rows = jnp.concatenate([rotated(total[:, :HD]), total[:, HD:]], 1).astype(jnp.bfloat16)
        rows = rows.astype(jnp.float32)
        kv_out[:tok] = rows[:tok].astype(jnp.bfloat16)
        chosen = pick[...]
        fresh = jnp.dot(chosen, rows[tok:], preferred_element_type=jnp.float32, precision=lax.Precision.HIGHEST)
        hit = jnp.sum(chosen, axis=1, keepdims=True) > 0.5
        kept = cache[...].astype(jnp.float32)
        kv_out[tok:] = jnp.where(hit, fresh, kept).astype(jnp.bfloat16)


def project(x_parts, x_ids, w_parts, w_ids, cosine, sine, cache, pick, tok):
    rows = x_parts[0].shape[1]
    blocks = sum(p.shape[0] for p in x_parts)
    span = tok + cache.shape[0]
    full = lambda a: pl.BlockSpec(a.shape, lambda t, n=a.ndim: (0,) * n)
    tiles = WIDTH // FEATS
    w_spec = lambda a: pl.BlockSpec(
        (a.shape[0], FEATS, FEATS), lambda t: (0, 0, lax.rem(t + tiles - 1, tiles))
    )
    return pl.pallas_call(
        functools.partial(project_kernel, len(x_parts), len(w_parts), tok),
        grid=(tiles,),
        out_shape=[
            jax.ShapeDtypeStruct((GROUP, tok, HD), jnp.bfloat16),
            jax.ShapeDtypeStruct((span, 2 * HD), jnp.bfloat16),
        ],
        in_specs=[SMEM, SMEM]
        + [full(a) for a in x_parts]
        + [w_spec(a) for a in w_parts]
        + [full(a) for a in (cosine, sine, cache, pick)],
        out_specs=[
            pl.BlockSpec((2, tok, HD), lambda t: (jnp.maximum(t - 1, 0), 0, 0)),
            pl.BlockSpec((span, 2 * HD), lambda t: (0, 0)),
        ],
        scratch_shapes=[pltpu.VMEM((blocks, rows, FEATS), jnp.bfloat16)],
        compiler_params=pltpu.CompilerParams(vmem_limit_bytes=40 * 2**20),
        cost_estimate=pl.CostEstimate(
            flops=2 * rows * blocks * FEATS * WIDTH,
            bytes_accessed=2 * blocks * FEATS * (WIDTH + rows),
            transcendentals=0,
        ),
        name="project",
    )(x_ids, w_ids, *x_parts, *w_parts, cosine, sine, cache, pick)


def attend_kernel(n_kv, tok, *refs):
    begin_ref, q_ids, kv_ids = refs[:3]
    q_ref = refs[3]
    kv_refs = refs[4 : 4 + n_kv]
    out, top, total, accum = refs[4 + n_kv :]
    begin = begin_ref[0]
    q_id = q_ids[pl.program_id(0)]
    query = q_ref[0].reshape(GROUP * tok, HD)
    scale = math.log2(math.e) / math.sqrt(HD)
    places = [(ref, i) for ref in kv_refs for i in range(ref.shape[0])]
    cache_rows = kv_refs[0].shape[1] - tok
    top[...] = jnp.full(top.shape, FAR, jnp.float32)
    total[...] = jnp.zeros(total.shape, jnp.float32)
    accum[...] = jnp.zeros(accum.shape, jnp.float32)

    def take(keys, values, allowed):
        score = lax.dot_general(
            query, keys, (((1,), (1,)), ((), ())), preferred_element_type=jnp.float32
        )
        score = score * scale
        if allowed is not None:
            score = jnp.where(allowed(score.shape), score, FAR)
        old = top[...]
        new = jnp.maximum(old, jnp.max(score, axis=1, keepdims=True))
        weights = jnp.exp2(score - new)
        keep = jnp.exp2(old - new)
        top[...] = new
        total[...] = total[...] * keep + jnp.sum(weights, axis=1, keepdims=True)
        accum[...] = accum[...] * keep + jnp.dot(
            weights.astype(jnp.bfloat16), values, preferred_element_type=jnp.float32
        )

    at = 0
    while at < len(places):
        group = places[at : at + 4]
        ids = [kv_ids[at + i] for i in range(len(group))]
        at += len(group)
        least = functools.reduce(jnp.minimum, ids)
        most = functools.reduce(jnp.maximum, ids)

        def rows(first, last, group=group):
            keys = jnp.concatenate([ref[i, first:last, :HD] for ref, i in group], 0)
            values = jnp.concatenate([ref[i, first:last, HD:] for ref, i in group], 0)
            return keys, values

        def starts(shape, step, ids=ids):
            column = lax.broadcasted_iota(jnp.int32, shape, 1)
            which = column // step
            first = jnp.zeros(shape, jnp.int32)
            for i, one in enumerate(ids):
                first = jnp.where(which == i, one * step, first)
            return first + column % step

        def causal(shape, starts=starts):
            row = lax.broadcasted_iota(jnp.int32, shape, 0)
            return starts(shape, tok) <= q_id * tok + row % tok

        def prefix(shape, starts=starts):
            return starts(shape, cache_rows) < begin

        @pl.when((most + 1) * cache_rows <= begin)
        def _(rows=rows):
            take(*rows(tok, tok + cache_rows), None)

        @pl.when(((most + 1) * cache_rows > begin) & (least * cache_rows < begin))
        def _(rows=rows, prefix=prefix):
            take(*rows(tok, tok + cache_rows), prefix)

        @pl.when(most < q_id)
        def _(rows=rows):
            take(*rows(0, tok), None)

        @pl.when((most >= q_id) & (least <= q_id))
        def _(rows=rows, causal=causal):
            take(*rows(0, tok), causal)

    mixed = (accum[...] / total[...]).astype(jnp.bfloat16)
    for head in range(GROUP):
        out[0, :, head * HD : (head + 1) * HD] = mixed[head * tok : (head + 1) * tok]


def attend(begin, query, q_ids, kv_parts, kv_ids, tok):
    slots = query.shape[0]
    full = lambda a: pl.BlockSpec(a.shape, lambda t, n=a.ndim: (0,) * n)
    n_rows = sum(a.shape[0] for a in kv_parts) * kv_parts[0].shape[1]
    return pl.pallas_call(
        functools.partial(attend_kernel, len(kv_parts), tok),
        grid=(slots,),
        out_shape=jax.ShapeDtypeStruct((slots, tok, GROUP * HD), jnp.bfloat16),
        in_specs=[SMEM, SMEM, SMEM, pl.BlockSpec((1, GROUP, tok, HD), lambda t: (t, 0, 0, 0))]
        + [full(a) for a in kv_parts],
        out_specs=pl.BlockSpec((1, tok, GROUP * HD), lambda t: (t, 0, 0)),
        scratch_shapes=[
            pltpu.VMEM((GROUP * tok, 1), jnp.float32),
            pltpu.VMEM((GROUP * tok, 1), jnp.float32),
            pltpu.VMEM((GROUP * tok, HD), jnp.float32),
        ],
        compiler_params=pltpu.CompilerParams(vmem_limit_bytes=40 * 2**20),
        cost_estimate=pl.CostEstimate(
            flops=4 * slots * GROUP * tok * n_rows * HD,
            bytes_accessed=4 * n_rows * HD,
            transcendentals=slots * GROUP * tok * n_rows,
        ),
        name="attend",
    )(begin, q_ids, kv_ids, query, *kv_parts)


def per_device(
    seq, tp, stream_x, norm_gain, w_qkv, cache_kv, recomp_hidden, recomp_index, prefix_len
):
    tok, redo = stream_x.shape[0], recomp_hidden.shape[0]
    cache_rows = cache_kv.shape[1]
    heads = w_qkv.shape[1] // WIDTH
    near = seq // heads
    at, side = lax.axis_index("seq"), lax.axis_index("tp")
    plane, inner = at // near, at % near
    begin = prefix_len[0]
    squared = near == 4 and heads == 4 and tp == 2

    def across(value, k):
        return swap(value, "seq", seq, k * near) if k else value

    w_mine = [
        across(lax.dynamic_slice_in_dim(w_qkv, (plane ^ k) * WIDTH, WIDTH, 1), k)
        for k in range(heads)
    ]
    caches = []
    for k in range(heads):
        part = lax.dynamic_slice_in_dim(cache_kv, (plane ^ k) * HD, HD, 2)
        caches.append(across(jnp.concatenate([part[0], part[1]], 1), k))
    index_all = lax.all_gather(recomp_index, "seq", axis=0, tiled=True)

    raw = jnp.concatenate([stream_x, recomp_hidden], 0)
    rows = tok + redo
    part_blocks = raw.shape[1] // FEATS
    block_ids = jnp.arange(part_blocks, dtype=jnp.int32)
    if tp == 2:
        other = swap(raw, "tp", tp, 1)
        wide = raw.shape[1]
        gains = [
            lax.dynamic_slice_in_dim(norm_gain, side * wide, wide),
            lax.dynamic_slice_in_dim(norm_gain, (1 - side) * wide, wide),
        ]
        own, opposite = norm([raw, other], gains)
        x_ids = jnp.concatenate([side * part_blocks + block_ids, (1 - side) * part_blocks + block_ids])
    else:
        whole = lax.all_gather(raw, "tp", axis=1, tiled=True)
        (own,) = norm([whole], [norm_gain])
        opposite = None
        x_ids = jnp.arange(own.shape[0], dtype=jnp.int32)
    if heads == 4:
        middle = [(i * near + j, (3 - i) * near + j) for i in (1, 2) for j in range(near)]
        outward = [(i * near + j, (i * 3 - 3) * near + j) for i in (1, 2) for j in range(near)]
        is_mid = (plane == 1) | (plane == 2)
        first = across(own, 1)
        mid_own = lax.ppermute(own, "seq", middle)
        mid_first = lax.ppermute(first, "seq", middle)
        out_own = lax.ppermute(mid_own, "seq", outward)
        out_first = lax.ppermute(mid_first, "seq", outward)
        chunks = [own, first, jnp.where(is_mid, mid_first, out_own), jnp.where(is_mid, mid_own, out_first)]
    else:
        chunks = [across(own, k) for k in range(heads)]
    if opposite is None:
        x_slots = [[chunk] for chunk in chunks]
    else:
        x_slots = [[own, opposite]] + [[chunk, swap(chunk, "tp", tp, 1)] for chunk in chunks[1:]]

    if squared:
        w_parts, w_ids = [], []
        for pair in (0, 2):
            mine = jnp.stack(w_mine[pair : pair + 2])
            line = swap(mine, "seq", seq, 2)
            both = jnp.concatenate([mine, line], 0)
            far = swap(both, "seq", seq, 1)
            w_parts += [both, far]
            for flip in (0, 1):
                for turn in (0, 2):
                    w_ids += [(plane ^ k) * near + (inner ^ turn ^ flip) for k in (pair, pair + 1)]
        w_ids = jnp.stack(w_ids).astype(jnp.int32)
    else:
        groups = [[i * near + j for j in range(near)] for i in range(heads)]
        gathered = [
            lax.all_gather(w, "seq", axis=0, tiled=True, axis_index_groups=groups) for w in w_mine
        ]
        per = gathered[0].shape[0] // FEATS
        w_parts = [g.reshape(per, FEATS, WIDTH) for g in gathered]
        w_ids = jnp.concatenate(
            [(plane ^ k) * per + jnp.arange(per, dtype=jnp.int32) for k in range(heads)]
        )

    half = HD // 2
    freq = jnp.exp(-math.log(1000000.0) * jnp.arange(half, dtype=jnp.float32) * 2.0 / (2 * half))
    queries, kv_new, q_ids = [], [], []
    for k in range(heads):
        source = (plane ^ k) * near + inner
        q_ids.append(source)
        rows_at = lax.dynamic_slice_in_dim(index_all, source * redo, redo)
        token_ids = source * tok + jnp.arange(tok, dtype=jnp.int32)
        places = jnp.concatenate([token_ids + begin, rows_at]).astype(jnp.float32)
        angle = places[:, None] * freq[None, :]
        cosine, sine = jnp.cos(angle), jnp.sin(angle)
        cosine = jnp.concatenate([cosine, cosine], 1)
        sine = jnp.concatenate([-sine, sine], 1)
        here = source * cache_rows + jnp.arange(cache_rows, dtype=jnp.int32)
        pick = (here[:, None] == rows_at[None, :]).astype(jnp.float32)
        q_one, kv_one = project(
            x_slots[k], x_ids, w_parts, w_ids, cosine, sine, caches[k], pick, tok
        )
        queries.append(q_one)
        kv_new.append(kv_one)
    q_ids = jnp.stack(q_ids).astype(jnp.int32)

    if squared:
        kv_parts, kv_ids = [], []
        for pair in (0, 2):
            mine = jnp.stack(kv_new[pair : pair + 2])
            line = swap(mine, "seq", seq, 2)
            both = jnp.concatenate([mine, line], 0)
            far = swap(both, "seq", seq, 1)
            parts = [both[0:1], both[2:3], far[0:1], far[2:3], both[1:2], both[3:4], far[1:2], far[3:4]]
            kv_parts += [jnp.concatenate(parts, 0)]
            for k in (pair, pair + 1):
                kv_ids += [(plane ^ k) * near + (inner ^ turn) for turn in (0, 2, 1, 3)]
        kv_ids = jnp.stack(kv_ids).astype(jnp.int32)
    else:
        kv_parts = [
            lax.all_gather(kv, "seq", axis=0, tiled=False, axis_index_groups=groups)
            for kv in kv_new
        ]
        kv_ids = jnp.concatenate(
            [(plane ^ k) * near + jnp.arange(near, dtype=jnp.int32) for k in range(heads)]
        )

    mixed = attend(prefix_len, jnp.stack(queries), q_ids, kv_parts, kv_ids, tok)
    back = jnp.stack([across(mixed[k], k) for k in range(heads)])
    columns = [lax.dynamic_index_in_dim(back, plane ^ h, 0, keepdims=False) for h in range(heads)]
    return jnp.concatenate(columns, 1)


def solution(mesh):
    placed = (
        P("seq", "tp"),
        P(),
        P("seq", "tp"),
        P(None, "seq", "tp"),
        P("seq", "tp"),
        P("seq"),
        P(),
    )
    return jax.shard_map(
        functools.partial(per_device, mesh.shape["seq"], mesh.shape["tp"]),
        mesh=mesh,
        in_specs=placed,
        out_specs=P("seq", "tp"),
        check_vma=False,
    )
```

```python
import functools
import math

import jax
import jax.numpy as jnp
from jax import lax
from jax.experimental import pallas as pl
from jax.experimental.pallas import tpu as pltpu
from jax.sharding import PartitionSpec as P

HEADS = 32
KVH = 8
HD = 128
GROUP = HEADS // KVH
WIDTH = (GROUP + 2) * HD
FEATS = 256
FAR = -1e30
VMEM = pl.BlockSpec(memory_space=pltpu.VMEM)
SMEM = pl.BlockSpec(memory_space=pltpu.SMEM)


def swap(value, axis, size, mask):
    return lax.ppermute(value, axis, [(i, i ^ mask) for i in range(size)])


def norm_kernel(count, *refs):
    parts, gains, outs = refs[:count], refs[count : 2 * count], refs[2 * count :]
    values = [part[...].astype(jnp.float32) for part in parts]
    total = sum(jnp.sum(v * v, axis=-1, keepdims=True) for v in values)
    width = sum(v.shape[1] for v in values)
    factor = lax.rsqrt(total / width + 1e-05)
    for value, gain, out in zip(values, gains, outs):
        rows = (value * factor * gain[...]).astype(jnp.bfloat16)
        for block in range(out.shape[0]):
            out[block] = rows[:, block * FEATS : (block + 1) * FEATS]


def norm(parts, gains):
    rows = parts[0].shape[0]
    return pl.pallas_call(
        functools.partial(norm_kernel, len(parts)),
        out_shape=[
            jax.ShapeDtypeStruct((p.shape[1] // FEATS, rows, FEATS), jnp.bfloat16) for p in parts
        ],
        in_specs=[VMEM] * (2 * len(parts)),
        out_specs=[VMEM] * len(parts),
        compiler_params=pltpu.CompilerParams(vmem_limit_bytes=24 * 2**20),
        name="norm",
    )(*parts, *[g.reshape(1, -1) for g in gains])


def project_kernel(n_x, n_w, tok, redo, *refs):
    x_ids, w_ids = refs[0], refs[1]
    x_parts = refs[2 : 2 + n_x]
    w_parts = refs[2 + n_x : 2 + n_x + n_w]
    cosine, sine, cache, q_out, kv_out, held = refs[2 + n_x + n_w :]
    tile = pl.program_id(0)
    span = kv_out.shape[0]
    cache_rows = span - tok

    @pl.when(tile == 0)
    def _():
        at = 0
        for part in x_parts:
            for block in range(part.shape[0]):
                held[x_ids[at]] = part[block]
                at += 1

    total = None
    at = 0
    for part in w_parts:
        for block in range(part.shape[0]):
            term = jnp.dot(held[w_ids[at]], part[block], preferred_element_type=jnp.float32)
            total = term if total is None else total + term
            at += 1

    def rotated(value, first, last):
        turned = pltpu.roll(value, HD // 2, 1)
        return value * cosine[0, first:last] + turned * sine[0, first:last]

    @pl.when(tile > 0)
    def _():
        for head in range(2):
            value = total[:tok, head * HD : (head + 1) * HD]
            q_out[head] = rotated(value, 0, tok).astype(jnp.bfloat16)

    @pl.when(tile == 0)
    def _():
        keys = rotated(total[:tok, :HD], 0, tok)
        kv_out[:tok] = jnp.concatenate([keys, total[:tok, HD:]], 1).astype(jnp.bfloat16)
        offsets = cache[cache_rows : cache_rows + 1, :redo].astype(jnp.float32)
        row = lax.broadcasted_iota(jnp.int32, (cache_rows, redo), 0).astype(jnp.float32)
        chosen = (row == offsets).astype(jnp.float32)
        fresh = jnp.dot(
            chosen,
            total[tok : tok + redo],
            preferred_element_type=jnp.float32,
            precision=lax.Precision.HIGHEST,
        )
        fresh = jnp.concatenate([rotated(fresh[:, :HD], tok, span), fresh[:, HD:]], 1)
        hit = jnp.sum(chosen, axis=1, keepdims=True) > 0.5
        kept = cache[:cache_rows].astype(jnp.float32)
        kv_out[tok:] = jnp.where(hit, fresh, kept).astype(jnp.bfloat16)


def project(slot, x_parts, x_ids, w_parts, w_ids, cosine, sine, cache, tok, redo):
    rows = x_parts[0].shape[1]
    blocks = sum(p.shape[0] for p in x_parts)
    span = cosine.shape[1]
    full = lambda a: pl.BlockSpec(a.shape, lambda t, n=a.ndim: (0,) * n)
    tiles = WIDTH // FEATS
    w_spec = lambda a: pl.BlockSpec(
        (a.shape[0], FEATS, FEATS), lambda t: (0, 0, lax.rem(t + tiles - 1, tiles))
    )
    table = pl.BlockSpec((1, span, HD), lambda t: (slot, 0, 0))
    return pl.pallas_call(
        functools.partial(project_kernel, len(x_parts), len(w_parts), tok, redo),
        grid=(tiles,),
        out_shape=[
            jax.ShapeDtypeStruct((GROUP, tok, HD), jnp.bfloat16),
            jax.ShapeDtypeStruct((span, 2 * HD), jnp.bfloat16),
        ],
        in_specs=[SMEM, SMEM]
        + [full(a) for a in x_parts]
        + [w_spec(a) for a in w_parts]
        + [table, table, full(cache)],
        out_specs=[
            pl.BlockSpec((2, tok, HD), lambda t: (jnp.maximum(t - 1, 0), 0, 0)),
            pl.BlockSpec((span, 2 * HD), lambda t: (0, 0)),
        ],
        scratch_shapes=[pltpu.VMEM((blocks, rows, FEATS), jnp.bfloat16)],
        compiler_params=pltpu.CompilerParams(vmem_limit_bytes=40 * 2**20),
        cost_estimate=pl.CostEstimate(
            flops=2 * rows * blocks * FEATS * WIDTH,
            bytes_accessed=2 * blocks * FEATS * (WIDTH + rows),
            transcendentals=0,
        ),
        name="project",
    )(x_ids, w_ids, *x_parts, *w_parts, cosine, sine, cache)


def attend_kernel(slot, tok, places, *refs):
    begin_ref, q_ids, kv_ids, q_ref = refs[:4]
    kv_refs = refs[4:-5]
    out, scores, top, total, accum = refs[-5:]
    begin = begin_ref[0]
    q_id = q_ids[slot]
    heads = GROUP * tok
    scale = math.log2(math.e) / math.sqrt(HD)
    span = kv_refs[0].shape[1]
    cache_rows = span - tok
    top[...] = jnp.full(top.shape, FAR, jnp.float32)
    total[...] = jnp.zeros(total.shape, jnp.float32)
    accum[...] = jnp.zeros(accum.shape, jnp.float32)

    def score(column, keys, allowed):
        value = lax.dot_general(
            q_ref[...].reshape(heads, HD),
            keys,
            (((1,), (1,)), ((), ())),
            preferred_element_type=jnp.float32,
        )
        if allowed is not None:
            value = jnp.where(allowed(value.shape), value, FAR)
        scores[:, column : column + value.shape[1]] = value
        most = top[...]
        for lane in range(0, value.shape[1], HD):
            most = jnp.maximum(most, value[:, lane : lane + HD])
        top[...] = most

    def mix(column, values):
        weights = []
        some = total[...]
        most = top[...]
        for lane in range(0, values.shape[0], HD):
            part = scores[:, column + lane : column + lane + HD]
            weight = jnp.exp2(part * scale - most)
            some = some + weight
            weights.append(weight.astype(jnp.bfloat16))
        total[...] = some
        accum[...] += jnp.dot(
            jnp.concatenate(weights, 1), values, preferred_element_type=jnp.float32
        )

    pending = []
    for at in range(0, len(places), 4):
        group = places[at : at + 4]
        ids = [kv_ids[at + i] for i in range(len(group))]
        least = functools.reduce(jnp.minimum, ids)
        most = functools.reduce(jnp.maximum, ids)
        base = at * span

        def rows(first, last, half, group=group):
            return jnp.concatenate(
                [kv_refs[n][i, first:last, half * HD : (half + 1) * HD] for n, i in group], 0
            )

        def starts(shape, step, ids=ids):
            column = lax.broadcasted_iota(jnp.int32, shape, 1)
            which = column // step
            first = jnp.zeros(shape, jnp.int32)
            for i, one in enumerate(ids):
                first = jnp.where(which == i, one * step, first)
            return first + column % step

        def causal(shape, starts=starts):
            row = lax.broadcasted_iota(jnp.int32, shape, 0)
            return starts(shape, tok) <= q_id * tok + row % tok

        def prefix(shape, starts=starts):
            return starts(shape, cache_rows) < begin

        shift = len(group) * tok

        @pl.when((most + 1) * cache_rows <= begin)
        def _(rows=rows, base=base):
            score(base + shift, rows(tok, span, 0), None)

        @pl.when(((most + 1) * cache_rows > begin) & (least * cache_rows < begin))
        def _(rows=rows, prefix=prefix, base=base):
            score(base + shift, rows(tok, span, 0), prefix)

        @pl.when(most < q_id)
        def _(rows=rows, base=base):
            score(base, rows(0, tok, 0), None)

        @pl.when((most >= q_id) & (least <= q_id))
        def _(rows=rows, causal=causal, base=base):
            score(base, rows(0, tok, 0), causal)

        pending.append((least * cache_rows < begin, least <= q_id, rows, base, shift))

    peak = jnp.max(top[...], axis=1, keepdims=True) * scale
    top[...] = jnp.broadcast_to(peak, top.shape)
    for cached, streamed, rows, base, shift in pending:

        @pl.when(cached)
        def _(rows=rows, base=base, shift=shift):
            mix(base + shift, rows(tok, span, 1))

        @pl.when(streamed)
        def _(rows=rows, base=base):
            mix(base, rows(0, tok, 1))

    mixed = (accum[...] / jnp.sum(total[...], axis=1, keepdims=True)).astype(jnp.bfloat16)
    for head in range(GROUP):
        out[:, head * HD : (head + 1) * HD] = mixed[head * tok : (head + 1) * tok]


def attend(slot, begin, query, q_ids, kv_parts, places, kv_ids, tok):
    span = kv_parts[0].shape[1]
    n_rows = len(places) * span
    heads = GROUP * tok
    return pl.pallas_call(
        functools.partial(attend_kernel, slot, tok, places),
        out_shape=jax.ShapeDtypeStruct((tok, GROUP * HD), jnp.bfloat16),
        in_specs=[SMEM, SMEM, SMEM] + [VMEM] * (1 + len(kv_parts)),
        out_specs=VMEM,
        scratch_shapes=[
            pltpu.VMEM((heads, n_rows), jnp.float32),
            pltpu.VMEM((heads, HD), jnp.float32),
            pltpu.VMEM((heads, HD), jnp.float32),
            pltpu.VMEM((heads, HD), jnp.float32),
        ],
        compiler_params=pltpu.CompilerParams(vmem_limit_bytes=50 * 2**20),
        cost_estimate=pl.CostEstimate(
            flops=4 * heads * n_rows * HD,
            bytes_accessed=4 * n_rows * HD,
            transcendentals=heads * n_rows,
        ),
        name="attend",
    )(begin, q_ids, kv_ids, query, *kv_parts)


def per_device(
    seq, tp, stream_x, norm_gain, w_qkv, cache_kv, recomp_hidden, recomp_index, prefix_len
):
    tok, redo = stream_x.shape[0], recomp_hidden.shape[0]
    cache_rows = cache_kv.shape[1]
    heads = w_qkv.shape[1] // WIDTH
    near = seq // heads
    at, side = lax.axis_index("seq"), lax.axis_index("tp")
    plane, inner = at // near, at % near
    begin = prefix_len[0]
    squared = near == 4 and heads == 4 and tp == 2

    def across(value, k):
        return swap(value, "seq", seq, k * near) if k else value

    w_mine = [
        across(lax.dynamic_slice_in_dim(w_qkv, (plane ^ k) * WIDTH, WIDTH, 1), k)
        for k in range(heads)
    ]
    offsets = (recomp_index - at * cache_rows).astype(jnp.bfloat16)
    offsets = jnp.pad(offsets[None, :], ((0, 15), (0, 2 * HD - redo)))
    caches = []
    for k in range(heads):
        part = lax.dynamic_slice_in_dim(cache_kv, (plane ^ k) * HD, HD, 2)
        part = jnp.concatenate([part[0], part[1]], 1)
        caches.append(across(jnp.concatenate([part, offsets], 0), k))

    raw = jnp.concatenate([stream_x, recomp_hidden], 0)
    rows = tok + redo
    part_blocks = raw.shape[1] // FEATS
    block_ids = jnp.arange(part_blocks, dtype=jnp.int32)
    if tp == 2:
        other = swap(raw, "tp", tp, 1)
        wide = raw.shape[1]
        gains = [
            lax.dynamic_slice_in_dim(norm_gain, side * wide, wide),
            lax.dynamic_slice_in_dim(norm_gain, (1 - side) * wide, wide),
        ]
        own, opposite = norm([raw, other], gains)
        x_ids = jnp.concatenate([side * part_blocks + block_ids, (1 - side) * part_blocks + block_ids])
    else:
        whole = lax.all_gather(raw, "tp", axis=1, tiled=True)
        (own,) = norm([whole], [norm_gain])
        opposite = None
        x_ids = jnp.arange(own.shape[0], dtype=jnp.int32)
    if heads == 4:
        beyond = across(own, 2)
        chunks = [own, across(own, 1), beyond, across(beyond, 1)]
    else:
        chunks = [across(own, k) for k in range(heads)]
    if opposite is None:
        x_slots = [[chunk] for chunk in chunks]
    else:
        x_slots = [[own, opposite]] + [[chunk, swap(chunk, "tp", tp, 1)] for chunk in chunks[1:]]

    if squared:
        w_parts, w_ids = [], []
        line = [swap(w, "seq", seq, 2) for w in w_mine]
        for pair in (0, 2):
            both = jnp.stack(w_mine[pair : pair + 2] + line[pair : pair + 2])
            far = swap(both, "seq", seq, 1)
            w_parts += [both, far]
            for flip in (0, 1):
                for turn in (0, 2):
                    w_ids += [(plane ^ k) * near + (inner ^ turn ^ flip) for k in (pair, pair + 1)]
        w_ids = jnp.stack(w_ids).astype(jnp.int32)
    else:
        groups = [[i * near + j for j in range(near)] for i in range(heads)]
        gathered = [
            lax.all_gather(w, "seq", axis=0, tiled=True, axis_index_groups=groups) for w in w_mine
        ]
        per = gathered[0].shape[0] // FEATS
        w_parts = [g.reshape(per, FEATS, WIDTH) for g in gathered]
        w_ids = jnp.concatenate(
            [(plane ^ k) * per + jnp.arange(per, dtype=jnp.int32) for k in range(heads)]
        )

    half = HD // 2
    freq = jnp.exp(-math.log(1000000.0) * jnp.arange(half, dtype=jnp.float32) * 2.0 / (2 * half))
    q_ids = jnp.stack([(plane ^ k) * near + inner for k in range(heads)]).astype(jnp.int32)
    token_ids = q_ids[:, None] * tok + jnp.arange(tok, dtype=jnp.int32) + begin
    row_ids = q_ids[:, None] * cache_rows + jnp.arange(cache_rows, dtype=jnp.int32)
    angle = jnp.concatenate([token_ids, row_ids], 1).astype(jnp.float32)[..., None] * freq
    cosine, sine = jnp.cos(angle), jnp.sin(angle)
    cosine = jnp.concatenate([cosine, cosine], -1)
    sine = jnp.concatenate([-sine, sine], -1)
    queries, kv_new = [], []
    for k in range(heads):
        q_one, kv_one = project(
            k, x_slots[k], x_ids, w_parts, w_ids, cosine, sine, caches[k], tok, redo
        )
        queries.append(q_one)
        kv_new.append(kv_one)

    if squared:
        kv_parts, places = [], []
        for slots in ((0, 1, 2), (3,)):
            mine = jnp.stack([kv_new[k] for k in slots])
            line = swap(mine, "seq", seq, 2)
            first = len(kv_parts)
            kv_parts += [mine, line, swap(mine, "seq", seq, 1), swap(line, "seq", seq, 1)]
            places += [(first + n, i) for i in range(len(slots)) for n in range(4)]
        turns = (0, 2, 1, 3)
        kv_ids = jnp.stack([(plane ^ k) * near + (inner ^ turn) for k in range(4) for turn in turns])
        kv_ids = kv_ids.astype(jnp.int32)
    else:
        kv_parts = [
            lax.all_gather(kv, "seq", axis=0, tiled=False, axis_index_groups=groups)
            for kv in kv_new
        ]
        places = [(k, i) for k in range(heads) for i in range(near)]
        kv_ids = jnp.concatenate(
            [(plane ^ k) * near + jnp.arange(near, dtype=jnp.int32) for k in range(heads)]
        )

    back = [None] * heads
    for k in reversed(range(heads)):
        mixed = attend(k, prefix_len, queries[k], q_ids, kv_parts, places, kv_ids, tok)
        back[k] = across(mixed, k)
    back = jnp.stack(back)
    columns = [lax.dynamic_index_in_dim(back, plane ^ h, 0, keepdims=False) for h in range(heads)]
    return jnp.concatenate(columns, 1)


def solution(mesh):
    placed = (
        P("seq", "tp"),
        P(),
        P("seq", "tp"),
        P(None, "seq", "tp"),
        P("seq", "tp"),
        P("seq"),
        P(),
    )
    return jax.shard_map(
        functools.partial(per_device, mesh.shape["seq"], mesh.shape["tp"]),
        mesh=mesh,
        in_specs=placed,
        out_specs=P("seq", "tp"),
        check_vma=False,
    )
```

```python
import functools
import math

import jax
import jax.numpy as jnp
from jax import lax
from jax.experimental import pallas as pl
from jax.experimental.pallas import tpu as pltpu
from jax.sharding import PartitionSpec as P

HEADS = 32
KVH = 8
HD = 128
GROUP = HEADS // KVH
WIDTH = (GROUP + 2) * HD
FEATS = 256
FAR = -1e30
VMEM = pl.BlockSpec(memory_space=pltpu.VMEM)
SMEM = pl.BlockSpec(memory_space=pltpu.SMEM)


def swap(value, axis, size, mask, name="move"):
    with jax.named_scope(name):
        return lax.ppermute(value, axis, [(i, i ^ mask) for i in range(size)])


def after(value, *earlier):
    return lax.optimization_barrier((value,) + earlier)[0]


def squares_kernel(stream, hidden, out):
    tok = stream.shape[0]
    for ref, first in ((stream, 0), (hidden, tok)):
        value = ref[...].astype(jnp.float32)
        total = jnp.sum(value * value, axis=-1, keepdims=True)
        out[first : first + value.shape[0]] = jnp.broadcast_to(total, (value.shape[0], HD))


def squares(stream, hidden):
    return pl.pallas_call(
        squares_kernel,
        out_shape=jax.ShapeDtypeStruct((stream.shape[0] + hidden.shape[0], HD), jnp.float32),
        in_specs=[VMEM] * 2,
        out_specs=VMEM,
        compiler_params=pltpu.CompilerParams(vmem_limit_bytes=8 * 2**20),
        name="squares",
    )(stream, hidden)


def norm_kernel(width, count, stream, hidden, gain, *refs):
    sums, out = refs[:count], refs[count]
    tok = stream.shape[0]
    factor = lax.rsqrt(sum(s[:, :1] for s in sums) / width + 1e-05)
    for ref, first in ((stream, 0), (hidden, tok)):
        last = first + ref.shape[0]
        for block in range(out.shape[0]):
            lanes = slice(block * FEATS, (block + 1) * FEATS)
            value = ref[:, lanes].astype(jnp.float32)
            value = value * factor[first:last] * gain[:, lanes]
            out[block, first:last] = value.astype(jnp.bfloat16)


def norm(stream, hidden, gain, sums, width):
    blocks = stream.shape[1] // FEATS
    rows = stream.shape[0] + hidden.shape[0]
    return pl.pallas_call(
        functools.partial(norm_kernel, width, len(sums)),
        out_shape=jax.ShapeDtypeStruct((blocks, rows, FEATS), jnp.bfloat16),
        in_specs=[VMEM] * (3 + len(sums)),
        out_specs=VMEM,
        compiler_params=pltpu.CompilerParams(vmem_limit_bytes=12 * 2**20),
        name="norm",
    )(stream, hidden, gain.reshape(1, -1), *sums)


def unpack_kernel(plain, packed, fold, *refs):
    sources, outs = refs[: plain + packed], refs[plain + packed :]
    depth = outs[0].shape[1]
    for i, source in enumerate(sources):
        outs[0][i] = source[:depth]
        if i >= plain:
            extra = source.shape[0] - depth
            for j in range(fold):
                lanes = slice(j * 2 * HD, (j + 1) * 2 * HD)
                outs[1 + i - plain][j * extra : (j + 1) * extra] = source[depth:, lanes]


def unpack(plain, packed, depth, fold):
    extra = packed[0].shape[0] - depth
    count = len(plain) + len(packed)
    return pl.pallas_call(
        functools.partial(unpack_kernel, len(plain), len(packed), fold),
        out_shape=[jax.ShapeDtypeStruct((count, depth, WIDTH), jnp.bfloat16)]
        + [jax.ShapeDtypeStruct((fold * extra, 2 * HD), jnp.bfloat16)] * len(packed),
        in_specs=[VMEM] * count,
        out_specs=[VMEM] * (1 + len(packed)),
        compiler_params=pltpu.CompilerParams(vmem_limit_bytes=8 * 2**20),
        cost_estimate=pl.CostEstimate(flops=2 * 10**10, bytes_accessed=10**7, transcendentals=0),
        name="unpack",
    )(*plain, *packed)


def project_kernel(kind, first_slot, tok, redo, pitch, n_x, n_w, *refs):
    x_ids, w_ids = refs[:2]
    x_refs, refs = refs[2 : 2 + sum(n_x)], refs[2 + sum(n_x) :]
    w_refs, refs = refs[:n_w], refs[n_w:]
    chunks = len(n_x)
    cosine, sine, *refs = refs
    caches, (out, held) = refs[:-2], refs[-2:]
    span = cosine.shape[1]
    cache_rows = span - tok

    @pl.when(pl.program_id(0) == 0)
    def _():
        first = 0
        for chunk, count in enumerate(n_x):
            at = 0
            for part in x_refs[first : first + count]:
                for block in range(part.shape[0]):
                    held[x_ids[at], chunk * pitch : chunk * pitch + tok + redo] = part[block]
                    at += 1
            first += count

    total = None
    at = 0
    for part in w_refs:
        for block in range(part.shape[0]):
            term = jnp.dot(held[w_ids[at]], part[block], preferred_element_type=jnp.float32)
            total = term if total is None else total + term
            at += 1

    def rotated(value, chunk, first, last):
        turned = pltpu.roll(value, HD // 2, 1)
        slot = first_slot + chunk
        return value * cosine[slot, first:last] + turned * sine[slot, first:last]

    for chunk in range(chunks):
        mine = total[chunk * pitch : chunk * pitch + tok + redo]
        if kind == "queries":
            for head in range(2):
                value = mine[:tok, head * HD : (head + 1) * HD]
                out[chunk, head] = rotated(value, chunk, 0, tok).astype(jnp.bfloat16)
            continue
        keys = rotated(mine[:tok, :HD], chunk, 0, tok)
        out[chunk, :tok] = jnp.concatenate([keys, mine[:tok, HD:]], 1).astype(jnp.bfloat16)
        cache = caches[chunk]
        offsets = cache[cache_rows : cache_rows + 1, :redo].astype(jnp.float32)
        row = lax.broadcasted_iota(jnp.int32, (cache_rows, redo), 0).astype(jnp.float32)
        chosen = (row == offsets).astype(jnp.float32)
        fresh = jnp.dot(
            chosen,
            mine[tok:],
            preferred_element_type=jnp.float32,
            precision=lax.Precision.HIGHEST,
        )
        turned = rotated(fresh[:, :HD], chunk, tok, span)
        fresh = jnp.concatenate([turned, fresh[:, HD:]], 1)
        hit = jnp.sum(chosen, axis=1, keepdims=True) > 0.5
        kept = cache[:cache_rows].astype(jnp.float32)
        out[chunk, tok:] = jnp.where(hit, fresh, kept).astype(jnp.bfloat16)


def project(kind, first_slot, x_chunks, x_ids, w_parts, w_ids, cosine, sine, caches, tok, redo):
    chunks = len(x_chunks)
    blocks = sum(p.shape[0] for p in x_chunks[0])
    span = cosine.shape[1]
    pitch = -(-(tok + redo) // 16) * 16
    full = lambda a: pl.BlockSpec(a.shape, lambda t, n=a.ndim: (0,) * n)
    tiles, first = (2, 0) if kind == "queries" else (1, 2)
    w_spec = lambda a: pl.BlockSpec((a.shape[0], FEATS, FEATS), lambda t: (0, 0, first + t))
    if kind == "queries":
        out_shape = jax.ShapeDtypeStruct((chunks, GROUP, tok, HD), jnp.bfloat16)
        out_spec = pl.BlockSpec((chunks, 2, tok, HD), lambda t: (0, t, 0, 0))
        caches = []
    else:
        out_shape = jax.ShapeDtypeStruct((chunks, span, 2 * HD), jnp.bfloat16)
        out_spec = full(out_shape)
    x_parts = [p for chunk in x_chunks for p in chunk]
    n_x = [len(chunk) for chunk in x_chunks]
    return pl.pallas_call(
        functools.partial(project_kernel, kind, first_slot, tok, redo, pitch, n_x, len(w_parts)),
        grid=(tiles,),
        out_shape=out_shape,
        in_specs=[SMEM, SMEM]
        + [full(a) for a in x_parts]
        + [w_spec(a) for a in w_parts]
        + [full(a) for a in (cosine, sine, *caches)],
        out_specs=out_spec,
        scratch_shapes=[pltpu.VMEM((blocks, chunks * pitch, FEATS), jnp.bfloat16)],
        compiler_params=pltpu.CompilerParams(vmem_limit_bytes=56 * 2**20),
        cost_estimate=pl.CostEstimate(
            flops=2 * chunks * pitch * blocks * FEATS * FEATS * tiles,
            bytes_accessed=2 * blocks * FEATS * (FEATS * tiles + chunks * pitch),
            transcendentals=0,
        ),
        name=kind,
    )(x_ids, w_ids, *x_parts, *w_parts, cosine, sine, *caches)


def attend_kernel(slot, tok, places, *refs):
    begin_ref, q_ids, kv_ids, q_ref = refs[:4]
    kv_refs = refs[4:-5]
    out, scores, top, total, accum = refs[-5:]
    begin = begin_ref[0]
    q_id = q_ids[slot]
    heads = GROUP * tok
    scale = math.log2(math.e) / math.sqrt(HD)
    span = kv_refs[0].shape[1]
    cache_rows = span - tok
    top[...] = jnp.full(top.shape, FAR, jnp.float32)
    total[...] = jnp.zeros(total.shape, jnp.float32)
    accum[...] = jnp.zeros(accum.shape, jnp.float32)

    def score(column, keys, allowed):
        value = lax.dot_general(
            q_ref[0].reshape(heads, HD),
            keys,
            (((1,), (1,)), ((), ())),
            preferred_element_type=jnp.float32,
        )
        if allowed is not None:
            value = jnp.where(allowed(value.shape), value, FAR)
        scores[:, column : column + value.shape[1]] = value
        most = top[...]
        for lane in range(0, value.shape[1], HD):
            most = jnp.maximum(most, value[:, lane : lane + HD])
        top[...] = most

    def mix(column, values):
        weights = []
        some = total[...]
        most = top[...]
        for lane in range(0, values.shape[0], HD):
            part = scores[:, column + lane : column + lane + HD]
            weight = jnp.exp2(part * scale - most)
            some = some + weight
            weights.append(weight.astype(jnp.bfloat16))
        total[...] = some
        accum[...] += jnp.dot(
            jnp.concatenate(weights, 1), values, preferred_element_type=jnp.float32
        )

    pending = []
    for at in range(0, len(places), 4):
        group = places[at : at + 4]
        ids = [kv_ids[at + i] for i in range(len(group))]
        least = functools.reduce(jnp.minimum, ids)
        most = functools.reduce(jnp.maximum, ids)
        base = at * span

        def rows(first, last, half, group=group):
            return jnp.concatenate(
                [kv_refs[n][i, first:last, half * HD : (half + 1) * HD] for n, i in group], 0
            )

        def starts(shape, step, ids=ids):
            column = lax.broadcasted_iota(jnp.int32, shape, 1)
            which = column // step
            first = jnp.zeros(shape, jnp.int32)
            for i, one in enumerate(ids):
                first = jnp.where(which == i, one * step, first)
            return first + column % step

        def causal(shape, starts=starts):
            row = lax.broadcasted_iota(jnp.int32, shape, 0)
            return starts(shape, tok) <= q_id * tok + row % tok

        def prefix(shape, starts=starts):
            return starts(shape, cache_rows) < begin

        shift = len(group) * tok

        @pl.when((most + 1) * cache_rows <= begin)
        def _(rows=rows, base=base):
            score(base + shift, rows(tok, span, 0), None)

        @pl.when(((most + 1) * cache_rows > begin) & (least * cache_rows < begin))
        def _(rows=rows, prefix=prefix, base=base):
            score(base + shift, rows(tok, span, 0), prefix)

        @pl.when(most < q_id)
        def _(rows=rows, base=base):
            score(base, rows(0, tok, 0), None)

        @pl.when((most >= q_id) & (least <= q_id))
        def _(rows=rows, causal=causal, base=base):
            score(base, rows(0, tok, 0), causal)

        pending.append((least * cache_rows < begin, least <= q_id, rows, base, shift))

    peak = jnp.max(top[...], axis=1, keepdims=True) * scale
    top[...] = jnp.broadcast_to(peak, top.shape)
    for cached, streamed, rows, base, shift in pending:

        @pl.when(cached)
        def _(rows=rows, base=base, shift=shift):
            mix(base + shift, rows(tok, span, 1))

        @pl.when(streamed)
        def _(rows=rows, base=base):
            mix(base, rows(0, tok, 1))

    mixed = (accum[...] / jnp.sum(total[...], axis=1, keepdims=True)).astype(jnp.bfloat16)
    for head in range(GROUP):
        out[:, head * HD : (head + 1) * HD] = mixed[head * tok : (head + 1) * tok]


def attend(slot, begin, queries, index, q_ids, kv_parts, places, kv_ids, tok):
    span = kv_parts[0].shape[1]
    n_rows = len(places) * span
    heads = GROUP * tok
    return pl.pallas_call(
        functools.partial(attend_kernel, slot, tok, places),
        out_shape=jax.ShapeDtypeStruct((tok, GROUP * HD), jnp.bfloat16),
        grid=(1,),
        in_specs=[SMEM, SMEM, SMEM, pl.BlockSpec((1, GROUP, tok, HD), lambda t: (index, 0, 0, 0))]
        + [VMEM] * len(kv_parts),
        out_specs=VMEM,
        scratch_shapes=[
            pltpu.VMEM((heads, n_rows), jnp.float32),
            pltpu.VMEM((heads, HD), jnp.float32),
            pltpu.VMEM((heads, HD), jnp.float32),
            pltpu.VMEM((heads, HD), jnp.float32),
        ],
        compiler_params=pltpu.CompilerParams(vmem_limit_bytes=8 * 2**20 + 5 * heads * n_rows),
        cost_estimate=pl.CostEstimate(
            flops=4 * heads * n_rows * HD,
            bytes_accessed=4 * n_rows * HD,
            transcendentals=heads * n_rows,
        ),
        name="attend",
    )(begin, q_ids, kv_ids, queries, *kv_parts)


def per_device(
    seq, tp, stream_x, norm_gain, w_qkv, cache_kv, recomp_hidden, recomp_index, prefix_len
):
    tok, redo = stream_x.shape[0], recomp_hidden.shape[0]
    cache_rows = cache_kv.shape[1]
    heads = w_qkv.shape[1] // WIDTH
    crew = seq // heads
    at, side = lax.axis_index("seq"), lax.axis_index("tp")
    plane, inner = at // crew, at % crew
    begin = prefix_len[0]
    squared = crew == 4 and heads == 4 and tp == 2

    def across(value, k, name="planes"):
        return swap(value, "seq", seq, k * crew, f"{name}_{k}") if k else value

    w_cut = [lax.dynamic_slice_in_dim(w_qkv, (plane ^ k) * WIDTH, WIDTH, 1) for k in range(heads)]
    stream_x, w_cut = lax.optimization_barrier((stream_x, w_cut))
    sums = squares(stream_x, recomp_hidden)
    wide = stream_x.shape[1]
    width = wide * tp
    gain = lax.dynamic_slice_in_dim(norm_gain, side * wide, wide)
    sums = [sums, swap(sums, "tp", tp, 1, "side_sums")] if squared else [lax.psum(sums, "tp")]
    own = norm(stream_x, recomp_hidden, gain, sums, width)

    offsets = (recomp_index - at * cache_rows).astype(jnp.bfloat16)
    fold = WIDTH // (2 * HD)
    extra = -(-(cache_rows + 1) // (16 * fold)) * 16
    offsets = jnp.pad(offsets[None, :], ((0, fold * extra - cache_rows - 1), (0, 2 * HD - redo)))
    caches = []
    for k in range(heads):
        part = lax.dynamic_slice_in_dim(cache_kv, (plane ^ k) * HD, HD, 2)
        part = jnp.concatenate([part[0], part[1]], 1)
        caches.append(jnp.concatenate([part, offsets], 0))

    def folded(cache):
        return jnp.concatenate([cache[i * extra : (i + 1) * extra] for i in range(fold)], 1)

    half = HD // 2
    freq = jnp.exp(-math.log(1000000.0) * jnp.arange(half, dtype=jnp.float32) * 2.0 / (2 * half))
    q_ids = jnp.stack([(plane ^ k) * crew + inner for k in range(heads)]).astype(jnp.int32)
    token_ids = q_ids[:, None] * tok + jnp.arange(tok, dtype=jnp.int32) + begin
    row_ids = q_ids[:, None] * cache_rows + jnp.arange(cache_rows, dtype=jnp.int32)
    angle = jnp.concatenate([token_ids, row_ids], 1).astype(jnp.float32)[..., None] * freq
    cosine, sine = jnp.cos(angle), jnp.sin(angle)
    cosine = jnp.concatenate([cosine, cosine], -1)
    sine = jnp.concatenate([-sine, sine], -1)

    count = wide // FEATS
    groups = [[i * crew + j for j in range(crew)] for i in range(heads)]
    if squared:

        def sides(value, name):
            return swap(value, "tp", tp, 1, f"side_{name}")

        def line(value, name):
            return swap(value, "seq", seq, 2, f"line_{name}")

        def core(value, name):
            return swap(value, "seq", seq, 1, f"core_{name}")

        depth = w_qkv.shape[0]
        w_sent = [jnp.concatenate([w, folded(c)], 0) for w, c in zip(w_cut, caches)]
        w_own = w_cut[0][None]
        w_1, w_2 = across(w_sent[1], 1, "w"), across(w_sent[2], 2, "w")
        far, next_x = across(own, 2, "x_far"), across(own, 1, "x_next")
        own_side, w_line = sides(own, "own"), line(w_own, "w0")
        w_mid, *cache_mid = unpack([], [w_1, w_2], depth, fold)
        own, own_side, next_x, far, w_mid, cache_mid, w_3, w_line, cosine, sine = (
            lax.optimization_barrier(
                (own, own_side, next_x, far, w_mid, cache_mid, w_sent[3], w_line, cosine, sine)
            )
        )
        w_3 = across(w_3, 3, "w")
        last = across(far, 1, "x_last")
        next_side, far_side = sides(next_x, "next"), sides(far, "far")
        w_mid_line = line(w_mid, "w12")
        w_last, cache_last = unpack([], [w_3], depth, fold)
        w_last_line = line(w_last, "w3")
        last, next_side, far_side, w_last, w_mid, w_mid_line, w_last_line, w_line = (
            lax.optimization_barrier(
                (last, next_side, far_side, w_last, w_mid, w_mid_line, w_last_line, w_line)
            )
        )
        caches = [caches[0], *cache_mid, cache_last]
        last_side = sides(last, "last")
        w_parts = [w_own, w_mid, w_last, w_line, w_mid_line, w_last_line]
        w_parts += [core(w, "w") for w in w_parts]
        x_chunks = [[own, own_side], [next_x, next_side], [far, far_side], [last, last_side]]
        ids = jnp.arange(count, dtype=jnp.int32)
        x_ids = jnp.concatenate([side * count + ids, (1 - side) * count + ids])
        w_ids = [
            (plane ^ k) * crew + (inner ^ turn) for turn in (0, 2, 1, 3) for k in range(heads)
        ]
        w_ids = jnp.stack(w_ids).astype(jnp.int32)
    else:
        caches = [across(c, k) for k, c in enumerate(caches)]
        members = [
            [(i * crew + j) * tp + t for i in range(heads) for t in range(tp)] for j in range(crew)
        ]
        x_all = lax.all_gather(own, ("seq", "tp"), axis=0, tiled=True, axis_index_groups=members)
        x_chunks = [
            [lax.dynamic_slice_in_dim(x_all, (plane ^ k) * count * tp, count * tp)]
            for k in range(heads)
        ]
        x_ids = jnp.arange(count * tp, dtype=jnp.int32)
        gathered = [
            lax.all_gather(across(w, k), "seq", axis=0, tiled=True, axis_index_groups=groups)
            for k, w in enumerate(w_cut)
        ]
        per = gathered[0].shape[0] // FEATS
        w_parts = [g.reshape(per, FEATS, WIDTH) for g in gathered]
        w_ids = jnp.concatenate(
            [(plane ^ k) * per + jnp.arange(per, dtype=jnp.int32) for k in range(heads)]
        )

    def projected(kind, slots):
        chunks = [x_chunks[k] for k in slots]
        some = [caches[k] for k in slots]
        return project(kind, slots[0], chunks, x_ids, w_parts, w_ids, cosine, sine, some, tok, redo)

    calls = ((0, 1, 2), (3,)) if squared else (tuple(range(heads)),)
    kv_new = [projected("keys_values", slots) for slots in calls]
    queries = [projected("queries", slots) for slots in calls]

    if squared:
        kv_parts, places = [], []
        for mine, some in zip(kv_new, queries):
            far = swap(mine, "seq", seq, 2, "kv_line")
            far, some = lax.optimization_barrier((far, some))
            places += [(len(kv_parts) + n, i) for i in range(mine.shape[0]) for n in range(4)]
            kv_parts += [mine, far, core(mine, "kv"), core(far, "kv_line")]
        turns = (0, 2, 1, 3)
        kv_ids = jnp.stack([(plane ^ k) * crew + (inner ^ turn) for k in range(4) for turn in turns])
        kv_ids = kv_ids.astype(jnp.int32)
    else:
        kv_parts = [
            lax.all_gather(kv_new[0][k : k + 1], "seq", axis=0, tiled=True, axis_index_groups=groups)
            for k in range(heads)
        ]
        places = [(k, i) for k in range(heads) for i in range(crew)]
        kv_ids = jnp.concatenate(
            [(plane ^ k) * crew + jnp.arange(crew, dtype=jnp.int32) for k in range(heads)]
        )

    back = [None] * heads
    for k in reversed(range(heads)):
        some, index = (queries[k // 3], k % 3) if squared else (queries[0], k)
        mixed = attend(k, prefix_len, some, index, q_ids, kv_parts, places, kv_ids, tok)
        back[k] = across(mixed, k, "mixed")
    back = jnp.stack(back)
    columns = [lax.dynamic_index_in_dim(back, plane ^ h, 0, keepdims=False) for h in range(heads)]
    return jnp.concatenate(columns, 1)


def solution(mesh):
    placed = (
        P("seq", "tp"),
        P(),
        P("seq", "tp"),
        P(None, "seq", "tp"),
        P("seq", "tp"),
        P("seq"),
        P(),
    )
    return jax.shard_map(
        functools.partial(per_device, mesh.shape["seq"], mesh.shape["tp"]),
        mesh=mesh,
        in_specs=placed,
        out_specs=P("seq", "tp"),
        check_vma=False,
    )
```

```python
import functools
import math

import jax
import jax.numpy as jnp
from jax import lax
from jax.experimental import pallas as pl
from jax.experimental.pallas import tpu as pltpu
from jax.sharding import PartitionSpec as P

HEADS = 32
KVH = 8
HD = 128
GROUP = HEADS // KVH
WIDTH = (GROUP + 2) * HD
FEATS = 256
FAR = -1e30
VMEM = pl.BlockSpec(memory_space=pltpu.VMEM)
SMEM = pl.BlockSpec(memory_space=pltpu.SMEM)


def swap(value, axis, size, mask, name="move"):
    with jax.named_scope(name):
        return lax.ppermute(value, axis, [(i, i ^ mask) for i in range(size)])


def after(value, *earlier):
    return lax.optimization_barrier((value,) + earlier)[0]


def squares_kernel(stream, hidden, out):
    tok = stream.shape[0]
    for ref, first in ((stream, 0), (hidden, tok)):
        value = ref[...].astype(jnp.float32)
        total = jnp.sum(value * value, axis=-1, keepdims=True)
        out[first : first + value.shape[0]] = jnp.broadcast_to(total, (value.shape[0], HD))


def squares(stream, hidden):
    return pl.pallas_call(
        squares_kernel,
        out_shape=jax.ShapeDtypeStruct((stream.shape[0] + hidden.shape[0], HD), jnp.float32),
        in_specs=[VMEM] * 2,
        out_specs=VMEM,
        compiler_params=pltpu.CompilerParams(vmem_limit_bytes=8 * 2**20),
        name="squares",
    )(stream, hidden)


def norm_kernel(width, count, stream, hidden, gain, *refs):
    sums, out = refs[:count], refs[count]
    tok = stream.shape[0]
    factor = lax.rsqrt(sum(s[:, :1] for s in sums) / width + 1e-05)
    for ref, first in ((stream, 0), (hidden, tok)):
        last = first + ref.shape[0]
        for block in range(out.shape[0]):
            lanes = slice(block * FEATS, (block + 1) * FEATS)
            value = ref[:, lanes].astype(jnp.float32)
            value = value * factor[first:last] * gain[:, lanes]
            out[block, first:last] = value.astype(jnp.bfloat16)


def norm(stream, hidden, gain, sums, width):
    blocks = stream.shape[1] // FEATS
    rows = stream.shape[0] + hidden.shape[0]
    return pl.pallas_call(
        functools.partial(norm_kernel, width, len(sums)),
        out_shape=jax.ShapeDtypeStruct((blocks, rows, FEATS), jnp.bfloat16),
        in_specs=[VMEM] * (3 + len(sums)),
        out_specs=VMEM,
        compiler_params=pltpu.CompilerParams(vmem_limit_bytes=12 * 2**20),
        name="norm",
    )(stream, hidden, gain.reshape(1, -1), *sums)


def unpack_kernel(plain, fold, sources, *refs):
    sources, (whole, last, *caches) = refs[:sources], refs[sources:]
    depth = whole.shape[1]
    at = 0
    for n, source in enumerate(sources):
        if n < plain:
            whole[at : at + source.shape[0]] = source[...]
            at += source.shape[0]
            continue
        whole[at] = source[:depth]
        last[n - plain] = source[:depth]
        at += 1
        extra = source.shape[0] - depth
        for j in range(fold):
            lanes = slice(j * 2 * HD, (j + 1) * 2 * HD)
            caches[n - plain][j * extra : (j + 1) * extra] = source[depth:, lanes]


def unpack(plain, packed, depth, fold):
    extra = packed[0].shape[0] - depth
    count = sum(p.shape[0] for p in plain) + len(packed)
    return pl.pallas_call(
        functools.partial(unpack_kernel, len(plain), fold, len(plain) + len(packed)),
        out_shape=[
            jax.ShapeDtypeStruct((n, depth, WIDTH), jnp.bfloat16) for n in (count, len(packed))
        ]
        + [jax.ShapeDtypeStruct((fold * extra, 2 * HD), jnp.bfloat16)] * len(packed),
        in_specs=[VMEM] * (len(plain) + len(packed)),
        out_specs=[VMEM] * (2 + len(packed)),
        compiler_params=pltpu.CompilerParams(vmem_limit_bytes=12 * 2**20),
        cost_estimate=pl.CostEstimate(flops=2 * 10**10, bytes_accessed=10**7, transcendentals=0),
        name="unpack",
    )(*plain, *packed)


def project_kernel(kv, tiles, first_slot, tok, redo, pitch, n_x, n_w, *refs):
    x_ids, w_ids = refs[:2]
    x_refs, refs = refs[2 : 2 + sum(n_x)], refs[2 + sum(n_x) :]
    w_refs, refs = refs[:n_w], refs[n_w:]
    chunks = len(n_x)
    cosine, sine, *refs = refs
    caches, outs, held = refs[: chunks * kv], list(refs[chunks * kv : -1]), refs[-1]
    kv_out = outs.pop(0) if kv else None
    q_out = outs.pop(0) if outs else None
    span = cosine.shape[1]
    cache_rows = span - tok

    @pl.when(pl.program_id(0) == 0)
    def _():
        first = 0
        for chunk, count in enumerate(n_x):
            at = 0
            for part in x_refs[first : first + count]:
                for block in range(part.shape[0]):
                    held[x_ids[at], chunk * pitch : chunk * pitch + tok + redo] = part[block]
                    at += 1
            first += count

    total = None
    at = 0
    for part in w_refs:
        for block in range(part.shape[0]):
            term = jnp.dot(held[w_ids[at]], part[block], preferred_element_type=jnp.float32)
            total = term if total is None else total + term
            at += 1

    def rotated(value, chunk, first, last):
        turned = pltpu.roll(value, HD // 2, 1)
        slot = first_slot + chunk
        return value * cosine[slot, first:last] + turned * sine[slot, first:last]

    def finish_queries():
        for chunk in range(chunks):
            for head in range(2):
                value = total[chunk * pitch : chunk * pitch + tok, head * HD : (head + 1) * HD]
                q_out[chunk, head] = rotated(value, chunk, 0, tok).astype(jnp.bfloat16)

    def finish_kv():
        for chunk in range(chunks):
            mine = total[chunk * pitch : chunk * pitch + tok + redo]
            keys = rotated(mine[:tok, :HD], chunk, 0, tok)
            kv_out[chunk, :tok] = jnp.concatenate([keys, mine[:tok, HD:]], 1).astype(jnp.bfloat16)
            cache = caches[chunk]
            offsets = cache[cache_rows : cache_rows + 1, :redo].astype(jnp.float32)
            row = lax.broadcasted_iota(jnp.int32, (cache_rows, redo), 0).astype(jnp.float32)
            chosen = (row == offsets).astype(jnp.float32)
            fresh = jnp.dot(
                chosen,
                mine[tok:],
                preferred_element_type=jnp.float32,
                precision=lax.Precision.HIGHEST,
            )
            turned = rotated(fresh[:, :HD], chunk, tok, span)
            fresh = jnp.concatenate([turned, fresh[:, HD:]], 1)
            hit = jnp.sum(chosen, axis=1, keepdims=True) > 0.5
            kept = cache[:cache_rows].astype(jnp.float32)
            kv_out[chunk, tok:] = jnp.where(hit, fresh, kept).astype(jnp.bfloat16)

    if kv and tiles > 1:
        pl.when(pl.program_id(0) == 0)(finish_kv)
        pl.when(pl.program_id(0) > 0)(finish_queries)
    elif kv:
        finish_kv()
    else:
        finish_queries()


def project(kv, q, first_slot, x_chunks, x_ids, w_parts, w_ids, cosine, sine, caches, tok, redo):
    chunks = len(x_chunks)
    blocks = sum(p.shape[0] for p in x_chunks[0])
    span = cosine.shape[1]
    pitch = -(-(tok + redo) // 16) * 16
    full = lambda a: pl.BlockSpec(a.shape, lambda t, n=a.ndim: (0,) * n)
    q_tiles = WIDTH // FEATS - 1
    tiles = kv + q * q_tiles
    w_spec = lambda a: pl.BlockSpec(
        (a.shape[0], FEATS, FEATS),
        lambda t: (0, 0, lax.rem(t + q_tiles, q_tiles + 1) if kv else t),
    )
    out_shape, out_specs = [], []
    if kv:
        out_shape.append(jax.ShapeDtypeStruct((chunks, span, 2 * HD), jnp.bfloat16))
        out_specs.append(full(out_shape[0]))
    else:
        caches = []
    if q:
        out_shape.append(jax.ShapeDtypeStruct((chunks, GROUP, tok, HD), jnp.bfloat16))
        out_specs.append(
            pl.BlockSpec((chunks, 2, tok, HD), lambda t: (0, jnp.maximum(t - kv, 0), 0, 0))
        )
    x_parts = [p for chunk in x_chunks for p in chunk]
    n_x = [len(chunk) for chunk in x_chunks]
    return pl.pallas_call(
        functools.partial(project_kernel, kv, tiles, first_slot, tok, redo, pitch, n_x, len(w_parts)),
        grid=(tiles,),
        out_shape=out_shape,
        in_specs=[SMEM, SMEM]
        + [full(a) for a in x_parts]
        + [w_spec(a) for a in w_parts]
        + [full(a) for a in (cosine, sine, *caches)],
        out_specs=out_specs,
        scratch_shapes=[pltpu.VMEM((blocks, chunks * pitch, FEATS), jnp.bfloat16)],
        compiler_params=pltpu.CompilerParams(vmem_limit_bytes=56 * 2**20),
        cost_estimate=pl.CostEstimate(
            flops=2 * chunks * pitch * blocks * FEATS * FEATS * tiles,
            bytes_accessed=2 * blocks * FEATS * (FEATS * tiles + chunks * pitch),
            transcendentals=0,
        ),
        name="_".join(["keys_values"] * kv + ["queries"] * q),
    )(x_ids, w_ids, *x_parts, *w_parts, cosine, sine, *caches)


def attend_kernel(slot, tok, places, *refs):
    begin_ref, q_ids, kv_ids, q_ref = refs[:4]
    kv_refs = refs[4:-5]
    out, scores, top, total, accum = refs[-5:]
    begin = begin_ref[0]
    q_id = q_ids[slot]
    heads = GROUP * tok
    scale = math.log2(math.e) / math.sqrt(HD)
    span = kv_refs[0].shape[1]
    cache_rows = span - tok
    top[...] = jnp.full(top.shape, FAR, jnp.float32)
    total[...] = jnp.zeros(total.shape, jnp.float32)
    accum[...] = jnp.zeros(accum.shape, jnp.float32)

    def score(column, keys, allowed):
        value = lax.dot_general(
            q_ref[0].reshape(heads, HD),
            keys,
            (((1,), (1,)), ((), ())),
            preferred_element_type=jnp.float32,
        )
        if allowed is not None:
            value = jnp.where(allowed(value.shape), value, FAR)
        scores[:, column : column + value.shape[1]] = value
        most = top[...]
        for lane in range(0, value.shape[1], HD):
            most = jnp.maximum(most, value[:, lane : lane + HD])
        top[...] = most

    def mix(column, values):
        weights = []
        some = total[...]
        most = top[...]
        for lane in range(0, values.shape[0], HD):
            part = scores[:, column + lane : column + lane + HD]
            weight = jnp.exp2(part * scale - most)
            some = some + weight
            weights.append(weight.astype(jnp.bfloat16))
        total[...] = some
        accum[...] += jnp.dot(
            jnp.concatenate(weights, 1), values, preferred_element_type=jnp.float32
        )

    pending = []
    for at in range(0, len(places), 4):
        group = places[at : at + 4]
        ids = [kv_ids[at + i] for i in range(len(group))]
        least = functools.reduce(jnp.minimum, ids)
        most = functools.reduce(jnp.maximum, ids)
        base = at * span

        def rows(first, last, half, group=group):
            return jnp.concatenate(
                [kv_refs[n][i, first:last, half * HD : (half + 1) * HD] for n, i in group], 0
            )

        def starts(shape, step, ids=ids):
            column = lax.broadcasted_iota(jnp.int32, shape, 1)
            which = column // step
            first = jnp.zeros(shape, jnp.int32)
            for i, one in enumerate(ids):
                first = jnp.where(which == i, one * step, first)
            return first + column % step

        def causal(shape, starts=starts):
            row = lax.broadcasted_iota(jnp.int32, shape, 0)
            return starts(shape, tok) <= q_id * tok + row % tok

        def prefix(shape, starts=starts):
            return starts(shape, cache_rows) < begin

        shift = len(group) * tok

        @pl.when((most + 1) * cache_rows <= begin)
        def _(rows=rows, base=base):
            score(base + shift, rows(tok, span, 0), None)

        @pl.when(((most + 1) * cache_rows > begin) & (least * cache_rows < begin))
        def _(rows=rows, prefix=prefix, base=base):
            score(base + shift, rows(tok, span, 0), prefix)

        @pl.when(most < q_id)
        def _(rows=rows, base=base):
            score(base, rows(0, tok, 0), None)

        @pl.when((most >= q_id) & (least <= q_id))
        def _(rows=rows, causal=causal, base=base):
            score(base, rows(0, tok, 0), causal)

        pending.append((least * cache_rows < begin, least <= q_id, rows, base, shift))

    peak = jnp.max(top[...], axis=1, keepdims=True) * scale
    top[...] = jnp.broadcast_to(peak, top.shape)
    for cached, streamed, rows, base, shift in pending:

        @pl.when(cached)
        def _(rows=rows, base=base, shift=shift):
            mix(base + shift, rows(tok, span, 1))

        @pl.when(streamed)
        def _(rows=rows, base=base):
            mix(base, rows(0, tok, 1))

    mixed = (accum[...] / jnp.sum(total[...], axis=1, keepdims=True)).astype(jnp.bfloat16)
    for head in range(GROUP):
        out[:, head * HD : (head + 1) * HD] = mixed[head * tok : (head + 1) * tok]


def attend(slot, begin, queries, index, q_ids, kv_parts, places, kv_ids, tok):
    span = kv_parts[0].shape[1]
    n_rows = len(places) * span
    heads = GROUP * tok
    return pl.pallas_call(
        functools.partial(attend_kernel, slot, tok, places),
        out_shape=jax.ShapeDtypeStruct((tok, GROUP * HD), jnp.bfloat16),
        grid=(1,),
        in_specs=[SMEM, SMEM, SMEM, pl.BlockSpec((1, GROUP, tok, HD), lambda t: (index, 0, 0, 0))]
        + [VMEM] * len(kv_parts),
        out_specs=VMEM,
        scratch_shapes=[
            pltpu.VMEM((heads, n_rows), jnp.float32),
            pltpu.VMEM((heads, HD), jnp.float32),
            pltpu.VMEM((heads, HD), jnp.float32),
            pltpu.VMEM((heads, HD), jnp.float32),
        ],
        compiler_params=pltpu.CompilerParams(vmem_limit_bytes=8 * 2**20 + 5 * heads * n_rows),
        cost_estimate=pl.CostEstimate(
            flops=4 * heads * n_rows * HD,
            bytes_accessed=4 * n_rows * HD,
            transcendentals=heads * n_rows,
        ),
        name="attend",
    )(begin, q_ids, kv_ids, queries, *kv_parts)


def per_device(
    seq, tp, stream_x, norm_gain, w_qkv, cache_kv, recomp_hidden, recomp_index, prefix_len
):
    tok, redo = stream_x.shape[0], recomp_hidden.shape[0]
    cache_rows = cache_kv.shape[1]
    heads = w_qkv.shape[1] // WIDTH
    crew = seq // heads
    at, side = lax.axis_index("seq"), lax.axis_index("tp")
    plane, inner = at // crew, at % crew
    begin = prefix_len[0]
    squared = crew == 4 and heads == 4 and tp == 2

    def across(value, k, name="planes"):
        return swap(value, "seq", seq, k * crew, f"{name}_{k}") if k else value

    w_cut = [lax.dynamic_slice_in_dim(w_qkv, (plane ^ k) * WIDTH, WIDTH, 1) for k in range(heads)]
    stream_x, w_cut = lax.optimization_barrier((stream_x, w_cut))
    sums = squares(stream_x, recomp_hidden)
    wide = stream_x.shape[1]
    width = wide * tp
    gain = lax.dynamic_slice_in_dim(norm_gain, side * wide, wide)
    sums = [sums, swap(sums, "tp", tp, 1, "side_sums")] if squared else [lax.psum(sums, "tp")]
    own = norm(stream_x, recomp_hidden, gain, sums, width)

    offsets = (recomp_index - at * cache_rows).astype(jnp.bfloat16)
    fold = WIDTH // (2 * HD)
    extra = -(-(cache_rows + 1) // (16 * fold)) * 16
    offsets = jnp.pad(offsets[None, :], ((0, fold * extra - cache_rows - 1), (0, 2 * HD - redo)))
    caches = []
    for k in range(heads):
        part = lax.dynamic_slice_in_dim(cache_kv, (plane ^ k) * HD, HD, 2)
        part = jnp.concatenate([part[0], part[1]], 1)
        caches.append(jnp.concatenate([part, offsets], 0))

    def folded(cache):
        return jnp.concatenate([cache[i * extra : (i + 1) * extra] for i in range(fold)], 1)

    def tables(plane):
        half = HD // 2
        freq = jnp.exp(
            -math.log(1000000.0) * jnp.arange(half, dtype=jnp.float32) * 2.0 / (2 * half)
        )
        q_ids = jnp.stack([(plane ^ k) * crew + inner for k in range(heads)]).astype(jnp.int32)
        token_ids = q_ids[:, None] * tok + jnp.arange(tok, dtype=jnp.int32) + begin
        row_ids = q_ids[:, None] * cache_rows + jnp.arange(cache_rows, dtype=jnp.int32)
        angle = jnp.concatenate([token_ids, row_ids], 1).astype(jnp.float32)[..., None] * freq
        cosine, sine = jnp.cos(angle), jnp.sin(angle)
        return q_ids, jnp.concatenate([cosine, cosine], -1), jnp.concatenate([-sine, sine], -1)

    count = wide // FEATS
    groups = [[i * crew + j for j in range(crew)] for i in range(heads)]
    if squared:

        def sides(value, name):
            return swap(value, "tp", tp, 1, f"side_{name}")

        def line(value, name):
            return swap(value, "seq", seq, 2, f"line_{name}")

        def core(value, name):
            return swap(value, "seq", seq, 1, f"core_{name}")

        depth = w_qkv.shape[0]
        w_sent = [jnp.concatenate([w, folded(c)], 0) for w, c in zip(w_cut[:3], caches)]
        w_own = w_cut[0][None]
        w_1, w_2 = across(w_sent[1], 1, "w"), across(w_sent[2], 2, "w")
        far, next_x = across(own, 2, "x_far"), across(own, 1, "x_next")
        own_side, w_line = sides(own, "own"), line(after(w_own, w_2), "w0")
        w_some, w_mid, *cache_mid = unpack([w_own], [w_1, w_2], depth, fold)
        late, late_cache, _ = lax.optimization_barrier((plane, caches[3], w_2))
        w_sent_3 = jnp.concatenate([w_cut[3], folded(late_cache)], 0)
        q_ids, cosine, sine = tables(late)
        ids = jnp.arange(count, dtype=jnp.int32)
        x_ids = jnp.concatenate([side * count + ids, (1 - side) * count + ids])
        w_ids = [
            (late ^ k) * crew + (inner ^ turn) for turn in (0, 2, 1, 3) for k in range(heads)
        ]
        w_ids = jnp.stack(w_ids).astype(jnp.int32)
        kv_ids = [(late ^ k) * crew + (inner ^ turn) for k in range(heads) for turn in (0, 2, 1, 3)]
        kv_ids = jnp.stack(kv_ids).astype(jnp.int32)
        numbers = (q_ids, cosine, sine, x_ids, w_ids, kv_ids)
        own, own_side, next_x, far, w_some, w_mid, cache_mid, w_3, w_line, numbers = (
            lax.optimization_barrier(
                (own, own_side, next_x, far, w_some, w_mid, cache_mid, w_sent_3, w_line, numbers)
            )
        )
        q_ids, cosine, sine, x_ids, w_ids, kv_ids = numbers
        next_side, far_side = sides(next_x, "next"), sides(far, "far")
        w_3 = across(w_3, 3, "w")
        last = across(far, 1, "x_last")
        w_mid_line = line(w_mid, "w12")
        w_all, w_last, cache_last = unpack([w_some], [w_3], depth, fold)
        w_last_line = line(w_last, "w3")
        last, next_side, far_side, w_all, w_mid_line, w_last_line, w_line = lax.optimization_barrier(
            (last, next_side, far_side, w_all, w_mid_line, w_last_line, w_line)
        )
        caches = [caches[0], *cache_mid, cache_last]
        last_side = sides(last, "last")
        w_parts = [w_all, w_line, w_mid_line, w_last_line]
        w_parts += [core(w, "w") for w in w_parts]
        x_chunks = [[own, own_side], [next_x, next_side], [far, far_side], [last, last_side]]
    else:
        q_ids, cosine, sine = tables(plane)
        caches = [across(c, k) for k, c in enumerate(caches)]
        members = [
            [(i * crew + j) * tp + t for i in range(heads) for t in range(tp)] for j in range(crew)
        ]
        x_all = lax.all_gather(own, ("seq", "tp"), axis=0, tiled=True, axis_index_groups=members)
        x_chunks = [
            [lax.dynamic_slice_in_dim(x_all, (plane ^ k) * count * tp, count * tp)]
            for k in range(heads)
        ]
        x_ids = jnp.arange(count * tp, dtype=jnp.int32)
        gathered = [
            lax.all_gather(across(w, k), "seq", axis=0, tiled=True, axis_index_groups=groups)
            for k, w in enumerate(w_cut)
        ]
        per = gathered[0].shape[0] // FEATS
        w_parts = [g.reshape(per, FEATS, WIDTH) for g in gathered]
        w_ids = jnp.concatenate(
            [(plane ^ k) * per + jnp.arange(per, dtype=jnp.int32) for k in range(heads)]
        )

    def projected(kv, q, slots):
        chunks = [x_chunks[k] for k in slots]
        some = [caches[k] for k in slots]
        return project(kv, q, slots[0], chunks, x_ids, w_parts, w_ids, cosine, sine, some, tok, redo)

    if squared:
        kv_some, q_some = projected(True, True, (0, 1, 2))
        kv_new, queries = [kv_some, *projected(True, False, (3,))], [q_some]
        x_chunks[3][0] = after(last, kv_new[1])
        queries += projected(False, True, (3,))
    else:
        kv_new, queries = [[value] for value in projected(True, True, tuple(range(heads)))]

    if squared:
        kv_parts, places = [], []
        fars = [swap(mine, "seq", seq, 2, "kv_line") for mine in kv_new]
        fars = lax.optimization_barrier((*fars, queries[1]))
        for mine, far in zip(kv_new, fars):
            places += [(len(kv_parts) + n, i) for i in range(mine.shape[0]) for n in range(4)]
            kv_parts += [mine, far, core(mine, "kv"), core(far, "kv_line")]
    else:
        kv_parts = [
            lax.all_gather(kv_new[0][k : k + 1], "seq", axis=0, tiled=True, axis_index_groups=groups)
            for k in range(heads)
        ]
        places = [(k, i) for k in range(heads) for i in range(crew)]
        kv_ids = jnp.concatenate(
            [(plane ^ k) * crew + jnp.arange(crew, dtype=jnp.int32) for k in range(heads)]
        )

    back = [None] * heads
    for k in reversed(range(heads)):
        some, index = (queries[k // 3], k % 3) if squared else (queries[0], k)
        if k + 2 < heads:
            some = after(some, mixed, back[k + 2])
        elif k + 1 < heads:
            some = after(some, mixed)
        mixed = attend(k, prefix_len, some, index, q_ids, kv_parts, places, kv_ids, tok)
        back[k] = across(mixed, k, "mixed")
    back = jnp.stack(back)
    columns = [lax.dynamic_index_in_dim(back, plane ^ h, 0, keepdims=False) for h in range(heads)]
    return jnp.concatenate(columns, 1)


def solution(mesh):
    placed = (
        P("seq", "tp"),
        P(),
        P("seq", "tp"),
        P(None, "seq", "tp"),
        P("seq", "tp"),
        P("seq"),
        P(),
    )
    return jax.shard_map(
        functools.partial(per_device, mesh.shape["seq"], mesh.shape["tp"]),
        mesh=mesh,
        in_specs=placed,
        out_specs=P("seq", "tp"),
        check_vma=False,
    )
```

```python
import functools
import math

import jax
import jax.numpy as jnp
from jax import lax
from jax.experimental import pallas as pl
from jax.experimental.pallas import tpu as pltpu
from jax.sharding import PartitionSpec as P

HEADS = 32
KVH = 8
HD = 128
GROUP = HEADS // KVH
WIDTH = (GROUP + 2) * HD
FEATS = 256
FAR = -1e30
VMEM = pl.BlockSpec(memory_space=pltpu.VMEM)
SMEM = pl.BlockSpec(memory_space=pltpu.SMEM)


def swap(value, axis, size, mask, name="move"):
    with jax.named_scope(name):
        return lax.ppermute(value, axis, [(i, i ^ mask) for i in range(size)])


def after(value, *earlier):
    return lax.optimization_barrier((value,) + earlier)[0]


def squares_kernel(stream, hidden, out):
    tok = stream.shape[0]
    for ref, first in ((stream, 0), (hidden, tok)):
        value = ref[...].astype(jnp.float32)
        total = jnp.sum(value * value, axis=-1, keepdims=True)
        out[first : first + value.shape[0]] = jnp.broadcast_to(total, (value.shape[0], HD))


def squares(stream, hidden):
    return pl.pallas_call(
        squares_kernel,
        out_shape=jax.ShapeDtypeStruct((stream.shape[0] + hidden.shape[0], HD), jnp.float32),
        in_specs=[VMEM] * 2,
        out_specs=VMEM,
        compiler_params=pltpu.CompilerParams(vmem_limit_bytes=8 * 2**20),
        name="squares",
    )(stream, hidden)


def norm_kernel(width, count, stream, hidden, gain, *refs):
    sums, out = refs[:count], refs[count]
    tok = stream.shape[0]
    factor = lax.rsqrt(sum(s[:, :1] for s in sums) / width + 1e-05)
    for ref, first in ((stream, 0), (hidden, tok)):
        last = first + ref.shape[0]
        for block in range(out.shape[0]):
            lanes = slice(block * FEATS, (block + 1) * FEATS)
            value = ref[:, lanes].astype(jnp.float32)
            value = value * factor[first:last] * gain[:, lanes]
            out[block, first:last] = value.astype(jnp.bfloat16)


def norm(stream, hidden, gain, sums, width):
    blocks = stream.shape[1] // FEATS
    rows = stream.shape[0] + hidden.shape[0]
    return pl.pallas_call(
        functools.partial(norm_kernel, width, len(sums)),
        out_shape=jax.ShapeDtypeStruct((blocks, rows, FEATS), jnp.bfloat16),
        in_specs=[VMEM] * (3 + len(sums)),
        out_specs=VMEM,
        compiler_params=pltpu.CompilerParams(vmem_limit_bytes=12 * 2**20),
        name="norm",
    )(stream, hidden, gain.reshape(1, -1), *sums)


def unpack_kernel(plain, fold, sources, *refs):
    sources, (whole, last, *caches) = refs[:sources], refs[sources:]
    depth = whole.shape[1]
    at = 0
    for n, source in enumerate(sources):
        if n < plain:
            whole[at : at + source.shape[0]] = source[...]
            at += source.shape[0]
            continue
        whole[at] = source[:depth]
        last[n - plain] = source[:depth]
        at += 1
        extra = source.shape[0] - depth
        for j in range(fold):
            lanes = slice(j * 2 * HD, (j + 1) * 2 * HD)
            caches[n - plain][j * extra : (j + 1) * extra] = source[depth:, lanes]


def unpack(plain, packed, depth, fold):
    extra = packed[0].shape[0] - depth
    count = sum(p.shape[0] for p in plain) + len(packed)
    return pl.pallas_call(
        functools.partial(unpack_kernel, len(plain), fold, len(plain) + len(packed)),
        out_shape=[
            jax.ShapeDtypeStruct((n, depth, WIDTH), jnp.bfloat16) for n in (count, len(packed))
        ]
        + [jax.ShapeDtypeStruct((fold * extra, 2 * HD), jnp.bfloat16)] * len(packed),
        in_specs=[VMEM] * (len(plain) + len(packed)),
        out_specs=[VMEM] * (2 + len(packed)),
        compiler_params=pltpu.CompilerParams(vmem_limit_bytes=12 * 2**20),
        cost_estimate=pl.CostEstimate(flops=2 * 10**10, bytes_accessed=10**7, transcendentals=0),
        name="unpack",
    )(*plain, *packed)


def join_kernel(*refs):
    at = 0
    for ref in refs[:-1]:
        refs[-1][at : at + ref.shape[0]] = ref[...]
        at += ref.shape[0]


def join(parts):
    count = sum(p.shape[0] for p in parts)
    return pl.pallas_call(
        join_kernel,
        out_shape=jax.ShapeDtypeStruct((count, *parts[0].shape[1:]), parts[0].dtype),
        in_specs=[VMEM] * len(parts),
        out_specs=VMEM,
        compiler_params=pltpu.CompilerParams(vmem_limit_bytes=12 * 2**20),
        name="join",
    )(*parts)


def half_kernel(value, out):
    out[...] = value[...]


def half(value, index):
    shape = (value.shape[0] // 2, *value.shape[1:])
    return pl.pallas_call(
        half_kernel,
        grid=(1,),
        out_shape=jax.ShapeDtypeStruct(shape, value.dtype),
        in_specs=[pl.BlockSpec(shape, lambda t: (index, 0, 0))],
        out_specs=pl.BlockSpec(shape, lambda t: (0, 0, 0)),
        compiler_params=pltpu.CompilerParams(vmem_limit_bytes=8 * 2**20),
        cost_estimate=pl.CostEstimate(flops=2 * 10**10, bytes_accessed=10**6, transcendentals=0),
        name="half",
    )(value)


def project_kernel(kv, tiles, first_slot, tok, redo, pitch, n_x, n_w, *refs):
    x_ids, w_ids = refs[:2]
    x_refs, refs = refs[2 : 2 + sum(n_x)], refs[2 + sum(n_x) :]
    w_refs, refs = refs[:n_w], refs[n_w:]
    chunks = len(n_x)
    cosine, sine, *refs = refs
    caches, outs, held = refs[: chunks * kv], list(refs[chunks * kv : -1]), refs[-1]
    kv_out = outs.pop(0) if kv else None
    q_out = outs.pop(0) if outs else None
    span = cosine.shape[1]
    cache_rows = span - tok

    @pl.when(pl.program_id(0) == 0)
    def _():
        first = 0
        for chunk, count in enumerate(n_x):
            at = 0
            for part in x_refs[first : first + count]:
                for block in range(part.shape[0]):
                    held[x_ids[at], chunk * pitch : chunk * pitch + tok + redo] = part[block]
                    at += 1
            first += count

    total = None
    at = 0
    for part in w_refs:
        for block in range(part.shape[0]):
            term = jnp.dot(held[w_ids[at]], part[block], preferred_element_type=jnp.float32)
            total = term if total is None else total + term
            at += 1

    def rotated(value, chunk, first, last):
        turned = pltpu.roll(value, HD // 2, 1)
        slot = first_slot + chunk
        return value * cosine[slot, first:last] + turned * sine[slot, first:last]

    def finish_queries():
        for chunk in range(chunks):
            for head in range(2):
                value = total[chunk * pitch : chunk * pitch + tok, head * HD : (head + 1) * HD]
                q_out[chunk, head] = rotated(value, chunk, 0, tok).astype(jnp.bfloat16)

    def finish_kv():
        for chunk in range(chunks):
            mine = total[chunk * pitch : chunk * pitch + tok + redo]
            keys = rotated(mine[:tok, :HD], chunk, 0, tok)
            kv_out[chunk, :tok] = jnp.concatenate([keys, mine[:tok, HD:]], 1).astype(jnp.bfloat16)
            cache = caches[chunk]
            offsets = cache[cache_rows : cache_rows + 1, :redo].astype(jnp.float32)
            row = lax.broadcasted_iota(jnp.int32, (cache_rows, redo), 0).astype(jnp.float32)
            chosen = (row == offsets).astype(jnp.float32)
            fresh = jnp.dot(
                chosen,
                mine[tok:],
                preferred_element_type=jnp.float32,
                precision=lax.Precision.HIGHEST,
            )
            turned = rotated(fresh[:, :HD], chunk, tok, span)
            fresh = jnp.concatenate([turned, fresh[:, HD:]], 1)
            hit = jnp.sum(chosen, axis=1, keepdims=True) > 0.5
            kept = cache[:cache_rows].astype(jnp.float32)
            kv_out[chunk, tok:] = jnp.where(hit, fresh, kept).astype(jnp.bfloat16)

    if kv and tiles > 1:
        pl.when(pl.program_id(0) == 0)(finish_kv)
        pl.when(pl.program_id(0) > 0)(finish_queries)
    elif kv:
        finish_kv()
    else:
        finish_queries()


def project(kv, q, first_slot, x_chunks, x_ids, w_parts, w_ids, cosine, sine, caches, tok, redo):
    chunks = len(x_chunks)
    blocks = sum(p.shape[0] for p in x_chunks[0])
    span = cosine.shape[1]
    pitch = -(-(tok + redo) // 16) * 16
    full = lambda a: pl.BlockSpec(a.shape, lambda t, n=a.ndim: (0,) * n)
    q_tiles = WIDTH // FEATS - 1
    tiles = kv + q * q_tiles
    w_spec = lambda a: pl.BlockSpec(
        (a.shape[0], FEATS, FEATS),
        lambda t: (0, 0, lax.rem(t + q_tiles, q_tiles + 1) if kv else t),
    )
    out_shape, out_specs = [], []
    if kv:
        out_shape.append(jax.ShapeDtypeStruct((chunks, span, 2 * HD), jnp.bfloat16))
        out_specs.append(full(out_shape[0]))
    else:
        caches = []
    if q:
        out_shape.append(jax.ShapeDtypeStruct((chunks, GROUP, tok, HD), jnp.bfloat16))
        out_specs.append(
            pl.BlockSpec((chunks, 2, tok, HD), lambda t: (0, jnp.maximum(t - kv, 0), 0, 0))
        )
    x_parts = [p for chunk in x_chunks for p in chunk]
    n_x = [len(chunk) for chunk in x_chunks]
    return pl.pallas_call(
        functools.partial(project_kernel, kv, tiles, first_slot, tok, redo, pitch, n_x, len(w_parts)),
        grid=(tiles,),
        out_shape=out_shape,
        in_specs=[SMEM, SMEM]
        + [full(a) for a in x_parts]
        + [w_spec(a) for a in w_parts]
        + [full(a) for a in (cosine, sine, *caches)],
        out_specs=out_specs,
        scratch_shapes=[pltpu.VMEM((blocks, chunks * pitch, FEATS), jnp.bfloat16)],
        compiler_params=pltpu.CompilerParams(vmem_limit_bytes=32 * 2**20),
        cost_estimate=pl.CostEstimate(
            flops=2 * chunks * pitch * blocks * FEATS * FEATS * tiles,
            bytes_accessed=2 * blocks * FEATS * (FEATS * tiles + chunks * pitch),
            transcendentals=0,
        ),
        name="_".join(["keys_values"] * kv + ["queries"] * q),
    )(x_ids, w_ids, *x_parts, *w_parts, cosine, sine, *caches)


def attend_kernel(slots, tok, places, *refs):
    begin_ref, q_ids, kv_ids = refs[:3]
    count = len(slots)
    q_refs, refs = refs[3 : 3 + count], refs[3 + count :]
    kv_refs, refs = refs[: -count - 4], refs[-count - 4 :]
    outs, (scores, top, total, accum) = refs[:count], refs[count:]
    begin = begin_ref[0]
    heads = GROUP * tok
    scale = math.log2(math.e) / math.sqrt(HD)
    span = kv_refs[0].shape[1]
    cache_rows = span - tok
    groups = []
    for at in range(0, len(places), 4):
        group = places[at : at + 4]
        ids = [kv_ids[at + i] for i in range(len(group))]
        least, most = functools.reduce(jnp.minimum, ids), functools.reduce(jnp.maximum, ids)
        groups.append((group, ids, least, most, at * span))

    for n, slot in enumerate(slots):
        q_id = q_ids[slot]
        top[...] = jnp.full(top.shape, FAR, jnp.float32)
        total[...] = jnp.zeros(total.shape, jnp.float32)
        accum[...] = jnp.zeros(accum.shape, jnp.float32)

        def rows(group, first, last, half):
            return jnp.concatenate(
                [kv_refs[r][i, first:last, half * HD : (half + 1) * HD] for r, i in group], 0
            )

        def score(column, keys, allowed, n=n):
            value = lax.dot_general(
                q_refs[n][0].reshape(heads, HD),
                keys,
                (((1,), (1,)), ((), ())),
                preferred_element_type=jnp.float32,
            )
            if allowed is not None:
                value = jnp.where(allowed(value.shape), value, FAR)
            scores[:, column : column + value.shape[1]] = value
            most = top[...]
            for lane in range(0, value.shape[1], HD):
                most = jnp.maximum(most, value[:, lane : lane + HD])
            top[...] = most

        def mix(column, values):
            weights = []
            some = total[...]
            most = top[...]
            for lane in range(0, values.shape[0], HD):
                part = scores[:, column + lane : column + lane + HD]
                weight = jnp.exp2(part * scale - most)
                some = some + weight
                weights.append(weight.astype(jnp.bfloat16))
            total[...] = some
            accum[...] += jnp.dot(
                jnp.concatenate(weights, 1), values, preferred_element_type=jnp.float32
            )

        for group, ids, least, most, base in groups:
            shift = len(group) * tok

            def starts(shape, step, ids=ids):
                column = lax.broadcasted_iota(jnp.int32, shape, 1)
                which = column // step
                first = jnp.zeros(shape, jnp.int32)
                for i, one in enumerate(ids):
                    first = jnp.where(which == i, one * step, first)
                return first + column % step

            def causal(shape, starts=starts):
                row = lax.broadcasted_iota(jnp.int32, (shape[0], 1), 0)
                return starts((1, shape[1]), tok) <= q_id * tok + row % tok

            def prefix(shape, starts=starts):
                return starts((1, shape[1]), cache_rows) < begin

            @pl.when((most + 1) * cache_rows <= begin)
            def _(group=group, base=base):
                score(base + shift, rows(group, tok, span, 0), None)

            @pl.when(((most + 1) * cache_rows > begin) & (least * cache_rows < begin))
            def _(group=group, prefix=prefix, base=base):
                score(base + shift, rows(group, tok, span, 0), prefix)

            @pl.when(most < q_id)
            def _(group=group, base=base):
                score(base, rows(group, 0, tok, 0), None)

            @pl.when((most >= q_id) & (least <= q_id))
            def _(group=group, causal=causal, base=base):
                score(base, rows(group, 0, tok, 0), causal)

        peak = jnp.max(top[...], axis=1, keepdims=True) * scale
        top[...] = jnp.broadcast_to(peak, top.shape)
        for group, ids, least, most, base in groups:
            shift = len(group) * tok

            @pl.when(least * cache_rows < begin)
            def _(group=group, base=base):
                mix(base + shift, rows(group, tok, span, 1))

            @pl.when(least <= q_id)
            def _(group=group, base=base):
                mix(base, rows(group, 0, tok, 1))

        mixed = (accum[...] / jnp.sum(total[...], axis=1, keepdims=True)).astype(jnp.bfloat16)
        for head in range(GROUP):
            outs[n][:, head * HD : (head + 1) * HD] = mixed[head * tok : (head + 1) * tok]


def attend(slots, begin, queries, q_ids, kv_parts, places, kv_ids, tok):
    span = kv_parts[0].shape[1]
    n_rows = len(places) * span
    heads = GROUP * tok
    q_specs = [pl.BlockSpec((1, GROUP, tok, HD), lambda t, i=i: (i, 0, 0, 0)) for _, i in queries]
    return pl.pallas_call(
        functools.partial(attend_kernel, slots, tok, places),
        grid=(1,),
        out_shape=[jax.ShapeDtypeStruct((tok, GROUP * HD), jnp.bfloat16)] * len(slots),
        in_specs=[SMEM, SMEM, SMEM] + q_specs + [VMEM] * len(kv_parts),
        out_specs=[VMEM] * len(slots),
        scratch_shapes=[
            pltpu.VMEM((heads, n_rows), jnp.float32),
            pltpu.VMEM((heads, HD), jnp.float32),
            pltpu.VMEM((heads, HD), jnp.float32),
            pltpu.VMEM((heads, HD), jnp.float32),
        ],
        compiler_params=pltpu.CompilerParams(vmem_limit_bytes=8 * 2**20 + 5 * heads * n_rows),
        cost_estimate=pl.CostEstimate(
            flops=4 * len(slots) * heads * n_rows * HD,
            bytes_accessed=4 * n_rows * HD,
            transcendentals=len(slots) * heads * n_rows,
        ),
        name="attend",
    )(begin, q_ids, kv_ids, *[q for q, _ in queries], *kv_parts)


def per_device(
    seq, tp, stream_x, norm_gain, w_qkv, cache_kv, recomp_hidden, recomp_index, prefix_len
):
    tok, redo = stream_x.shape[0], recomp_hidden.shape[0]
    cache_rows = cache_kv.shape[1]
    heads = w_qkv.shape[1] // WIDTH
    crew = seq // heads
    at, side = lax.axis_index("seq"), lax.axis_index("tp")
    plane, inner = at // crew, at % crew
    begin = prefix_len[0]
    squared = crew == 4 and heads == 4 and tp == 2

    def across(value, k, name="planes"):
        return swap(value, "seq", seq, k * crew, f"{name}_{k}") if k else value

    w_cut = [lax.dynamic_slice_in_dim(w_qkv, (plane ^ k) * WIDTH, WIDTH, 1) for k in range(heads)]
    stream_x, w_cut = lax.optimization_barrier((stream_x, w_cut))
    sums = squares(stream_x, recomp_hidden)
    wide = stream_x.shape[1]
    width = wide * tp
    gain = lax.dynamic_slice_in_dim(norm_gain, side * wide, wide)
    sums = [sums, swap(sums, "tp", tp, 1, "side_sums")] if squared else [lax.psum(sums, "tp")]
    own = norm(stream_x, recomp_hidden, gain, sums, width)

    offsets = (recomp_index - at * cache_rows).astype(jnp.bfloat16)
    fold = WIDTH // (2 * HD)
    extra = -(-(cache_rows + 1) // (16 * fold)) * 16
    offsets = jnp.pad(offsets[None, :], ((0, fold * extra - cache_rows - 1), (0, 2 * HD - redo)))
    caches = []
    for k in range(heads):
        part = lax.dynamic_slice_in_dim(cache_kv, (plane ^ k) * HD, HD, 2)
        part = jnp.concatenate([part[0], part[1]], 1)
        caches.append(jnp.concatenate([part, offsets], 0))

    def folded(cache):
        return jnp.concatenate([cache[i * extra : (i + 1) * extra] for i in range(fold)], 1)

    def tables(plane):
        half = HD // 2
        freq = jnp.exp(
            -math.log(1000000.0) * jnp.arange(half, dtype=jnp.float32) * 2.0 / (2 * half)
        )
        q_ids = jnp.stack([(plane ^ k) * crew + inner for k in range(heads)]).astype(jnp.int32)
        token_ids = q_ids[:, None] * tok + jnp.arange(tok, dtype=jnp.int32) + begin
        row_ids = q_ids[:, None] * cache_rows + jnp.arange(cache_rows, dtype=jnp.int32)
        angle = jnp.concatenate([token_ids, row_ids], 1).astype(jnp.float32)[..., None] * freq
        cosine, sine = jnp.cos(angle), jnp.sin(angle)
        return q_ids, jnp.concatenate([cosine, cosine], -1), jnp.concatenate([-sine, sine], -1)

    count = wide // FEATS
    groups = [[i * crew + j for j in range(crew)] for i in range(heads)]
    if squared:

        def sides(value, name):
            return swap(value, "tp", tp, 1, f"side_{name}")

        def line(value, name):
            return swap(value, "seq", seq, 2, f"line_{name}")

        def core(value, name):
            return swap(value, "seq", seq, 1, f"core_{name}")

        depth = w_qkv.shape[0]
        w_sent = [jnp.concatenate([w, folded(c)], 0) for w, c in zip(w_cut[:3], caches)]
        w_own = w_cut[0][None]
        w_1, w_2 = across(w_sent[1], 1, "w"), across(w_sent[2], 2, "w")
        far, next_x = across(after(own, w_2), 2, "x_far"), across(own, 1, "x_next")
        own_side = sides(own, "own")
        w_some, _, cache_2 = unpack([w_own], [w_2], depth, fold)
        w_line = line(w_some, "w02")
        w_some, w_mid, cache_1 = unpack([w_some], [w_1], depth, fold)
        cache_mid = (cache_1, cache_2)
        late, late_cache, _ = lax.optimization_barrier((plane, caches[3], w_2))
        w_sent_3 = jnp.concatenate([w_cut[3], folded(late_cache)], 0)
        q_ids, cosine, sine = tables(late)
        ids = jnp.arange(count, dtype=jnp.int32)
        x_ids = jnp.concatenate([side * count + ids, (1 - side) * count + ids])
        order = ((0, 0), (2, 0), (1, 0), (0, 2), (2, 2), (1, 2), (3, 0), (3, 2))
        w_ids = [(late ^ k) * crew + (inner ^ turn ^ flip) for flip in (0, 1) for k, turn in order]
        w_ids = jnp.stack(w_ids).astype(jnp.int32)
        kv_ids = [(late ^ k) * crew + (inner ^ turn) for k in range(heads) for turn in (0, 2, 1, 3)]
        kv_ids = jnp.stack(kv_ids).astype(jnp.int32)
        numbers = (q_ids, cosine, sine, x_ids, w_ids, kv_ids)
        own, own_side, next_x, far, w_some, w_mid, cache_mid, w_3, w_line, numbers = (
            lax.optimization_barrier(
                (own, own_side, next_x, far, w_some, w_mid, cache_mid, w_sent_3, w_line, numbers)
            )
        )
        q_ids, cosine, sine, x_ids, w_ids, kv_ids = numbers
        next_side, far_side = sides(next_x, "next"), sides(far, "far")
        w_3 = across(w_3, 3, "w")
        last = across(far, 1, "x_last")
        w_mid_line = line(w_mid, "w1")
        w_last, _, cache_last = unpack([], [w_3], depth, fold)
        w_last_line = line(w_last, "w3")
        w_some = join([w_some, w_line, w_mid_line])
        w_some_core = core(w_some, "w")
        last_low, far_high = half(last, 0), half(far_side, 1)
        moved = (last, next_side, far_side, w_last, w_last_line, w_some)
        moved, w_some_core, last_low, far_high = lax.optimization_barrier(
            (moved, w_some_core, last_low, far_high)
        )
        last, next_side, far_side, w_last, w_last_line, w_some = moved
        caches = [caches[0], *cache_mid, cache_last]
        last_side = [sides(last_low, "last"), across(far_high, 1, "x_last_side")]
        w_parts = [w_some, w_last, w_last_line]
        w_parts += [w_some_core, core(w_last, "w3"), core(w_last_line, "w3_line")]
        x_chunks = [[own, own_side], [next_x, next_side], [far, far_side], [last, *last_side]]
    else:
        q_ids, cosine, sine = tables(plane)
        caches = [across(c, k) for k, c in enumerate(caches)]
        members = [
            [(i * crew + j) * tp + t for i in range(heads) for t in range(tp)] for j in range(crew)
        ]
        x_all = lax.all_gather(own, ("seq", "tp"), axis=0, tiled=True, axis_index_groups=members)
        x_chunks = [
            [lax.dynamic_slice_in_dim(x_all, (plane ^ k) * count * tp, count * tp)]
            for k in range(heads)
        ]
        x_ids = jnp.arange(count * tp, dtype=jnp.int32)
        gathered = [
            lax.all_gather(across(w, k), "seq", axis=0, tiled=True, axis_index_groups=groups)
            for k, w in enumerate(w_cut)
        ]
        per = gathered[0].shape[0] // FEATS
        w_parts = [g.reshape(per, FEATS, WIDTH) for g in gathered]
        w_ids = jnp.concatenate(
            [(plane ^ k) * per + jnp.arange(per, dtype=jnp.int32) for k in range(heads)]
        )

    def projected(kv, q, slots):
        chunks = [x_chunks[k] for k in slots]
        some = [caches[k] for k in slots]
        return project(kv, q, slots[0], chunks, x_ids, w_parts, w_ids, cosine, sine, some, tok, redo)

    if squared:
        kv_new = [*projected(True, False, (0, 1, 2)), *projected(True, False, (3,))]
        for chunk in x_chunks:
            chunk[0] = after(chunk[0], kv_new[1])
        queries = [*projected(False, True, (0, 1, 2)), *projected(False, True, (3,))]
    else:
        kv_new, queries = [[value] for value in projected(True, True, tuple(range(heads)))]

    if squared:
        kv_parts, places = [], []
        fars = [swap(mine, "seq", seq, 2, "kv_line") for mine in kv_new]
        fars = lax.optimization_barrier((*fars, queries[1]))
        for mine, far in zip(kv_new, fars):
            places += [(len(kv_parts) + n, i) for i in range(mine.shape[0]) for n in range(4)]
            kv_parts += [mine, far, core(mine, "kv"), core(far, "kv_line")]
    else:
        kv_parts = [
            lax.all_gather(kv_new[0][k : k + 1], "seq", axis=0, tiled=True, axis_index_groups=groups)
            for k in range(heads)
        ]
        places = [(k, i) for k in range(heads) for i in range(crew)]
        kv_ids = jnp.concatenate(
            [(plane ^ k) * crew + jnp.arange(crew, dtype=jnp.int32) for k in range(heads)]
        )

    back = [None] * heads
    for slots in tuple((k,) for k in reversed(range(heads))):
        some = [(queries[k // 3], k % 3) if squared else (queries[0], k) for k in slots]
        if squared and slots != (3,):
            earlier = [value for value in back[slots[0] + 2 :][:1] if value is not None]
            some = [(after(some[0][0], *mixed, *earlier), some[0][1])]
        mixed = attend(slots, prefix_len, some, q_ids, kv_parts, places, kv_ids, tok)
        for k, value in zip(slots, mixed):
            back[k] = across(value, k, "mixed")
    back = jnp.stack(back)
    columns = [lax.dynamic_index_in_dim(back, plane ^ h, 0, keepdims=False) for h in range(heads)]
    return jnp.concatenate(columns, 1)


def solution(mesh):
    placed = (
        P("seq", "tp"),
        P(),
        P("seq", "tp"),
        P(None, "seq", "tp"),
        P("seq", "tp"),
        P("seq"),
        P(),
    )
    return jax.shard_map(
        functools.partial(per_device, mesh.shape["seq"], mesh.shape["tp"]),
        mesh=mesh,
        in_specs=placed,
        out_specs=P("seq", "tp"),
        check_vma=False,
    )
```

```python
import functools
import math

import jax
import jax.numpy as jnp
from jax import lax
from jax.experimental import pallas as pl
from jax.experimental.pallas import tpu as pltpu
from jax.sharding import PartitionSpec as P

HEADS = 32
KVH = 8
HD = 128
GROUP = HEADS // KVH
WIDTH = (GROUP + 2) * HD
FEATS = 256
FAR = -1e30
VMEM = pl.BlockSpec(memory_space=pltpu.VMEM)
SMEM = pl.BlockSpec(memory_space=pltpu.SMEM)


def swap(value, axis, size, mask, name="move"):
    with jax.named_scope(name):
        return lax.ppermute(value, axis, [(i, i ^ mask) for i in range(size)])


def after(value, *earlier):
    return lax.optimization_barrier((value,) + earlier)[0]


def squares_kernel(stream, hidden, out):
    tok = stream.shape[0]
    for ref, first in ((stream, 0), (hidden, tok)):
        value = ref[...].astype(jnp.float32)
        total = jnp.sum(value * value, axis=-1, keepdims=True)
        out[first : first + value.shape[0]] = jnp.broadcast_to(total, (value.shape[0], HD))


def squares(stream, hidden):
    return pl.pallas_call(
        squares_kernel,
        out_shape=jax.ShapeDtypeStruct((stream.shape[0] + hidden.shape[0], HD), jnp.float32),
        in_specs=[VMEM] * 2,
        out_specs=VMEM,
        compiler_params=pltpu.CompilerParams(vmem_limit_bytes=8 * 2**20),
        name="squares",
    )(stream, hidden)


def norm_kernel(width, count, stream, hidden, gain, *refs):
    sums, out = refs[:count], refs[count]
    tok = stream.shape[0]
    factor = lax.rsqrt(sum(s[:, :1] for s in sums) / width + 1e-05)
    for ref, first in ((stream, 0), (hidden, tok)):
        last = first + ref.shape[0]
        for block in range(out.shape[0]):
            lanes = slice(block * FEATS, (block + 1) * FEATS)
            value = ref[:, lanes].astype(jnp.float32)
            value = value * factor[first:last] * gain[:, lanes]
            out[block, first:last] = value.astype(jnp.bfloat16)


def norm(stream, hidden, gain, sums, width):
    blocks = stream.shape[1] // FEATS
    rows = stream.shape[0] + hidden.shape[0]
    return pl.pallas_call(
        functools.partial(norm_kernel, width, len(sums)),
        out_shape=jax.ShapeDtypeStruct((blocks, rows, FEATS), jnp.bfloat16),
        in_specs=[VMEM] * (3 + len(sums)),
        out_specs=VMEM,
        compiler_params=pltpu.CompilerParams(vmem_limit_bytes=12 * 2**20),
        name="norm",
    )(stream, hidden, gain.reshape(1, -1), *sums)


def unpack_kernel(plain, fold, sources, *refs):
    sources, (whole, last, *caches) = refs[:sources], refs[sources:]
    depth = whole.shape[1]
    at = 0
    for n, source in enumerate(sources):
        if n < plain:
            whole[at : at + source.shape[0]] = source[...]
            at += source.shape[0]
            continue
        whole[at] = source[:depth]
        last[n - plain] = source[:depth]
        at += 1
        extra = source.shape[0] - depth
        for j in range(fold):
            lanes = slice(j * 2 * HD, (j + 1) * 2 * HD)
            caches[n - plain][j * extra : (j + 1) * extra] = source[depth:, lanes]


def unpack(plain, packed, depth, fold):
    extra = packed[0].shape[0] - depth
    count = sum(p.shape[0] for p in plain) + len(packed)
    return pl.pallas_call(
        functools.partial(unpack_kernel, len(plain), fold, len(plain) + len(packed)),
        out_shape=[
            jax.ShapeDtypeStruct((n, depth, WIDTH), jnp.bfloat16) for n in (count, len(packed))
        ]
        + [jax.ShapeDtypeStruct((fold * extra, 2 * HD), jnp.bfloat16)] * len(packed),
        in_specs=[VMEM] * (len(plain) + len(packed)),
        out_specs=[VMEM] * (2 + len(packed)),
        compiler_params=pltpu.CompilerParams(vmem_limit_bytes=12 * 2**20),
        cost_estimate=pl.CostEstimate(flops=2 * 10**10, bytes_accessed=10**7, transcendentals=0),
        name="unpack",
    )(*plain, *packed)


def join_kernel(*refs):
    at = 0
    for ref in refs[:-1]:
        refs[-1][at : at + ref.shape[0]] = ref[...]
        at += ref.shape[0]


def join(parts):
    count = sum(p.shape[0] for p in parts)
    return pl.pallas_call(
        join_kernel,
        out_shape=jax.ShapeDtypeStruct((count, *parts[0].shape[1:]), parts[0].dtype),
        in_specs=[VMEM] * len(parts),
        out_specs=VMEM,
        compiler_params=pltpu.CompilerParams(vmem_limit_bytes=12 * 2**20),
        name="join",
    )(*parts)


def half_kernel(value, out):
    out[...] = value[...]


def half(value, index):
    shape = (value.shape[0] // 2, *value.shape[1:])
    return pl.pallas_call(
        half_kernel,
        grid=(1,),
        out_shape=jax.ShapeDtypeStruct(shape, value.dtype),
        in_specs=[pl.BlockSpec(shape, lambda t: (index, 0, 0))],
        out_specs=pl.BlockSpec(shape, lambda t: (0, 0, 0)),
        compiler_params=pltpu.CompilerParams(vmem_limit_bytes=8 * 2**20),
        cost_estimate=pl.CostEstimate(flops=2 * 10**10, bytes_accessed=10**6, transcendentals=0),
        name="half",
    )(value)


def project_kernel(kv, tiles, first_slot, tok, redo, pitch, n_x, n_w, *refs):
    x_ids, w_ids = refs[:2]
    x_refs, refs = refs[2 : 2 + sum(n_x)], refs[2 + sum(n_x) :]
    w_refs, refs = refs[:n_w], refs[n_w:]
    chunks = len(n_x)
    cosine, sine, *refs = refs
    caches, outs, held = refs[: chunks * kv], list(refs[chunks * kv : -1]), refs[-1]
    kv_out = outs.pop(0) if kv else None
    q_out = outs.pop(0) if outs else None
    span = cosine.shape[1]
    cache_rows = span - tok

    @pl.when(pl.program_id(0) == 0)
    def _():
        first = 0
        for chunk, count in enumerate(n_x):
            at = 0
            for part in x_refs[first : first + count]:
                for block in range(part.shape[0]):
                    held[x_ids[at], chunk * pitch : chunk * pitch + tok + redo] = part[block]
                    at += 1
            first += count

    total = None
    at = 0
    for part in w_refs:
        for block in range(part.shape[0]):
            term = jnp.dot(held[w_ids[at]], part[block], preferred_element_type=jnp.float32)
            total = term if total is None else total + term
            at += 1

    def rotated(value, chunk, first, last):
        turned = pltpu.roll(value, HD // 2, 1)
        slot = first_slot + chunk
        return value * cosine[slot, first:last] + turned * sine[slot, first:last]

    def finish_queries():
        for chunk in range(chunks):
            for head in range(2):
                value = total[chunk * pitch : chunk * pitch + tok, head * HD : (head + 1) * HD]
                q_out[chunk, head] = rotated(value, chunk, 0, tok).astype(jnp.bfloat16)

    def finish_kv():
        for chunk in range(chunks):
            mine = total[chunk * pitch : chunk * pitch + tok + redo]
            keys = rotated(mine[:tok, :HD], chunk, 0, tok)
            kv_out[chunk, :tok] = jnp.concatenate([keys, mine[:tok, HD:]], 1).astype(jnp.bfloat16)
            cache = caches[chunk]
            offsets = cache[cache_rows : cache_rows + 1, :redo].astype(jnp.float32)
            row = lax.broadcasted_iota(jnp.int32, (cache_rows, redo), 0).astype(jnp.float32)
            chosen = (row == offsets).astype(jnp.float32)
            fresh = jnp.dot(
                chosen,
                mine[tok:],
                preferred_element_type=jnp.float32,
                precision=lax.Precision.HIGHEST,
            )
            turned = rotated(fresh[:, :HD], chunk, tok, span)
            fresh = jnp.concatenate([turned, fresh[:, HD:]], 1)
            hit = jnp.sum(chosen, axis=1, keepdims=True) > 0.5
            kept = cache[:cache_rows].astype(jnp.float32)
            kv_out[chunk, tok:] = jnp.where(hit, fresh, kept).astype(jnp.bfloat16)

    if kv and tiles > 1:
        pl.when(pl.program_id(0) == 0)(finish_kv)
        pl.when(pl.program_id(0) > 0)(finish_queries)
    elif kv:
        finish_kv()
    else:
        finish_queries()


def project(kv, q, first_slot, x_chunks, x_ids, w_parts, w_ids, cosine, sine, caches, tok, redo):
    chunks = len(x_chunks)
    blocks = sum(p.shape[0] for p in x_chunks[0])
    span = cosine.shape[1]
    pitch = -(-(tok + redo) // 16) * 16
    full = lambda a: pl.BlockSpec(a.shape, lambda t, n=a.ndim: (0,) * n)
    q_tiles = WIDTH // FEATS - 1
    tiles = kv + q * q_tiles
    w_spec = lambda a: pl.BlockSpec(
        (a.shape[0], FEATS, FEATS),
        lambda t: (0, 0, lax.rem(t + q_tiles, q_tiles + 1) if kv else t),
    )
    out_shape, out_specs = [], []
    if kv:
        out_shape.append(jax.ShapeDtypeStruct((chunks, span, 2 * HD), jnp.bfloat16))
        out_specs.append(full(out_shape[0]))
    else:
        caches = []
    if q:
        out_shape.append(jax.ShapeDtypeStruct((chunks, GROUP, tok, HD), jnp.bfloat16))
        out_specs.append(
            pl.BlockSpec((chunks, 2, tok, HD), lambda t: (0, jnp.maximum(t - kv, 0), 0, 0))
        )
    x_parts = [p for chunk in x_chunks for p in chunk]
    n_x = [len(chunk) for chunk in x_chunks]
    return pl.pallas_call(
        functools.partial(project_kernel, kv, tiles, first_slot, tok, redo, pitch, n_x, len(w_parts)),
        grid=(tiles,),
        out_shape=out_shape,
        in_specs=[SMEM, SMEM]
        + [full(a) for a in x_parts]
        + [w_spec(a) for a in w_parts]
        + [full(a) for a in (cosine, sine, *caches)],
        out_specs=out_specs,
        scratch_shapes=[pltpu.VMEM((blocks, chunks * pitch, FEATS), jnp.bfloat16)],
        compiler_params=pltpu.CompilerParams(vmem_limit_bytes=32 * 2**20),
        cost_estimate=pl.CostEstimate(
            flops=2 * chunks * pitch * blocks * FEATS * FEATS * tiles,
            bytes_accessed=2 * blocks * FEATS * (FEATS * tiles + chunks * pitch),
            transcendentals=0,
        ),
        name="_".join(["keys_values"] * kv + ["queries"] * q),
    )(x_ids, w_ids, *x_parts, *w_parts, cosine, sine, *caches)


def attend_kernel(slots, tok, places, *refs):
    begin_ref, q_ids, kv_ids = refs[:3]
    count = len(slots)
    q_refs, refs = refs[3 : 3 + count], refs[3 + count :]
    kv_refs, refs = refs[: -count - 4], refs[-count - 4 :]
    outs, (scores, top, total, accum) = refs[:count], refs[count:]
    begin = begin_ref[0]
    heads = GROUP * tok
    scale = math.log2(math.e) / math.sqrt(HD)
    span = kv_refs[0].shape[1]
    cache_rows = span - tok
    groups = []
    for at in range(0, len(places), 4):
        group = places[at : at + 4]
        ids = [kv_ids[at + i] for i in range(len(group))]
        least, most = functools.reduce(jnp.minimum, ids), functools.reduce(jnp.maximum, ids)
        groups.append((group, ids, least, most, at * span))

    for n, slot in enumerate(slots):
        q_id = q_ids[slot]
        top[...] = jnp.full(top.shape, FAR, jnp.float32)
        total[...] = jnp.zeros(total.shape, jnp.float32)
        accum[...] = jnp.zeros(accum.shape, jnp.float32)

        def rows(group, first, last, half):
            return jnp.concatenate(
                [kv_refs[r][i, first:last, half * HD : (half + 1) * HD] for r, i in group], 0
            )

        def score(column, keys, allowed, n=n):
            value = lax.dot_general(
                q_refs[n][0].reshape(heads, HD),
                keys,
                (((1,), (1,)), ((), ())),
                preferred_element_type=jnp.float32,
            )
            if allowed is not None:
                value = jnp.where(allowed(value.shape), value, FAR)
            scores[:, column : column + value.shape[1]] = value
            most = top[...]
            for lane in range(0, value.shape[1], HD):
                most = jnp.maximum(most, value[:, lane : lane + HD])
            top[...] = most

        def mix(column, values):
            weights = []
            some = total[...]
            most = top[...]
            for lane in range(0, values.shape[0], HD):
                part = scores[:, column + lane : column + lane + HD]
                weight = jnp.exp2(part * scale - most)
                some = some + weight
                weights.append(weight.astype(jnp.bfloat16))
            total[...] = some
            accum[...] += jnp.dot(
                jnp.concatenate(weights, 1), values, preferred_element_type=jnp.float32
            )

        for group, ids, least, most, base in groups:
            shift = len(group) * tok

            def starts(shape, step, ids=ids):
                column = lax.broadcasted_iota(jnp.int32, shape, 1)
                which = column // step
                first = jnp.zeros(shape, jnp.int32)
                for i, one in enumerate(ids):
                    first = jnp.where(which == i, one * step, first)
                return first + column % step

            def causal(shape, starts=starts):
                row = lax.broadcasted_iota(jnp.int32, (shape[0], 1), 0)
                return starts((1, shape[1]), tok) <= q_id * tok + row % tok

            def prefix(shape, starts=starts):
                return starts((1, shape[1]), cache_rows) < begin

            @pl.when((most + 1) * cache_rows <= begin)
            def _(group=group, base=base):
                score(base + shift, rows(group, tok, span, 0), None)

            @pl.when(((most + 1) * cache_rows > begin) & (least * cache_rows < begin))
            def _(group=group, prefix=prefix, base=base):
                score(base + shift, rows(group, tok, span, 0), prefix)

            @pl.when(most < q_id)
            def _(group=group, base=base):
                score(base, rows(group, 0, tok, 0), None)

            @pl.when((most >= q_id) & (least <= q_id))
            def _(group=group, causal=causal, base=base):
                score(base, rows(group, 0, tok, 0), causal)

        peak = jnp.max(top[...], axis=1, keepdims=True) * scale
        top[...] = jnp.broadcast_to(peak, top.shape)
        for group, ids, least, most, base in groups:
            shift = len(group) * tok

            @pl.when(least * cache_rows < begin)
            def _(group=group, base=base):
                mix(base + shift, rows(group, tok, span, 1))

            @pl.when(least <= q_id)
            def _(group=group, base=base):
                mix(base, rows(group, 0, tok, 1))

        mixed = (accum[...] / jnp.sum(total[...], axis=1, keepdims=True)).astype(jnp.bfloat16)
        for head in range(GROUP):
            outs[n][:, head * HD : (head + 1) * HD] = mixed[head * tok : (head + 1) * tok]


def attend(slots, begin, queries, q_ids, kv_parts, places, kv_ids, tok):
    span = kv_parts[0].shape[1]
    n_rows = len(places) * span
    heads = GROUP * tok
    q_specs = [pl.BlockSpec((1, GROUP, tok, HD), lambda t, i=i: (i, 0, 0, 0)) for _, i in queries]
    return pl.pallas_call(
        functools.partial(attend_kernel, slots, tok, places),
        grid=(1,),
        out_shape=[jax.ShapeDtypeStruct((tok, GROUP * HD), jnp.bfloat16)] * len(slots),
        in_specs=[SMEM, SMEM, SMEM] + q_specs + [VMEM] * len(kv_parts),
        out_specs=[VMEM] * len(slots),
        scratch_shapes=[
            pltpu.VMEM((heads, n_rows), jnp.float32),
            pltpu.VMEM((heads, HD), jnp.float32),
            pltpu.VMEM((heads, HD), jnp.float32),
            pltpu.VMEM((heads, HD), jnp.float32),
        ],
        compiler_params=pltpu.CompilerParams(vmem_limit_bytes=8 * 2**20 + 5 * heads * n_rows),
        cost_estimate=pl.CostEstimate(
            flops=4 * len(slots) * heads * n_rows * HD,
            bytes_accessed=4 * n_rows * HD,
            transcendentals=len(slots) * heads * n_rows,
        ),
        name="attend",
    )(begin, q_ids, kv_ids, *[q for q, _ in queries], *kv_parts)


def per_device(
    seq, tp, stream_x, norm_gain, w_qkv, cache_kv, recomp_hidden, recomp_index, prefix_len
):
    tok, redo = stream_x.shape[0], recomp_hidden.shape[0]
    cache_rows = cache_kv.shape[1]
    heads = w_qkv.shape[1] // WIDTH
    crew = seq // heads
    at, side = lax.axis_index("seq"), lax.axis_index("tp")
    plane, inner = at // crew, at % crew
    begin = prefix_len[0]
    squared = crew == 4 and heads == 4 and tp == 2

    def across(value, k, name="planes"):
        return swap(value, "seq", seq, k * crew, f"{name}_{k}") if k else value

    w_cut = [lax.dynamic_slice_in_dim(w_qkv, (plane ^ k) * WIDTH, WIDTH, 1) for k in range(heads)]
    stream_x, w_cut = lax.optimization_barrier((stream_x, w_cut))
    sums = squares(stream_x, recomp_hidden)
    wide = stream_x.shape[1]
    width = wide * tp
    gain = lax.dynamic_slice_in_dim(norm_gain, side * wide, wide)
    sums = [sums, swap(sums, "tp", tp, 1, "side_sums")] if squared else [lax.psum(sums, "tp")]
    own = norm(stream_x, recomp_hidden, gain, sums, width)

    offsets = (recomp_index - at * cache_rows).astype(jnp.bfloat16)
    fold = WIDTH // (2 * HD)
    extra = -(-(cache_rows + 1) // (16 * fold)) * 16
    offsets = jnp.pad(offsets[None, :], ((0, fold * extra - cache_rows - 1), (0, 2 * HD - redo)))
    caches = []
    for k in range(heads):
        part = lax.dynamic_slice_in_dim(cache_kv, (plane ^ k) * HD, HD, 2)
        part = jnp.concatenate([part[0], part[1]], 1)
        caches.append(jnp.concatenate([part, offsets], 0))

    def folded(cache):
        return jnp.concatenate([cache[i * extra : (i + 1) * extra] for i in range(fold)], 1)

    def tables(plane):
        half = HD // 2
        freq = jnp.exp(
            -math.log(1000000.0) * jnp.arange(half, dtype=jnp.float32) * 2.0 / (2 * half)
        )
        q_ids = jnp.stack([(plane ^ k) * crew + inner for k in range(heads)]).astype(jnp.int32)
        token_ids = q_ids[:, None] * tok + jnp.arange(tok, dtype=jnp.int32) + begin
        row_ids = q_ids[:, None] * cache_rows + jnp.arange(cache_rows, dtype=jnp.int32)
        angle = jnp.concatenate([token_ids, row_ids], 1).astype(jnp.float32)[..., None] * freq
        cosine, sine = jnp.cos(angle), jnp.sin(angle)
        return q_ids, jnp.concatenate([cosine, cosine], -1), jnp.concatenate([-sine, sine], -1)

    count = wide // FEATS
    groups = [[i * crew + j for j in range(crew)] for i in range(heads)]
    if squared:

        def sides(value, name):
            return swap(value, "tp", tp, 1, f"side_{name}")

        def line(value, name):
            return swap(value, "seq", seq, 2, f"line_{name}")

        def core(value, name):
            return swap(value, "seq", seq, 1, f"core_{name}")

        depth = w_qkv.shape[0]
        w_sent = [jnp.concatenate([w, folded(c)], 0) for w, c in zip(w_cut[:3], caches)]
        w_own = w_cut[0][None]
        w_1, w_2 = across(w_sent[1], 1, "w"), across(w_sent[2], 2, "w")
        far, next_x = across(after(own, w_2), 2, "x_far"), across(own, 1, "x_next")
        own_side = sides(own, "own")
        w_some, _, cache_2 = unpack([w_own], [w_2], depth, fold)
        w_line = line(w_some, "w02")
        w_some, w_mid, cache_1 = unpack([w_some], [w_1], depth, fold)
        cache_mid = (cache_1, cache_2)
        late, late_cache, _ = lax.optimization_barrier((plane, caches[3], w_2))
        w_sent_3 = jnp.concatenate([w_cut[3], folded(late_cache)], 0)
        q_ids, cosine, sine = tables(late)
        ids = jnp.arange(count, dtype=jnp.int32)
        x_ids = jnp.concatenate([side * count + ids, (1 - side) * count + ids])
        order = ((0, 0), (2, 0), (1, 0), (0, 2), (2, 2), (1, 2), (3, 0), (3, 2))
        w_ids = [(late ^ k) * crew + (inner ^ turn ^ flip) for flip in (0, 1) for k, turn in order]
        w_ids = jnp.stack(w_ids).astype(jnp.int32)
        kv_ids = [(late ^ k) * crew + (inner ^ turn) for k in range(heads) for turn in (0, 2, 1, 3)]
        kv_ids = jnp.stack(kv_ids).astype(jnp.int32)
        numbers = (q_ids, cosine, sine, x_ids, w_ids, kv_ids)
        own, own_side, next_x, far, w_some, w_mid, cache_mid, w_3, w_line, numbers = (
            lax.optimization_barrier(
                (own, own_side, next_x, far, w_some, w_mid, cache_mid, w_sent_3, w_line, numbers)
            )
        )
        q_ids, cosine, sine, x_ids, w_ids, kv_ids = numbers
        next_side, far_side = sides(next_x, "next"), sides(far, "far")
        w_3 = across(w_3, 3, "w")
        last = across(far, 1, "x_last")
        w_mid_line = line(w_mid, "w1")
        w_last, _, cache_last = unpack([], [w_3], depth, fold)
        w_last_line = line(w_last, "w3")
        w_some = join([w_some, w_line, w_mid_line])
        w_some_core = core(w_some, "w")
        last_low, far_high = half(last, 0), half(far_side, 1)
        moved = (last, next_side, far_side, w_last, w_last_line, w_some)
        moved, w_some_core, last_low, far_high = lax.optimization_barrier(
            (moved, w_some_core, last_low, far_high)
        )
        last, next_side, far_side, w_last, w_last_line, w_some = moved
        caches = [caches[0], *cache_mid, cache_last]
        last_side = [sides(last_low, "last"), across(far_high, 1, "x_last_side")]
        w_parts = [w_some, w_last, w_last_line]
        w_parts += [w_some_core, core(w_last, "w3"), core(w_last_line, "w3_line")]
        x_chunks = [[own, own_side], [next_x, next_side], [far, far_side], [last, *last_side]]
    else:
        q_ids, cosine, sine = tables(plane)
        caches = [across(c, k) for k, c in enumerate(caches)]
        members = [
            [(i * crew + j) * tp + t for i in range(heads) for t in range(tp)] for j in range(crew)
        ]
        x_all = lax.all_gather(own, ("seq", "tp"), axis=0, tiled=True, axis_index_groups=members)
        x_chunks = [
            [lax.dynamic_slice_in_dim(x_all, (plane ^ k) * count * tp, count * tp)]
            for k in range(heads)
        ]
        x_ids = jnp.arange(count * tp, dtype=jnp.int32)
        gathered = [
            lax.all_gather(across(w, k), "seq", axis=0, tiled=True, axis_index_groups=groups)
            for k, w in enumerate(w_cut)
        ]
        per = gathered[0].shape[0] // FEATS
        w_parts = [g.reshape(per, FEATS, WIDTH) for g in gathered]
        w_ids = jnp.concatenate(
            [(plane ^ k) * per + jnp.arange(per, dtype=jnp.int32) for k in range(heads)]
        )

    def projected(kv, q, slots):
        chunks = [x_chunks[k] for k in slots]
        some = [caches[k] for k in slots]
        return project(kv, q, slots[0], chunks, x_ids, w_parts, w_ids, cosine, sine, some, tok, redo)

    if squared:
        kv_new = [*projected(True, False, (0, 1, 2)), *projected(True, False, (3,))]
        for chunk in x_chunks:
            chunk[0] = after(chunk[0], kv_new[1])
        queries = [*projected(False, True, (0, 1, 2)), *projected(False, True, (3,))]
        queries = list(lax.optimization_barrier(tuple(queries)))
    else:
        kv_new, queries = [[value] for value in projected(True, True, tuple(range(heads)))]

    if squared:
        kv_parts, places = [], []
        fars = [swap(mine, "seq", seq, 2, "kv_line") for mine in kv_new]
        fars = lax.optimization_barrier((*fars, queries[1]))
        for mine, far in zip(kv_new, fars):
            places += [(len(kv_parts) + n, i) for i in range(mine.shape[0]) for n in range(4)]
            kv_parts += [mine, far, core(mine, "kv"), core(far, "kv_line")]
    else:
        kv_parts = [
            lax.all_gather(kv_new[0][k : k + 1], "seq", axis=0, tiled=True, axis_index_groups=groups)
            for k in range(heads)
        ]
        places = [(k, i) for k in range(heads) for i in range(crew)]
        kv_ids = jnp.concatenate(
            [(plane ^ k) * crew + jnp.arange(crew, dtype=jnp.int32) for k in range(heads)]
        )

    back = [None] * heads
    for slots in tuple((k,) for k in reversed(range(heads))):
        some = [(queries[k // 3], k % 3) if squared else (queries[0], k) for k in slots]
        if squared and slots != (3,):
            earlier = back[3:] if slots == (0,) else []
            some = [(after(some[0][0], *mixed, *earlier), some[0][1])]
        mixed = attend(slots, prefix_len, some, q_ids, kv_parts, places, kv_ids, tok)
        for k, value in zip(slots, mixed):
            back[k] = across(value, k, "mixed")
    back = jnp.stack(back)
    columns = [lax.dynamic_index_in_dim(back, plane ^ h, 0, keepdims=False) for h in range(heads)]
    return jnp.concatenate(columns, 1)


def solution(mesh):
    placed = (
        P("seq", "tp"),
        P(),
        P("seq", "tp"),
        P(None, "seq", "tp"),
        P("seq", "tp"),
        P("seq"),
        P(),
    )
    return jax.shard_map(
        functools.partial(per_device, mesh.shape["seq"], mesh.shape["tp"]),
        mesh=mesh,
        in_specs=placed,
        out_specs=P("seq", "tp"),
        check_vma=False,
    )
```

```python
import functools
import math

import jax
import jax.numpy as jnp
from jax import lax
from jax.experimental import pallas as pl
from jax.experimental.pallas import tpu as pltpu
from jax.sharding import PartitionSpec as P

HEADS = 32
KVH = 8
HD = 128
GROUP = HEADS // KVH
WIDTH = (GROUP + 2) * HD
FEATS = 256
FAR = -1e30
VMEM = pl.BlockSpec(memory_space=pltpu.VMEM)
SMEM = pl.BlockSpec(memory_space=pltpu.SMEM)


def swap(value, axis, size, mask, name="move"):
    with jax.named_scope(name):
        return lax.ppermute(value, axis, [(i, i ^ mask) for i in range(size)])


def after(value, *earlier):
    return lax.optimization_barrier((value,) + earlier)[0]


def squares_kernel(stream, hidden, out):
    tok = stream.shape[0]
    for ref, first in ((stream, 0), (hidden, tok)):
        value = ref[...].astype(jnp.float32)
        total = jnp.sum(value * value, axis=-1, keepdims=True)
        out[first : first + value.shape[0]] = jnp.broadcast_to(total, (value.shape[0], HD))


def squares(stream, hidden):
    return pl.pallas_call(
        squares_kernel,
        out_shape=jax.ShapeDtypeStruct((stream.shape[0] + hidden.shape[0], HD), jnp.float32),
        in_specs=[VMEM] * 2,
        out_specs=VMEM,
        compiler_params=pltpu.CompilerParams(vmem_limit_bytes=8 * 2**20),
        cost_estimate=pl.CostEstimate(flops=1, bytes_accessed=1, transcendentals=0),
        name="squares",
    )(stream, hidden)


def norm_kernel(width, count, stream, hidden, gain, *refs):
    sums, out = refs[:count], refs[count]
    tok = stream.shape[0]
    factor = lax.rsqrt(sum(s[:, :1] for s in sums) / width + 1e-05)
    for ref, first in ((stream, 0), (hidden, tok)):
        last = first + ref.shape[0]
        for block in range(out.shape[0]):
            lanes = slice(block * FEATS, (block + 1) * FEATS)
            value = ref[:, lanes].astype(jnp.float32)
            value = value * factor[first:last] * gain[:, lanes]
            out[block, first:last] = value.astype(jnp.bfloat16)


def norm(stream, hidden, gain, sums, width):
    blocks = stream.shape[1] // FEATS
    rows = stream.shape[0] + hidden.shape[0]
    return pl.pallas_call(
        functools.partial(norm_kernel, width, len(sums)),
        out_shape=jax.ShapeDtypeStruct((blocks, rows, FEATS), jnp.bfloat16),
        in_specs=[VMEM] * (3 + len(sums)),
        out_specs=VMEM,
        compiler_params=pltpu.CompilerParams(vmem_limit_bytes=12 * 2**20),
        cost_estimate=pl.CostEstimate(flops=1, bytes_accessed=1, transcendentals=0),
        name="norm",
    )(stream, hidden, gain.reshape(1, -1), *sums)


def unpack_kernel(plain, fold, sources, *refs):
    sources, (whole, last, *caches) = refs[:sources], refs[sources:]
    depth = whole.shape[1]
    at = 0
    for n, source in enumerate(sources):
        if n < plain:
            whole[at : at + source.shape[0]] = source[...]
            at += source.shape[0]
            continue
        whole[at] = source[:depth]
        last[n - plain] = source[:depth]
        at += 1
        extra = source.shape[0] - depth
        for j in range(fold):
            lanes = slice(j * 2 * HD, (j + 1) * 2 * HD)
            caches[n - plain][j * extra : (j + 1) * extra] = source[depth:, lanes]


def unpack(plain, packed, depth, fold):
    extra = packed[0].shape[0] - depth
    count = sum(p.shape[0] for p in plain) + len(packed)
    return pl.pallas_call(
        functools.partial(unpack_kernel, len(plain), fold, len(plain) + len(packed)),
        out_shape=[
            jax.ShapeDtypeStruct((n, depth, WIDTH), jnp.bfloat16) for n in (count, len(packed))
        ]
        + [jax.ShapeDtypeStruct((fold * extra, 2 * HD), jnp.bfloat16)] * len(packed),
        in_specs=[VMEM] * (len(plain) + len(packed)),
        out_specs=[VMEM] * (2 + len(packed)),
        compiler_params=pltpu.CompilerParams(vmem_limit_bytes=12 * 2**20),
        cost_estimate=pl.CostEstimate(flops=2 * 10**10, bytes_accessed=10**7, transcendentals=0),
        name="unpack",
    )(*plain, *packed)


def join_kernel(*refs):
    at = 0
    for ref in refs[:-1]:
        refs[-1][at : at + ref.shape[0]] = ref[...]
        at += ref.shape[0]


def join(parts):
    count = sum(p.shape[0] for p in parts)
    return pl.pallas_call(
        join_kernel,
        out_shape=jax.ShapeDtypeStruct((count, *parts[0].shape[1:]), parts[0].dtype),
        in_specs=[VMEM] * len(parts),
        out_specs=VMEM,
        compiler_params=pltpu.CompilerParams(vmem_limit_bytes=12 * 2**20),
        name="join",
    )(*parts)


def half_kernel(value, out):
    out[...] = value[...]


def half(value, index):
    shape = (value.shape[0] // 2, *value.shape[1:])
    return pl.pallas_call(
        half_kernel,
        grid=(1,),
        out_shape=jax.ShapeDtypeStruct(shape, value.dtype),
        in_specs=[pl.BlockSpec(shape, lambda t: (index, 0, 0))],
        out_specs=pl.BlockSpec(shape, lambda t: (0, 0, 0)),
        compiler_params=pltpu.CompilerParams(vmem_limit_bytes=8 * 2**20),
        cost_estimate=pl.CostEstimate(flops=2 * 10**10, bytes_accessed=10**6, transcendentals=0),
        name="half",
    )(value)


def project_kernel(kv, tiles, first_slot, tok, redo, pitch, n_x, n_w, *refs):
    x_ids, w_ids = refs[:2]
    x_refs, refs = refs[2 : 2 + sum(n_x)], refs[2 + sum(n_x) :]
    w_refs, refs = refs[:n_w], refs[n_w:]
    chunks = len(n_x)
    cosine, sine, *refs = refs
    caches, outs, held = refs[: chunks * kv], list(refs[chunks * kv : -1]), refs[-1]
    kv_out = outs.pop(0) if kv else None
    q_out = outs.pop(0) if outs else None
    span = cosine.shape[1]
    cache_rows = span - tok

    @pl.when(pl.program_id(0) == 0)
    def _():
        first = 0
        for chunk, count in enumerate(n_x):
            at = 0
            for part in x_refs[first : first + count]:
                for block in range(part.shape[0]):
                    held[x_ids[at], chunk * pitch : chunk * pitch + tok + redo] = part[block]
                    at += 1
            first += count

    total = None
    at = 0
    for part in w_refs:
        for block in range(part.shape[0]):
            term = jnp.dot(held[w_ids[at]], part[block], preferred_element_type=jnp.float32)
            total = term if total is None else total + term
            at += 1

    def rotated(value, chunk, first, last):
        turned = pltpu.roll(value, HD // 2, 1)
        slot = first_slot + chunk
        return value * cosine[slot, first:last] + turned * sine[slot, first:last]

    def finish_queries():
        for chunk in range(chunks):
            for head in range(2):
                value = total[chunk * pitch : chunk * pitch + tok, head * HD : (head + 1) * HD]
                q_out[chunk, head] = rotated(value, chunk, 0, tok).astype(jnp.bfloat16)

    def finish_kv():
        for chunk in range(chunks):
            mine = total[chunk * pitch : chunk * pitch + tok + redo]
            keys = rotated(mine[:tok, :HD], chunk, 0, tok)
            kv_out[chunk, :tok] = jnp.concatenate([keys, mine[:tok, HD:]], 1).astype(jnp.bfloat16)
            cache = caches[chunk]
            offsets = cache[cache_rows : cache_rows + 1, :redo].astype(jnp.float32)
            row = lax.broadcasted_iota(jnp.int32, (cache_rows, redo), 0).astype(jnp.float32)
            chosen = (row == offsets).astype(jnp.float32)
            fresh = jnp.dot(
                chosen,
                mine[tok:],
                preferred_element_type=jnp.float32,
                precision=lax.Precision.HIGHEST,
            )
            turned = rotated(fresh[:, :HD], chunk, tok, span)
            fresh = jnp.concatenate([turned, fresh[:, HD:]], 1)
            hit = jnp.sum(chosen, axis=1, keepdims=True) > 0.5
            kept = cache[:cache_rows].astype(jnp.float32)
            kv_out[chunk, tok:] = jnp.where(hit, fresh, kept).astype(jnp.bfloat16)

    if kv and tiles > 1:
        pl.when(pl.program_id(0) == 0)(finish_kv)
        pl.when(pl.program_id(0) > 0)(finish_queries)
    elif kv:
        finish_kv()
    else:
        finish_queries()


def project(kv, q, first_slot, x_chunks, x_ids, w_parts, w_ids, cosine, sine, caches, tok, redo):
    chunks = len(x_chunks)
    blocks = sum(p.shape[0] for p in x_chunks[0])
    span = cosine.shape[1]
    pitch = -(-(tok + redo) // 16) * 16
    full = lambda a: pl.BlockSpec(a.shape, lambda t, n=a.ndim: (0,) * n)
    q_tiles = WIDTH // FEATS - 1
    tiles = kv + q * q_tiles
    w_spec = lambda a: pl.BlockSpec(
        (a.shape[0], FEATS, FEATS),
        lambda t: (0, 0, lax.rem(t + q_tiles, q_tiles + 1) if kv else t),
    )
    out_shape, out_specs = [], []
    if kv:
        out_shape.append(jax.ShapeDtypeStruct((chunks, span, 2 * HD), jnp.bfloat16))
        out_specs.append(full(out_shape[0]))
    else:
        caches = []
    if q:
        out_shape.append(jax.ShapeDtypeStruct((chunks, GROUP, tok, HD), jnp.bfloat16))
        out_specs.append(
            pl.BlockSpec((chunks, 2, tok, HD), lambda t: (0, jnp.maximum(t - kv, 0), 0, 0))
        )
    x_parts = [p for chunk in x_chunks for p in chunk]
    n_x = [len(chunk) for chunk in x_chunks]
    return pl.pallas_call(
        functools.partial(project_kernel, kv, tiles, first_slot, tok, redo, pitch, n_x, len(w_parts)),
        grid=(tiles,),
        out_shape=out_shape,
        in_specs=[SMEM, SMEM]
        + [full(a) for a in x_parts]
        + [w_spec(a) for a in w_parts]
        + [full(a) for a in (cosine, sine, *caches)],
        out_specs=out_specs,
        scratch_shapes=[pltpu.VMEM((blocks, chunks * pitch, FEATS), jnp.bfloat16)],
        compiler_params=pltpu.CompilerParams(vmem_limit_bytes=32 * 2**20),
        cost_estimate=pl.CostEstimate(
            flops=2 * chunks * pitch * blocks * FEATS * FEATS * tiles,
            bytes_accessed=2 * blocks * FEATS * (FEATS * tiles + chunks * pitch),
            transcendentals=0,
        ),
        name="_".join(["keys_values"] * kv + ["queries"] * q),
    )(x_ids, w_ids, *x_parts, *w_parts, cosine, sine, *caches)


def attend_kernel(slots, tok, places, *refs):
    begin_ref, q_ids, kv_ids = refs[:3]
    count = len(slots)
    q_refs, refs = refs[3 : 3 + count], refs[3 + count :]
    kv_refs, refs = refs[: -count - 4], refs[-count - 4 :]
    outs, (scores, top, total, accum) = refs[:count], refs[count:]
    begin = begin_ref[0]
    heads = GROUP * tok
    scale = math.log2(math.e) / math.sqrt(HD)
    span = kv_refs[0].shape[1]
    cache_rows = span - tok
    groups = []
    for at in range(0, len(places), 4):
        group = places[at : at + 4]
        ids = [kv_ids[at + i] for i in range(len(group))]
        least, most = functools.reduce(jnp.minimum, ids), functools.reduce(jnp.maximum, ids)
        groups.append((group, ids, least, most, at * span))

    for n, slot in enumerate(slots):
        q_id = q_ids[slot]
        top[...] = jnp.full(top.shape, FAR, jnp.float32)
        total[...] = jnp.zeros(total.shape, jnp.float32)
        accum[...] = jnp.zeros(accum.shape, jnp.float32)

        def rows(group, first, last, half):
            return jnp.concatenate(
                [kv_refs[r][i, first:last, half * HD : (half + 1) * HD] for r, i in group], 0
            )

        def score(column, keys, allowed, n=n):
            value = lax.dot_general(
                q_refs[n][0].reshape(heads, HD),
                keys,
                (((1,), (1,)), ((), ())),
                preferred_element_type=jnp.float32,
            )
            if allowed is not None:
                value = jnp.where(allowed(value.shape), value, FAR)
            scores[:, column : column + value.shape[1]] = value
            most = top[...]
            for lane in range(0, value.shape[1], HD):
                most = jnp.maximum(most, value[:, lane : lane + HD])
            top[...] = most

        def mix(column, values):
            weights = []
            some = total[...]
            most = top[...]
            for lane in range(0, values.shape[0], HD):
                part = scores[:, column + lane : column + lane + HD]
                weight = jnp.exp2(part * scale - most)
                some = some + weight
                weights.append(weight.astype(jnp.bfloat16))
            total[...] = some
            accum[...] += jnp.dot(
                jnp.concatenate(weights, 1), values, preferred_element_type=jnp.float32
            )

        for group, ids, least, most, base in groups:
            shift = len(group) * tok

            def starts(shape, step, ids=ids):
                column = lax.broadcasted_iota(jnp.int32, shape, 1)
                which = column // step
                first = jnp.zeros(shape, jnp.int32)
                for i, one in enumerate(ids):
                    first = jnp.where(which == i, one * step, first)
                return first + column % step

            def causal(shape, starts=starts):
                row = lax.broadcasted_iota(jnp.int32, (shape[0], 1), 0)
                return starts((1, shape[1]), tok) <= q_id * tok + row % tok

            def prefix(shape, starts=starts):
                return starts((1, shape[1]), cache_rows) < begin

            @pl.when((most + 1) * cache_rows <= begin)
            def _(group=group, base=base):
                score(base + shift, rows(group, tok, span, 0), None)

            @pl.when(((most + 1) * cache_rows > begin) & (least * cache_rows < begin))
            def _(group=group, prefix=prefix, base=base):
                score(base + shift, rows(group, tok, span, 0), prefix)

            @pl.when(most < q_id)
            def _(group=group, base=base):
                score(base, rows(group, 0, tok, 0), None)

            @pl.when((most >= q_id) & (least <= q_id))
            def _(group=group, causal=causal, base=base):
                score(base, rows(group, 0, tok, 0), causal)

        peak = jnp.max(top[...], axis=1, keepdims=True) * scale
        top[...] = jnp.broadcast_to(peak, top.shape)
        for group, ids, least, most, base in groups:
            shift = len(group) * tok

            @pl.when(least * cache_rows < begin)
            def _(group=group, base=base):
                mix(base + shift, rows(group, tok, span, 1))

            @pl.when(least <= q_id)
            def _(group=group, base=base):
                mix(base, rows(group, 0, tok, 1))

        mixed = (accum[...] / jnp.sum(total[...], axis=1, keepdims=True)).astype(jnp.bfloat16)
        for head in range(GROUP):
            outs[n][:, head * HD : (head + 1) * HD] = mixed[head * tok : (head + 1) * tok]


def attend(slots, begin, queries, q_ids, kv_parts, places, kv_ids, tok):
    span = kv_parts[0].shape[1]
    n_rows = len(places) * span
    heads = GROUP * tok
    q_specs = [pl.BlockSpec((1, GROUP, tok, HD), lambda t, i=i: (i, 0, 0, 0)) for _, i in queries]
    return pl.pallas_call(
        functools.partial(attend_kernel, slots, tok, places),
        grid=(1,),
        out_shape=[jax.ShapeDtypeStruct((tok, GROUP * HD), jnp.bfloat16)] * len(slots),
        in_specs=[SMEM, SMEM, SMEM] + q_specs + [VMEM] * len(kv_parts),
        out_specs=[VMEM] * len(slots),
        scratch_shapes=[
            pltpu.VMEM((heads, n_rows), jnp.float32),
            pltpu.VMEM((heads, HD), jnp.float32),
            pltpu.VMEM((heads, HD), jnp.float32),
            pltpu.VMEM((heads, HD), jnp.float32),
        ],
        compiler_params=pltpu.CompilerParams(vmem_limit_bytes=8 * 2**20 + 5 * heads * n_rows),
        cost_estimate=pl.CostEstimate(
            flops=4 * len(slots) * heads * n_rows * HD,
            bytes_accessed=4 * n_rows * HD,
            transcendentals=len(slots) * heads * n_rows,
        ),
        name="attend",
    )(begin, q_ids, kv_ids, *[q for q, _ in queries], *kv_parts)


def per_device(
    seq, tp, stream_x, norm_gain, w_qkv, cache_kv, recomp_hidden, recomp_index, prefix_len
):
    tok, redo = stream_x.shape[0], recomp_hidden.shape[0]
    cache_rows = cache_kv.shape[1]
    heads = w_qkv.shape[1] // WIDTH
    crew = seq // heads
    at, side = lax.axis_index("seq"), lax.axis_index("tp")
    plane, inner = at // crew, at % crew
    begin = prefix_len[0]
    squared = crew == 4 and heads == 4 and tp == 2

    def across(value, k, name="planes"):
        return swap(value, "seq", seq, k * crew, f"{name}_{k}") if k else value

    w_cut = [lax.dynamic_slice_in_dim(w_qkv, (plane ^ k) * WIDTH, WIDTH, 1) for k in range(heads)]
    stream_x, w_cut = lax.optimization_barrier((stream_x, w_cut))
    sums = squares(stream_x, recomp_hidden)
    wide = stream_x.shape[1]
    width = wide * tp
    gain = lax.dynamic_slice_in_dim(norm_gain, side * wide, wide)
    sums = [sums, swap(sums, "tp", tp, 1, "side_sums")] if squared else [lax.psum(sums, "tp")]
    own = norm(stream_x, recomp_hidden, gain, sums, width)

    offsets = (recomp_index - at * cache_rows).astype(jnp.bfloat16)
    fold = WIDTH // (2 * HD)
    extra = -(-(cache_rows + 1) // (16 * fold)) * 16
    offsets = jnp.pad(offsets[None, :], ((0, fold * extra - cache_rows - 1), (0, 2 * HD - redo)))
    caches = []
    for k in range(heads):
        part = lax.dynamic_slice_in_dim(cache_kv, (plane ^ k) * HD, HD, 2)
        part = jnp.concatenate([part[0], part[1]], 1)
        caches.append(jnp.concatenate([part, offsets], 0))

    def folded(cache):
        return jnp.concatenate([cache[i * extra : (i + 1) * extra] for i in range(fold)], 1)

    def tables(plane):
        half = HD // 2
        freq = jnp.exp(
            -math.log(1000000.0) * jnp.arange(half, dtype=jnp.float32) * 2.0 / (2 * half)
        )
        q_ids = jnp.stack([(plane ^ k) * crew + inner for k in range(heads)]).astype(jnp.int32)
        token_ids = q_ids[:, None] * tok + jnp.arange(tok, dtype=jnp.int32) + begin
        row_ids = q_ids[:, None] * cache_rows + jnp.arange(cache_rows, dtype=jnp.int32)
        angle = jnp.concatenate([token_ids, row_ids], 1).astype(jnp.float32)[..., None] * freq
        cosine, sine = jnp.cos(angle), jnp.sin(angle)
        return q_ids, jnp.concatenate([cosine, cosine], -1), jnp.concatenate([-sine, sine], -1)

    count = wide // FEATS
    groups = [[i * crew + j for j in range(crew)] for i in range(heads)]
    if squared:

        def sides(value, name):
            return swap(value, "tp", tp, 1, f"side_{name}")

        def line(value, name):
            return swap(value, "seq", seq, 2, f"line_{name}")

        def core(value, name):
            return swap(value, "seq", seq, 1, f"core_{name}")

        depth = w_qkv.shape[0]
        w_sent = [jnp.concatenate([w, folded(c)], 0) for w, c in zip(w_cut[:3], caches)]
        w_own = w_cut[0][None]
        w_1, w_2 = across(w_sent[1], 1, "w"), across(w_sent[2], 2, "w")
        far, next_x = across(own, 2, "x_far"), across(own, 1, "x_next")
        own_line = line(w_own, "w0")
        own_side = sides(after(own, own_line), "own")
        w_some, w_line, cache_2 = unpack([w_own], [w_2], depth, fold)
        w_line = line(w_line, "w2")
        w_some, w_mid, cache_1 = unpack([w_some], [w_1], depth, fold)
        cache_mid = (cache_1, cache_2)
        late, late_cache, _ = lax.optimization_barrier((plane, caches[3], own))
        w_sent_3 = jnp.concatenate([w_cut[3], folded(late_cache)], 0)
        q_ids, cosine, sine = tables(late)
        ids = jnp.arange(count, dtype=jnp.int32)
        x_ids = jnp.concatenate([side * count + ids, (1 - side) * count + ids])
        order = ((0, 0), (2, 0), (1, 0), (0, 2), (2, 2), (1, 2), (3, 0), (3, 2))
        w_ids = [(late ^ k) * crew + (inner ^ turn ^ flip) for flip in (0, 1) for k, turn in order]
        w_ids = jnp.stack(w_ids).astype(jnp.int32)
        kv_ids = [(late ^ k) * crew + (inner ^ turn) for k in range(heads) for turn in (0, 2, 1, 3)]
        kv_ids = jnp.stack(kv_ids).astype(jnp.int32)
        numbers = (q_ids, cosine, sine, x_ids, w_ids, kv_ids)
        lines = (own_line, w_line)
        own, own_side, next_x, far, w_some, w_mid, cache_mid, w_3, lines, numbers = (
            lax.optimization_barrier(
                (own, own_side, next_x, far, w_some, w_mid, cache_mid, w_sent_3, lines, numbers)
            )
        )
        q_ids, cosine, sine, x_ids, w_ids, kv_ids = numbers
        next_side, far_side = sides(next_x, "next"), sides(far, "far")
        w_3 = across(w_3, 3, "w")
        last = across(far, 1, "x_last")
        w_mid_line = line(w_mid, "w1")
        w_last, _, cache_last = unpack([], [w_3], depth, fold)
        w_last_line = line(w_last, "w3")
        w_some = join([w_some, *lines, w_mid_line])
        w_some_core = core(w_some, "w")
        last_low, far_high = half(last, 0), half(far_side, 1)
        moved = (last, next_side, far_side, w_last, w_last_line, w_some)
        moved, w_some_core, last_low, far_high = lax.optimization_barrier(
            (moved, w_some_core, last_low, far_high)
        )
        last, next_side, far_side, w_last, w_last_line, w_some = moved
        caches = [caches[0], *cache_mid, cache_last]
        last_side = [sides(last_low, "last"), across(far_high, 1, "x_last_side")]
        w_parts = [w_some, w_last, w_last_line]
        w_parts += [w_some_core, core(w_last, "w3"), core(w_last_line, "w3_line")]
        x_chunks = [[own, own_side], [next_x, next_side], [far, far_side], [last, *last_side]]
    else:
        q_ids, cosine, sine = tables(plane)
        caches = [across(c, k) for k, c in enumerate(caches)]
        members = [
            [(i * crew + j) * tp + t for i in range(heads) for t in range(tp)] for j in range(crew)
        ]
        x_all = lax.all_gather(own, ("seq", "tp"), axis=0, tiled=True, axis_index_groups=members)
        x_chunks = [
            [lax.dynamic_slice_in_dim(x_all, (plane ^ k) * count * tp, count * tp)]
            for k in range(heads)
        ]
        x_ids = jnp.arange(count * tp, dtype=jnp.int32)
        gathered = [
            lax.all_gather(across(w, k), "seq", axis=0, tiled=True, axis_index_groups=groups)
            for k, w in enumerate(w_cut)
        ]
        per = gathered[0].shape[0] // FEATS
        w_parts = [g.reshape(per, FEATS, WIDTH) for g in gathered]
        w_ids = jnp.concatenate(
            [(plane ^ k) * per + jnp.arange(per, dtype=jnp.int32) for k in range(heads)]
        )

    def projected(kv, q, slots):
        chunks = [x_chunks[k] for k in slots]
        some = [caches[k] for k in slots]
        return project(kv, q, slots[0], chunks, x_ids, w_parts, w_ids, cosine, sine, some, tok, redo)

    if squared:
        kv_new = [*projected(True, False, (0, 1, 2)), *projected(True, False, (3,))]
        for chunk in x_chunks:
            chunk[0] = after(chunk[0], kv_new[1])
        queries = [*projected(False, True, (0, 1, 2)), *projected(False, True, (3,))]
        first_queries = queries[0]
        queries = list(lax.optimization_barrier(tuple(queries)))
    else:
        kv_new, queries = [[value] for value in projected(True, True, tuple(range(heads)))]

    if squared:
        kv_parts, places = [], []
        fars = [swap(mine, "seq", seq, 2, "kv_line") for mine in kv_new]
        fars = lax.optimization_barrier((*fars, first_queries))
        for mine, far in zip(kv_new, fars):
            places += [(len(kv_parts) + n, i) for i in range(mine.shape[0]) for n in range(4)]
            kv_parts += [mine, far, core(mine, "kv"), core(far, "kv_line")]
    else:
        kv_parts = [
            lax.all_gather(kv_new[0][k : k + 1], "seq", axis=0, tiled=True, axis_index_groups=groups)
            for k in range(heads)
        ]
        places = [(k, i) for k in range(heads) for i in range(crew)]
        kv_ids = jnp.concatenate(
            [(plane ^ k) * crew + jnp.arange(crew, dtype=jnp.int32) for k in range(heads)]
        )

    back = [None] * heads
    for slots in tuple((k,) for k in reversed(range(heads))):
        some = [(queries[k // 3], k % 3) if squared else (queries[0], k) for k in slots]
        if squared and slots != (3,):
            earlier = back[3:] if slots == (0,) else []
            some = [(after(some[0][0], *mixed, *earlier), some[0][1])]
        mixed = attend(slots, prefix_len, some, q_ids, kv_parts, places, kv_ids, tok)
        for k, value in zip(slots, mixed):
            back[k] = across(value, k, "mixed")
    back = jnp.stack(back)
    columns = [lax.dynamic_index_in_dim(back, plane ^ h, 0, keepdims=False) for h in range(heads)]
    return jnp.concatenate(columns, 1)


def solution(mesh):
    placed = (
        P("seq", "tp"),
        P(),
        P("seq", "tp"),
        P(None, "seq", "tp"),
        P("seq", "tp"),
        P("seq"),
        P(),
    )
    return jax.shard_map(
        functools.partial(per_device, mesh.shape["seq"], mesh.shape["tp"]),
        mesh=mesh,
        in_specs=placed,
        out_specs=P("seq", "tp"),
        check_vma=False,
    )
```

```python
import functools
import math

import jax
import jax.numpy as jnp
from jax import lax
from jax.experimental import pallas as pl
from jax.experimental.pallas import tpu as pltpu
from jax.sharding import PartitionSpec as P

HEADS = 32
KVH = 8
HD = 128
GROUP = HEADS // KVH
WIDTH = (GROUP + 2) * HD
FEATS = 256
FAR = -1e30
VMEM = pl.BlockSpec(memory_space=pltpu.VMEM)
SMEM = pl.BlockSpec(memory_space=pltpu.SMEM)


def swap(value, axis, size, mask, name="move"):
    with jax.named_scope(name):
        return lax.ppermute(value, axis, [(i, i ^ mask) for i in range(size)])


def after(value, *earlier):
    return lax.optimization_barrier((value,) + earlier)[0]


def squares_kernel(stream, hidden, out):
    tok = stream.shape[0]
    for ref, first in ((stream, 0), (hidden, tok)):
        value = ref[...].astype(jnp.float32)
        total = jnp.sum(value * value, axis=-1, keepdims=True)
        out[first : first + value.shape[0]] = jnp.broadcast_to(total, (value.shape[0], HD))


def squares(stream, hidden):
    return pl.pallas_call(
        squares_kernel,
        out_shape=jax.ShapeDtypeStruct((stream.shape[0] + hidden.shape[0], HD), jnp.float32),
        in_specs=[VMEM] * 2,
        out_specs=VMEM,
        compiler_params=pltpu.CompilerParams(vmem_limit_bytes=8 * 2**20),
        cost_estimate=pl.CostEstimate(flops=1, bytes_accessed=1, transcendentals=0),
        name="squares",
    )(stream, hidden)


def norm_kernel(width, count, stream, hidden, gain, *refs):
    sums, out = refs[:count], refs[count]
    tok = stream.shape[0]
    factor = lax.rsqrt(sum(s[:, :1] for s in sums) / width + 1e-05)
    for ref, first in ((stream, 0), (hidden, tok)):
        last = first + ref.shape[0]
        for block in range(out.shape[0]):
            lanes = slice(block * FEATS, (block + 1) * FEATS)
            value = ref[:, lanes].astype(jnp.float32)
            value = value * factor[first:last] * gain[:, lanes]
            out[block, first:last] = value.astype(jnp.bfloat16)


def norm(stream, hidden, gain, sums, width):
    blocks = stream.shape[1] // FEATS
    rows = stream.shape[0] + hidden.shape[0]
    return pl.pallas_call(
        functools.partial(norm_kernel, width, len(sums)),
        out_shape=jax.ShapeDtypeStruct((blocks, rows, FEATS), jnp.bfloat16),
        in_specs=[VMEM] * (3 + len(sums)),
        out_specs=VMEM,
        compiler_params=pltpu.CompilerParams(vmem_limit_bytes=12 * 2**20),
        cost_estimate=pl.CostEstimate(flops=1, bytes_accessed=1, transcendentals=0),
        name="norm",
    )(stream, hidden, gain.reshape(1, -1), *sums)


def unpack_kernel(plain, fold, sources, *refs):
    sources, (whole, last, *caches) = refs[:sources], refs[sources:]
    depth = whole.shape[1]
    at = 0
    for n, source in enumerate(sources):
        if n < plain:
            whole[at : at + source.shape[0]] = source[...]
            at += source.shape[0]
            continue
        whole[at] = source[:depth]
        last[n - plain] = source[:depth]
        at += 1
        extra = source.shape[0] - depth
        for j in range(fold):
            lanes = slice(j * 2 * HD, (j + 1) * 2 * HD)
            caches[n - plain][j * extra : (j + 1) * extra] = source[depth:, lanes]


def unpack(plain, packed, depth, fold):
    extra = packed[0].shape[0] - depth
    count = sum(p.shape[0] for p in plain) + len(packed)
    return pl.pallas_call(
        functools.partial(unpack_kernel, len(plain), fold, len(plain) + len(packed)),
        out_shape=[
            jax.ShapeDtypeStruct((n, depth, WIDTH), jnp.bfloat16) for n in (count, len(packed))
        ]
        + [jax.ShapeDtypeStruct((fold * extra, 2 * HD), jnp.bfloat16)] * len(packed),
        in_specs=[VMEM] * (len(plain) + len(packed)),
        out_specs=[VMEM] * (2 + len(packed)),
        compiler_params=pltpu.CompilerParams(vmem_limit_bytes=12 * 2**20),
        cost_estimate=pl.CostEstimate(flops=2 * 10**10, bytes_accessed=10**7, transcendentals=0),
        name="unpack",
    )(*plain, *packed)


def join_kernel(*refs):
    at = 0
    for ref in refs[:-1]:
        refs[-1][at : at + ref.shape[0]] = ref[...]
        at += ref.shape[0]


def join(parts):
    count = sum(p.shape[0] for p in parts)
    return pl.pallas_call(
        join_kernel,
        out_shape=jax.ShapeDtypeStruct((count, *parts[0].shape[1:]), parts[0].dtype),
        in_specs=[VMEM] * len(parts),
        out_specs=VMEM,
        compiler_params=pltpu.CompilerParams(vmem_limit_bytes=12 * 2**20),
        name="join",
    )(*parts)


def half_kernel(value, out):
    out[...] = value[...]


def half(value, index):
    shape = (value.shape[0] // 2, *value.shape[1:])
    return pl.pallas_call(
        half_kernel,
        grid=(1,),
        out_shape=jax.ShapeDtypeStruct(shape, value.dtype),
        in_specs=[pl.BlockSpec(shape, lambda t: (index, 0, 0))],
        out_specs=pl.BlockSpec(shape, lambda t: (0, 0, 0)),
        compiler_params=pltpu.CompilerParams(vmem_limit_bytes=8 * 2**20),
        cost_estimate=pl.CostEstimate(flops=2 * 10**10, bytes_accessed=10**6, transcendentals=0),
        name="half",
    )(value)


def project_kernel(kv, tiles, first_slot, tok, redo, pitch, n_x, n_w, *refs):
    x_ids, w_ids = refs[:2]
    x_refs, refs = refs[2 : 2 + sum(n_x)], refs[2 + sum(n_x) :]
    w_refs, refs = refs[:n_w], refs[n_w:]
    chunks = len(n_x)
    cosine, sine, *refs = refs
    caches, outs, held = refs[: chunks * kv], list(refs[chunks * kv : -1]), refs[-1]
    kv_out = outs.pop(0) if kv else None
    q_out = outs.pop(0) if outs else None
    span = cosine.shape[1]
    cache_rows = span - tok

    @pl.when(pl.program_id(0) == 0)
    def _():
        first = 0
        for chunk, count in enumerate(n_x):
            at = 0
            for part in x_refs[first : first + count]:
                for block in range(part.shape[0]):
                    held[x_ids[at], chunk * pitch : chunk * pitch + tok + redo] = part[block]
                    at += 1
            first += count

    total = None
    at = 0
    for part in w_refs:
        for block in range(part.shape[0]):
            term = jnp.dot(held[w_ids[at]], part[block], preferred_element_type=jnp.float32)
            total = term if total is None else total + term
            at += 1

    def rotated(value, chunk, first, last):
        turned = pltpu.roll(value, HD // 2, 1)
        slot = first_slot + chunk
        return value * cosine[slot, first:last] + turned * sine[slot, first:last]

    def finish_queries():
        for chunk in range(chunks):
            for head in range(2):
                value = total[chunk * pitch : chunk * pitch + tok, head * HD : (head + 1) * HD]
                q_out[chunk, head] = rotated(value, chunk, 0, tok).astype(jnp.bfloat16)

    def finish_kv():
        for chunk in range(chunks):
            mine = total[chunk * pitch : chunk * pitch + tok + redo]
            keys = rotated(mine[:tok, :HD], chunk, 0, tok)
            kv_out[chunk, :tok] = jnp.concatenate([keys, mine[:tok, HD:]], 1).astype(jnp.bfloat16)
            cache = caches[chunk]
            offsets = cache[cache_rows : cache_rows + 1, :redo].astype(jnp.float32)
            row = lax.broadcasted_iota(jnp.int32, (cache_rows, redo), 0).astype(jnp.float32)
            chosen = (row == offsets).astype(jnp.float32)
            fresh = jnp.dot(
                chosen,
                mine[tok:],
                preferred_element_type=jnp.float32,
                precision=lax.Precision.HIGHEST,
            )
            turned = rotated(fresh[:, :HD], chunk, tok, span)
            fresh = jnp.concatenate([turned, fresh[:, HD:]], 1)
            hit = jnp.sum(chosen, axis=1, keepdims=True) > 0.5
            kept = cache[:cache_rows].astype(jnp.float32)
            kv_out[chunk, tok:] = jnp.where(hit, fresh, kept).astype(jnp.bfloat16)

    if kv and tiles > 1:
        pl.when(pl.program_id(0) == 0)(finish_kv)
        pl.when(pl.program_id(0) > 0)(finish_queries)
    elif kv:
        finish_kv()
    else:
        finish_queries()


def project(kv, q, first_slot, x_chunks, x_ids, w_parts, w_ids, cosine, sine, caches, tok, redo):
    chunks = len(x_chunks)
    blocks = sum(p.shape[0] for p in x_chunks[0])
    span = cosine.shape[1]
    pitch = -(-(tok + redo) // 16) * 16
    full = lambda a: pl.BlockSpec(a.shape, lambda t, n=a.ndim: (0,) * n)
    q_tiles = WIDTH // FEATS - 1
    tiles = kv + q * q_tiles
    w_spec = lambda a: pl.BlockSpec(
        (a.shape[0], FEATS, FEATS),
        lambda t: (0, 0, lax.rem(t + q_tiles, q_tiles + 1) if kv else t),
    )
    out_shape, out_specs = [], []
    if kv:
        out_shape.append(jax.ShapeDtypeStruct((chunks, span, 2 * HD), jnp.bfloat16))
        out_specs.append(full(out_shape[0]))
    else:
        caches = []
    if q:
        out_shape.append(jax.ShapeDtypeStruct((chunks, GROUP, tok, HD), jnp.bfloat16))
        out_specs.append(
            pl.BlockSpec((chunks, 2, tok, HD), lambda t: (0, jnp.maximum(t - kv, 0), 0, 0))
        )
    x_parts = [p for chunk in x_chunks for p in chunk]
    n_x = [len(chunk) for chunk in x_chunks]
    return pl.pallas_call(
        functools.partial(project_kernel, kv, tiles, first_slot, tok, redo, pitch, n_x, len(w_parts)),
        grid=(tiles,),
        out_shape=out_shape,
        in_specs=[SMEM, SMEM]
        + [full(a) for a in x_parts]
        + [w_spec(a) for a in w_parts]
        + [full(a) for a in (cosine, sine, *caches)],
        out_specs=out_specs,
        scratch_shapes=[pltpu.VMEM((blocks, chunks * pitch, FEATS), jnp.bfloat16)],
        compiler_params=pltpu.CompilerParams(vmem_limit_bytes=32 * 2**20),
        cost_estimate=pl.CostEstimate(
            flops=2 * chunks * pitch * blocks * FEATS * FEATS * tiles,
            bytes_accessed=2 * blocks * FEATS * (FEATS * tiles + chunks * pitch),
            transcendentals=0,
        ),
        name="_".join(["keys_values"] * kv + ["queries"] * q),
    )(x_ids, w_ids, *x_parts, *w_parts, cosine, sine, *caches)


def attend_kernel(slots, tok, places, *refs):
    begin_ref, q_ids, kv_ids = refs[:3]
    count = len(slots)
    q_refs, refs = refs[3 : 3 + count], refs[3 + count :]
    kv_refs, refs = refs[: -count - 4], refs[-count - 4 :]
    outs, (scores, top, total, accum) = refs[:count], refs[count:]
    begin = begin_ref[0]
    heads = GROUP * tok
    scale = math.log2(math.e) / math.sqrt(HD)
    span = kv_refs[0].shape[1]
    cache_rows = span - tok
    groups = []
    for at in range(0, len(places), 4):
        group = places[at : at + 4]
        ids = [kv_ids[at + i] for i in range(len(group))]
        least, most = functools.reduce(jnp.minimum, ids), functools.reduce(jnp.maximum, ids)
        groups.append((group, ids, least, most, at * span))

    for n, slot in enumerate(slots):
        q_id = q_ids[slot]
        top[...] = jnp.full(top.shape, FAR, jnp.float32)
        total[...] = jnp.zeros(total.shape, jnp.float32)
        accum[...] = jnp.zeros(accum.shape, jnp.float32)

        def rows(group, first, last, half):
            return jnp.concatenate(
                [kv_refs[r][i, first:last, half * HD : (half + 1) * HD] for r, i in group], 0
            )

        def score(column, keys, allowed, n=n):
            value = lax.dot_general(
                q_refs[n][0].reshape(heads, HD),
                keys,
                (((1,), (1,)), ((), ())),
                preferred_element_type=jnp.float32,
            )
            if allowed is not None:
                value = jnp.where(allowed(value.shape), value, FAR)
            scores[:, column : column + value.shape[1]] = value
            most = top[...]
            for lane in range(0, value.shape[1], HD):
                most = jnp.maximum(most, value[:, lane : lane + HD])
            top[...] = most

        def mix(column, values):
            weights = []
            some = total[...]
            most = top[...]
            for lane in range(0, values.shape[0], HD):
                part = scores[:, column + lane : column + lane + HD]
                weight = jnp.exp2(part * scale - most)
                some = some + weight
                weights.append(weight.astype(jnp.bfloat16))
            total[...] = some
            accum[...] += jnp.dot(
                jnp.concatenate(weights, 1), values, preferred_element_type=jnp.float32
            )

        for group, ids, least, most, base in groups:
            shift = len(group) * tok

            def starts(shape, step, ids=ids):
                column = lax.broadcasted_iota(jnp.int32, shape, 1)
                which = column // step
                first = jnp.zeros(shape, jnp.int32)
                for i, one in enumerate(ids):
                    first = jnp.where(which == i, one * step, first)
                return first + column % step

            def causal(shape, starts=starts):
                row = lax.broadcasted_iota(jnp.int32, (shape[0], 1), 0)
                return starts((1, shape[1]), tok) <= q_id * tok + row % tok

            def prefix(shape, starts=starts):
                return starts((1, shape[1]), cache_rows) < begin

            @pl.when((most + 1) * cache_rows <= begin)
            def _(group=group, base=base):
                score(base + shift, rows(group, tok, span, 0), None)

            @pl.when(((most + 1) * cache_rows > begin) & (least * cache_rows < begin))
            def _(group=group, prefix=prefix, base=base):
                score(base + shift, rows(group, tok, span, 0), prefix)

            @pl.when(most < q_id)
            def _(group=group, base=base):
                score(base, rows(group, 0, tok, 0), None)

            @pl.when((most >= q_id) & (least <= q_id))
            def _(group=group, causal=causal, base=base):
                score(base, rows(group, 0, tok, 0), causal)

        peak = jnp.max(top[...], axis=1, keepdims=True) * scale
        top[...] = jnp.broadcast_to(peak, top.shape)
        for group, ids, least, most, base in groups:
            shift = len(group) * tok

            @pl.when(least * cache_rows < begin)
            def _(group=group, base=base):
                mix(base + shift, rows(group, tok, span, 1))

            @pl.when(least <= q_id)
            def _(group=group, base=base):
                mix(base, rows(group, 0, tok, 1))

        mixed = (accum[...] / jnp.sum(total[...], axis=1, keepdims=True)).astype(jnp.bfloat16)
        for head in range(GROUP):
            outs[n][:, head * HD : (head + 1) * HD] = mixed[head * tok : (head + 1) * tok]


def attend(slots, begin, queries, q_ids, kv_parts, places, kv_ids, tok):
    span = kv_parts[0].shape[1]
    n_rows = len(places) * span
    heads = GROUP * tok
    q_specs = [pl.BlockSpec((1, GROUP, tok, HD), lambda t, i=i: (i, 0, 0, 0)) for _, i in queries]
    return pl.pallas_call(
        functools.partial(attend_kernel, slots, tok, places),
        grid=(1,),
        out_shape=[jax.ShapeDtypeStruct((tok, GROUP * HD), jnp.bfloat16)] * len(slots),
        in_specs=[SMEM, SMEM, SMEM] + q_specs + [VMEM] * len(kv_parts),
        out_specs=[VMEM] * len(slots),
        scratch_shapes=[
            pltpu.VMEM((heads, n_rows), jnp.float32),
            pltpu.VMEM((heads, HD), jnp.float32),
            pltpu.VMEM((heads, HD), jnp.float32),
            pltpu.VMEM((heads, HD), jnp.float32),
        ],
        compiler_params=pltpu.CompilerParams(vmem_limit_bytes=8 * 2**20 + 5 * heads * n_rows),
        cost_estimate=pl.CostEstimate(
            flops=4 * len(slots) * heads * n_rows * HD,
            bytes_accessed=4 * n_rows * HD,
            transcendentals=len(slots) * heads * n_rows,
        ),
        name="attend",
    )(begin, q_ids, kv_ids, *[q for q, _ in queries], *kv_parts)


def per_device(
    seq, tp, stream_x, norm_gain, w_qkv, cache_kv, recomp_hidden, recomp_index, prefix_len
):
    tok, redo = stream_x.shape[0], recomp_hidden.shape[0]
    cache_rows = cache_kv.shape[1]
    heads = w_qkv.shape[1] // WIDTH
    crew = seq // heads
    at, side = lax.axis_index("seq"), lax.axis_index("tp")
    plane, inner = at // crew, at % crew
    begin = prefix_len[0]
    squared = crew == 4 and heads == 4 and tp == 2

    def across(value, k, name="planes"):
        return swap(value, "seq", seq, k * crew, f"{name}_{k}") if k else value

    w_cut = [lax.dynamic_slice_in_dim(w_qkv, (plane ^ k) * WIDTH, WIDTH, 1) for k in range(heads)]
    stream_x, w_cut = lax.optimization_barrier((stream_x, w_cut))
    sums = squares(stream_x, recomp_hidden)
    wide = stream_x.shape[1]
    width = wide * tp
    gain = lax.dynamic_slice_in_dim(norm_gain, side * wide, wide)
    sums = [sums, swap(sums, "tp", tp, 1, "side_sums")] if squared else [lax.psum(sums, "tp")]
    own = norm(stream_x, recomp_hidden, gain, sums, width)

    offsets = (recomp_index - at * cache_rows).astype(jnp.bfloat16)
    fold = WIDTH // (2 * HD)
    extra = -(-(cache_rows + 1) // (16 * fold)) * 16
    offsets = jnp.pad(offsets[None, :], ((0, fold * extra - cache_rows - 1), (0, 2 * HD - redo)))
    caches = []
    for k in range(heads):
        part = lax.dynamic_slice_in_dim(cache_kv, (plane ^ k) * HD, HD, 2)
        part = jnp.concatenate([part[0], part[1]], 1)
        caches.append(jnp.concatenate([part, offsets], 0))

    def folded(cache):
        return jnp.concatenate([cache[i * extra : (i + 1) * extra] for i in range(fold)], 1)

    def tables(plane):
        half = HD // 2
        freq = jnp.exp(
            -math.log(1000000.0) * jnp.arange(half, dtype=jnp.float32) * 2.0 / (2 * half)
        )
        q_ids = jnp.stack([(plane ^ k) * crew + inner for k in range(heads)]).astype(jnp.int32)
        token_ids = q_ids[:, None] * tok + jnp.arange(tok, dtype=jnp.int32) + begin
        row_ids = q_ids[:, None] * cache_rows + jnp.arange(cache_rows, dtype=jnp.int32)
        angle = jnp.concatenate([token_ids, row_ids], 1).astype(jnp.float32)[..., None] * freq
        cosine, sine = jnp.cos(angle), jnp.sin(angle)
        return q_ids, jnp.concatenate([cosine, cosine], -1), jnp.concatenate([-sine, sine], -1)

    count = wide // FEATS
    groups = [[i * crew + j for j in range(crew)] for i in range(heads)]
    if squared:

        def sides(value, name):
            return swap(value, "tp", tp, 1, f"side_{name}")

        def line(value, name):
            return swap(value, "seq", seq, 2, f"line_{name}")

        def core(value, name):
            return swap(value, "seq", seq, 1, f"core_{name}")

        depth = w_qkv.shape[0]
        w_sent = [jnp.concatenate([w, folded(c)], 0) for w, c in zip(w_cut[:3], caches)]
        w_own = w_cut[0][None]
        w_1, w_2 = across(w_sent[1], 1, "w"), across(w_sent[2], 2, "w")
        far, next_x = across(own, 2, "x_far"), across(own, 1, "x_next")
        own_line = line(w_own, "w0")
        own_side = sides(after(own, own_line), "own")
        w_some, w_line, cache_2 = unpack([w_own], [w_2], depth, fold)
        w_line = line(w_line, "w2")
        w_some, w_mid, cache_1 = unpack([w_some], [w_1], depth, fold)
        cache_mid = (cache_1, cache_2)
        late, late_cache, _ = lax.optimization_barrier((plane, caches[3], own))
        w_sent_3 = jnp.concatenate([w_cut[3], folded(late_cache)], 0)
        q_ids, cosine, sine = tables(late)
        ids = jnp.arange(count, dtype=jnp.int32)
        x_ids = jnp.concatenate([side * count + ids, (1 - side) * count + ids])
        order = ((0, 0), (2, 0), (1, 0), (0, 2), (2, 2), (1, 2), (3, 0), (3, 2))
        w_ids = [(late ^ k) * crew + (inner ^ turn ^ flip) for flip in (0, 1) for k, turn in order]
        w_ids = jnp.stack(w_ids).astype(jnp.int32)
        kv_ids = [(late ^ k) * crew + (inner ^ turn) for k in range(heads) for turn in (0, 2, 1, 3)]
        kv_ids = jnp.stack(kv_ids).astype(jnp.int32)
        numbers = (q_ids, cosine, sine, x_ids, w_ids, kv_ids)
        lines = (own_line, w_line)
        own, own_side, next_x, far, w_some, w_mid, cache_mid, w_3, lines, numbers = (
            lax.optimization_barrier(
                (own, own_side, next_x, far, w_some, w_mid, cache_mid, w_sent_3, lines, numbers)
            )
        )
        q_ids, cosine, sine, x_ids, w_ids, kv_ids = numbers
        next_side, far_side = sides(next_x, "next"), sides(far, "far")
        w_3 = across(w_3, 3, "w")
        last = across(far, 1, "x_last")
        w_mid_line = line(w_mid, "w1")
        w_last, _, cache_last = unpack([], [w_3], depth, fold)
        w_last_line = line(w_last, "w3")
        w_some = join([w_some, *lines, w_mid_line])
        w_some_core = core(w_some, "w")
        last_low, far_high = half(last, 0), half(far_side, 1)
        moved = (last, next_side, far_side, w_last, w_last_line, w_some)
        moved, w_some_core, last_low, far_high = lax.optimization_barrier(
            (moved, w_some_core, last_low, far_high)
        )
        last, next_side, far_side, w_last, w_last_line, w_some = moved
        caches = [caches[0], *cache_mid, cache_last]
        last_side = [sides(last_low, "last"), across(far_high, 1, "x_last_side")]
        w_parts = [w_some, w_last, w_last_line]
        w_parts += [w_some_core, core(w_last, "w3"), core(w_last_line, "w3_line")]
        x_chunks = [[own, own_side], [next_x, next_side], [far, far_side], [last, *last_side]]
    else:
        q_ids, cosine, sine = tables(plane)
        caches = [across(c, k) for k, c in enumerate(caches)]
        members = [
            [(i * crew + j) * tp + t for i in range(heads) for t in range(tp)] for j in range(crew)
        ]
        x_all = lax.all_gather(own, ("seq", "tp"), axis=0, tiled=True, axis_index_groups=members)
        x_chunks = [
            [lax.dynamic_slice_in_dim(x_all, (plane ^ k) * count * tp, count * tp)]
            for k in range(heads)
        ]
        x_ids = jnp.arange(count * tp, dtype=jnp.int32)
        gathered = [
            lax.all_gather(across(w, k), "seq", axis=0, tiled=True, axis_index_groups=groups)
            for k, w in enumerate(w_cut)
        ]
        per = gathered[0].shape[0] // FEATS
        w_parts = [g.reshape(per, FEATS, WIDTH) for g in gathered]
        w_ids = jnp.concatenate(
            [(plane ^ k) * per + jnp.arange(per, dtype=jnp.int32) for k in range(heads)]
        )

    def projected(kv, q, slots):
        chunks = [x_chunks[k] for k in slots]
        some = [caches[k] for k in slots]
        return project(kv, q, slots[0], chunks, x_ids, w_parts, w_ids, cosine, sine, some, tok, redo)

    if squared:
        kv_new = [*projected(True, False, (0, 1, 2)), *projected(True, False, (3,))]
        for chunk in x_chunks:
            chunk[0] = after(chunk[0], kv_new[1])
        queries = [*projected(False, True, (0, 1, 2)), *projected(False, True, (3,))]
        first_queries = queries[0]
        queries = list(lax.optimization_barrier(tuple(queries)))
    else:
        kv_new, queries = [[value] for value in projected(True, True, tuple(range(heads)))]

    if squared:
        kv_parts, places = [], []
        fars = [swap(mine, "seq", seq, 2, "kv_line") for mine in kv_new]
        fars = lax.optimization_barrier((*fars, first_queries))
        for mine, far in zip(kv_new, fars):
            places += [(len(kv_parts) + n, i) for i in range(mine.shape[0]) for n in range(4)]
            kv_parts += [mine, far, core(mine, "kv"), core(far, "kv_line")]
    else:
        kv_parts = [
            lax.all_gather(kv_new[0][k : k + 1], "seq", axis=0, tiled=True, axis_index_groups=groups)
            for k in range(heads)
        ]
        places = [(k, i) for k in range(heads) for i in range(crew)]
        kv_ids = jnp.concatenate(
            [(plane ^ k) * crew + jnp.arange(crew, dtype=jnp.int32) for k in range(heads)]
        )

    back = [None] * heads
    for slots in ((3, 2), (1,), (0,)) if squared else tuple((k,) for k in range(heads)):
        some = [(queries[k // 3], k % 3) if squared else (queries[0], k) for k in slots]
        if squared and slots[0] < 3:
            earlier = back[3:] if slots == (0,) else []
            some = [(after(some[0][0], *mixed, *earlier), some[0][1])]
        mixed = attend(slots, prefix_len, some, q_ids, kv_parts, places, kv_ids, tok)
        for k, value in zip(slots, mixed):
            back[k] = across(value, k, "mixed")
    back = jnp.stack(back)
    columns = [lax.dynamic_index_in_dim(back, plane ^ h, 0, keepdims=False) for h in range(heads)]
    return jnp.concatenate(columns, 1)


def solution(mesh):
    placed = (
        P("seq", "tp"),
        P(),
        P("seq", "tp"),
        P(None, "seq", "tp"),
        P("seq", "tp"),
        P("seq"),
        P(),
    )
    return jax.shard_map(
        functools.partial(per_device, mesh.shape["seq"], mesh.shape["tp"]),
        mesh=mesh,
        in_specs=placed,
        out_specs=P("seq", "tp"),
        check_vma=False,
    )
```

```python
import functools
import math

import jax
import jax.numpy as jnp
from jax import lax
from jax.experimental import pallas as pl
from jax.experimental.pallas import tpu as pltpu
from jax.sharding import PartitionSpec as P

HEADS = 32
KVH = 8
HD = 128
GROUP = HEADS // KVH
WIDTH = (GROUP + 2) * HD
FEATS = 256
FAR = -1e30
VMEM = pl.BlockSpec(memory_space=pltpu.VMEM)
SMEM = pl.BlockSpec(memory_space=pltpu.SMEM)


def swap(value, axis, size, mask, name="move"):
    with jax.named_scope(name):
        return lax.ppermute(value, axis, [(i, i ^ mask) for i in range(size)])


def after(value, *earlier):
    return lax.optimization_barrier((value,) + earlier)[0]


def squares_kernel(stream, hidden, out):
    tok = stream.shape[0]
    for ref, first in ((stream, 0), (hidden, tok)):
        value = ref[...].astype(jnp.float32)
        total = jnp.sum(value * value, axis=-1, keepdims=True)
        out[first : first + value.shape[0]] = jnp.broadcast_to(total, (value.shape[0], HD))


def squares(stream, hidden):
    return pl.pallas_call(
        squares_kernel,
        out_shape=jax.ShapeDtypeStruct((stream.shape[0] + hidden.shape[0], HD), jnp.float32),
        in_specs=[VMEM] * 2,
        out_specs=VMEM,
        compiler_params=pltpu.CompilerParams(vmem_limit_bytes=8 * 2**20),
        cost_estimate=pl.CostEstimate(flops=1, bytes_accessed=1, transcendentals=0),
        name="squares",
    )(stream, hidden)


def norm_kernel(width, count, stream, hidden, gain, *refs):
    sums, out = refs[:count], refs[count]
    tok = stream.shape[0]
    factor = lax.rsqrt(sum(s[:, :1] for s in sums) / width + 1e-05)
    for ref, first in ((stream, 0), (hidden, tok)):
        last = first + ref.shape[0]
        for block in range(out.shape[0]):
            lanes = slice(block * FEATS, (block + 1) * FEATS)
            value = ref[:, lanes].astype(jnp.float32)
            value = value * factor[first:last] * gain[:, lanes]
            out[block, first:last] = value.astype(jnp.bfloat16)


def norm(stream, hidden, gain, sums, width):
    blocks = stream.shape[1] // FEATS
    rows = stream.shape[0] + hidden.shape[0]
    return pl.pallas_call(
        functools.partial(norm_kernel, width, len(sums)),
        out_shape=jax.ShapeDtypeStruct((blocks, rows, FEATS), jnp.bfloat16),
        in_specs=[VMEM] * (3 + len(sums)),
        out_specs=VMEM,
        compiler_params=pltpu.CompilerParams(vmem_limit_bytes=12 * 2**20),
        cost_estimate=pl.CostEstimate(flops=1, bytes_accessed=1, transcendentals=0),
        name="norm",
    )(stream, hidden, gain.reshape(1, -1), *sums)


def unpack_kernel(plain, fold, sources, *refs):
    sources, (whole, last, *caches) = refs[:sources], refs[sources:]
    depth = whole.shape[1]
    at = 0
    for n, source in enumerate(sources):
        if n < plain:
            whole[at : at + source.shape[0]] = source[...]
            at += source.shape[0]
            continue
        whole[at] = source[:depth]
        last[n - plain] = source[:depth]
        at += 1
        extra = source.shape[0] - depth
        for j in range(fold):
            lanes = slice(j * 2 * HD, (j + 1) * 2 * HD)
            caches[n - plain][j * extra : (j + 1) * extra] = source[depth:, lanes]


def unpack(plain, packed, depth, fold):
    extra = packed[0].shape[0] - depth
    count = sum(p.shape[0] for p in plain) + len(packed)
    return pl.pallas_call(
        functools.partial(unpack_kernel, len(plain), fold, len(plain) + len(packed)),
        out_shape=[
            jax.ShapeDtypeStruct((n, depth, WIDTH), jnp.bfloat16) for n in (count, len(packed))
        ]
        + [jax.ShapeDtypeStruct((fold * extra, 2 * HD), jnp.bfloat16)] * len(packed),
        in_specs=[VMEM] * (len(plain) + len(packed)),
        out_specs=[VMEM] * (2 + len(packed)),
        compiler_params=pltpu.CompilerParams(vmem_limit_bytes=12 * 2**20),
        cost_estimate=pl.CostEstimate(flops=2 * 10**10, bytes_accessed=10**7, transcendentals=0),
        name="unpack",
    )(*plain, *packed)


def join_kernel(*refs):
    at = 0
    for ref in refs[:-1]:
        refs[-1][at : at + ref.shape[0]] = ref[...]
        at += ref.shape[0]


def join(parts):
    count = sum(p.shape[0] for p in parts)
    return pl.pallas_call(
        join_kernel,
        out_shape=jax.ShapeDtypeStruct((count, *parts[0].shape[1:]), parts[0].dtype),
        in_specs=[VMEM] * len(parts),
        out_specs=VMEM,
        compiler_params=pltpu.CompilerParams(vmem_limit_bytes=12 * 2**20),
        name="join",
    )(*parts)


def half_kernel(value, out):
    out[...] = value[...]


def half(value, index):
    shape = (value.shape[0] // 2, *value.shape[1:])
    return pl.pallas_call(
        half_kernel,
        grid=(1,),
        out_shape=jax.ShapeDtypeStruct(shape, value.dtype),
        in_specs=[pl.BlockSpec(shape, lambda t: (index, 0, 0))],
        out_specs=pl.BlockSpec(shape, lambda t: (0, 0, 0)),
        compiler_params=pltpu.CompilerParams(vmem_limit_bytes=8 * 2**20),
        cost_estimate=pl.CostEstimate(flops=2 * 10**10, bytes_accessed=10**6, transcendentals=0),
        name="half",
    )(value)


def project_kernel(kv, tiles, first_slot, tok, redo, pitch, n_x, n_w, *refs):
    x_ids, w_ids = refs[:2]
    x_refs, refs = refs[2 : 2 + sum(n_x)], refs[2 + sum(n_x) :]
    w_refs, refs = refs[:n_w], refs[n_w:]
    chunks = len(n_x)
    cosine, sine, *refs = refs
    caches, outs, held = refs[: chunks * kv], list(refs[chunks * kv : -1]), refs[-1]
    kv_out = outs.pop(0) if kv else None
    q_out = outs.pop(0) if outs else None
    span = cosine.shape[1]
    cache_rows = span - tok

    @pl.when(pl.program_id(0) == 0)
    def _():
        first = 0
        for chunk, count in enumerate(n_x):
            at = 0
            for part in x_refs[first : first + count]:
                for block in range(part.shape[0]):
                    held[x_ids[at], chunk * pitch : chunk * pitch + tok + redo] = part[block]
                    at += 1
            first += count

    total = None
    at = 0
    for part in w_refs:
        for block in range(part.shape[0]):
            term = jnp.dot(held[w_ids[at]], part[block], preferred_element_type=jnp.float32)
            total = term if total is None else total + term
            at += 1

    def rotated(value, chunk, first, last):
        turned = pltpu.roll(value, HD // 2, 1)
        slot = first_slot + chunk
        return value * cosine[slot, first:last] + turned * sine[slot, first:last]

    def finish_queries():
        for chunk in range(chunks):
            for head in range(2):
                value = total[chunk * pitch : chunk * pitch + tok, head * HD : (head + 1) * HD]
                q_out[chunk, head] = rotated(value, chunk, 0, tok).astype(jnp.bfloat16)

    def finish_kv():
        for chunk in range(chunks):
            mine = total[chunk * pitch : chunk * pitch + tok + redo]
            keys = rotated(mine[:tok, :HD], chunk, 0, tok)
            kv_out[chunk, :tok] = jnp.concatenate([keys, mine[:tok, HD:]], 1).astype(jnp.bfloat16)
            cache = caches[chunk]
            offsets = cache[cache_rows : cache_rows + 1, :redo].astype(jnp.float32)
            row = lax.broadcasted_iota(jnp.int32, (cache_rows, redo), 0).astype(jnp.float32)
            chosen = (row == offsets).astype(jnp.float32)
            fresh = jnp.dot(
                chosen,
                mine[tok:],
                preferred_element_type=jnp.float32,
                precision=lax.Precision.HIGHEST,
            )
            turned = rotated(fresh[:, :HD], chunk, tok, span)
            fresh = jnp.concatenate([turned, fresh[:, HD:]], 1)
            hit = jnp.sum(chosen, axis=1, keepdims=True) > 0.5
            kept = cache[:cache_rows].astype(jnp.float32)
            kv_out[chunk, tok:] = jnp.where(hit, fresh, kept).astype(jnp.bfloat16)

    if kv and tiles > 1:
        pl.when(pl.program_id(0) == 0)(finish_kv)
        pl.when(pl.program_id(0) > 0)(finish_queries)
    elif kv:
        finish_kv()
    else:
        finish_queries()


def project(kv, q, first_slot, x_chunks, x_ids, w_parts, w_ids, cosine, sine, caches, tok, redo):
    chunks = len(x_chunks)
    blocks = sum(p.shape[0] for p in x_chunks[0])
    span = cosine.shape[1]
    pitch = -(-(tok + redo) // 16) * 16
    full = lambda a: pl.BlockSpec(a.shape, lambda t, n=a.ndim: (0,) * n)
    q_tiles = WIDTH // FEATS - 1
    tiles = kv + q * q_tiles
    w_spec = lambda a: pl.BlockSpec(
        (a.shape[0], FEATS, FEATS),
        lambda t: (0, 0, lax.rem(t + q_tiles, q_tiles + 1) if kv else t),
    )
    out_shape, out_specs = [], []
    if kv:
        out_shape.append(jax.ShapeDtypeStruct((chunks, span, 2 * HD), jnp.bfloat16))
        out_specs.append(full(out_shape[0]))
    else:
        caches = []
    if q:
        out_shape.append(jax.ShapeDtypeStruct((chunks, GROUP, tok, HD), jnp.bfloat16))
        out_specs.append(
            pl.BlockSpec((chunks, 2, tok, HD), lambda t: (0, jnp.maximum(t - kv, 0), 0, 0))
        )
    x_parts = [p for chunk in x_chunks for p in chunk]
    n_x = [len(chunk) for chunk in x_chunks]
    return pl.pallas_call(
        functools.partial(project_kernel, kv, tiles, first_slot, tok, redo, pitch, n_x, len(w_parts)),
        grid=(tiles,),
        out_shape=out_shape,
        in_specs=[SMEM, SMEM]
        + [full(a) for a in x_parts]
        + [w_spec(a) for a in w_parts]
        + [full(a) for a in (cosine, sine, *caches)],
        out_specs=out_specs,
        scratch_shapes=[pltpu.VMEM((blocks, chunks * pitch, FEATS), jnp.bfloat16)],
        compiler_params=pltpu.CompilerParams(vmem_limit_bytes=32 * 2**20),
        cost_estimate=pl.CostEstimate(
            flops=2 * chunks * pitch * blocks * FEATS * FEATS * tiles,
            bytes_accessed=2 * blocks * FEATS * (FEATS * tiles + chunks * pitch),
            transcendentals=0,
        ),
        name="_".join(["keys_values"] * kv + ["queries"] * q),
    )(x_ids, w_ids, *x_parts, *w_parts, cosine, sine, *caches)


def attend_kernel(slots, tok, places, *refs):
    begin_ref, q_ids, kv_ids = refs[:3]
    count = len(slots)
    q_refs, refs = refs[3 : 3 + count], refs[3 + count :]
    kv_refs, refs = refs[: -count - 4], refs[-count - 4 :]
    outs, (scores, top, total, accum) = refs[:count], refs[count:]
    begin = begin_ref[0]
    heads = GROUP * tok
    scale = math.log2(math.e) / math.sqrt(HD)
    span = kv_refs[0].shape[1]
    cache_rows = span - tok
    groups = []
    for at in range(0, len(places), 4):
        group = places[at : at + 4]
        ids = [kv_ids[at + i] for i in range(len(group))]
        least, most = functools.reduce(jnp.minimum, ids), functools.reduce(jnp.maximum, ids)
        groups.append((group, ids, least, most, at * span))

    for n, slot in enumerate(slots):
        q_id = q_ids[slot]
        top[...] = jnp.full(top.shape, FAR, jnp.float32)
        total[...] = jnp.zeros(total.shape, jnp.float32)
        accum[...] = jnp.zeros(accum.shape, jnp.float32)

        def rows(group, first, last, half):
            return jnp.concatenate(
                [kv_refs[r][i, first:last, half * HD : (half + 1) * HD] for r, i in group], 0
            )

        def score(column, keys, allowed, n=n):
            value = lax.dot_general(
                q_refs[n][0].reshape(heads, HD),
                keys,
                (((1,), (1,)), ((), ())),
                preferred_element_type=jnp.float32,
            )
            if allowed is not None:
                value = jnp.where(allowed(value.shape), value, FAR)
            scores[:, column : column + value.shape[1]] = value
            most = top[...]
            for lane in range(0, value.shape[1], HD):
                most = jnp.maximum(most, value[:, lane : lane + HD])
            top[...] = most

        def mix(column, values):
            weights = []
            some = total[...]
            most = top[...]
            for lane in range(0, values.shape[0], HD):
                part = scores[:, column + lane : column + lane + HD]
                weight = jnp.exp2(part * scale - most)
                some = some + weight
                weights.append(weight.astype(jnp.bfloat16))
            total[...] = some
            accum[...] += jnp.dot(
                jnp.concatenate(weights, 1), values, preferred_element_type=jnp.float32
            )

        for group, ids, least, most, base in groups:
            shift = len(group) * tok

            def starts(shape, step, ids=ids):
                column = lax.broadcasted_iota(jnp.int32, shape, 1)
                which = column // step
                first = jnp.zeros(shape, jnp.int32)
                for i, one in enumerate(ids):
                    first = jnp.where(which == i, one * step, first)
                return first + column % step

            def causal(shape, starts=starts):
                row = lax.broadcasted_iota(jnp.int32, (shape[0], 1), 0)
                return starts((1, shape[1]), tok) <= q_id * tok + row % tok

            def prefix(shape, starts=starts):
                return starts((1, shape[1]), cache_rows) < begin

            @pl.when((most + 1) * cache_rows <= begin)
            def _(group=group, base=base):
                score(base + shift, rows(group, tok, span, 0), None)

            @pl.when(((most + 1) * cache_rows > begin) & (least * cache_rows < begin))
            def _(group=group, prefix=prefix, base=base):
                score(base + shift, rows(group, tok, span, 0), prefix)

            @pl.when(most < q_id)
            def _(group=group, base=base):
                score(base, rows(group, 0, tok, 0), None)

            @pl.when((most >= q_id) & (least <= q_id))
            def _(group=group, causal=causal, base=base):
                score(base, rows(group, 0, tok, 0), causal)

        peak = jnp.max(top[...], axis=1, keepdims=True) * scale
        top[...] = jnp.broadcast_to(peak, top.shape)
        for group, ids, least, most, base in groups:
            shift = len(group) * tok

            @pl.when(least * cache_rows < begin)
            def _(group=group, base=base):
                mix(base + shift, rows(group, tok, span, 1))

            @pl.when(least <= q_id)
            def _(group=group, base=base):
                mix(base, rows(group, 0, tok, 1))

        mixed = (accum[...] / jnp.sum(total[...], axis=1, keepdims=True)).astype(jnp.bfloat16)
        for head in range(GROUP):
            outs[n][:, head * HD : (head + 1) * HD] = mixed[head * tok : (head + 1) * tok]


def attend(slots, begin, queries, q_ids, kv_parts, places, kv_ids, tok):
    span = kv_parts[0].shape[1]
    n_rows = len(places) * span
    heads = GROUP * tok
    q_specs = [pl.BlockSpec((1, GROUP, tok, HD), lambda t, i=i: (i, 0, 0, 0)) for _, i in queries]
    return pl.pallas_call(
        functools.partial(attend_kernel, slots, tok, places),
        grid=(1,),
        out_shape=[jax.ShapeDtypeStruct((tok, GROUP * HD), jnp.bfloat16)] * len(slots),
        in_specs=[SMEM, SMEM, SMEM] + q_specs + [VMEM] * len(kv_parts),
        out_specs=[VMEM] * len(slots),
        scratch_shapes=[
            pltpu.VMEM((heads, n_rows), jnp.float32),
            pltpu.VMEM((heads, HD), jnp.float32),
            pltpu.VMEM((heads, HD), jnp.float32),
            pltpu.VMEM((heads, HD), jnp.float32),
        ],
        compiler_params=pltpu.CompilerParams(vmem_limit_bytes=8 * 2**20 + 5 * heads * n_rows),
        cost_estimate=pl.CostEstimate(
            flops=4 * len(slots) * heads * n_rows * HD,
            bytes_accessed=4 * n_rows * HD,
            transcendentals=len(slots) * heads * n_rows,
        ),
        name="attend",
    )(begin, q_ids, kv_ids, *[q for q, _ in queries], *kv_parts)


def per_device(
    seq, tp, stream_x, norm_gain, w_qkv, cache_kv, recomp_hidden, recomp_index, prefix_len
):
    tok, redo = stream_x.shape[0], recomp_hidden.shape[0]
    cache_rows = cache_kv.shape[1]
    heads = w_qkv.shape[1] // WIDTH
    crew = seq // heads
    at, side = lax.axis_index("seq"), lax.axis_index("tp")
    plane, inner = at // crew, at % crew
    begin = prefix_len[0]
    squared = crew == 4 and heads == 4 and tp == 2

    def across(value, k, name="planes"):
        return swap(value, "seq", seq, k * crew, f"{name}_{k}") if k else value

    w_cut = [lax.dynamic_slice_in_dim(w_qkv, (plane ^ k) * WIDTH, WIDTH, 1) for k in range(heads)]
    stream_x, w_cut = lax.optimization_barrier((stream_x, w_cut))
    sums = squares(stream_x, recomp_hidden)
    wide = stream_x.shape[1]
    width = wide * tp
    gain = lax.dynamic_slice_in_dim(norm_gain, side * wide, wide)
    sums = [sums, swap(sums, "tp", tp, 1, "side_sums")] if squared else [lax.psum(sums, "tp")]
    own = norm(stream_x, recomp_hidden, gain, sums, width)

    offsets = (recomp_index - at * cache_rows).astype(jnp.bfloat16)
    fold = WIDTH // (2 * HD)
    extra = -(-(cache_rows + 1) // (16 * fold)) * 16
    offsets = jnp.pad(offsets[None, :], ((0, fold * extra - cache_rows - 1), (0, 2 * HD - redo)))
    caches = []
    for k in range(heads):
        part = lax.dynamic_slice_in_dim(cache_kv, (plane ^ k) * HD, HD, 2)
        part = jnp.concatenate([part[0], part[1]], 1)
        caches.append(jnp.concatenate([part, offsets], 0))

    def folded(cache):
        return jnp.concatenate([cache[i * extra : (i + 1) * extra] for i in range(fold)], 1)

    def tables(plane):
        half = HD // 2
        freq = jnp.exp(
            -math.log(1000000.0) * jnp.arange(half, dtype=jnp.float32) * 2.0 / (2 * half)
        )
        q_ids = jnp.stack([(plane ^ k) * crew + inner for k in range(heads)]).astype(jnp.int32)
        token_ids = q_ids[:, None] * tok + jnp.arange(tok, dtype=jnp.int32) + begin
        row_ids = q_ids[:, None] * cache_rows + jnp.arange(cache_rows, dtype=jnp.int32)
        angle = jnp.concatenate([token_ids, row_ids], 1).astype(jnp.float32)[..., None] * freq
        cosine, sine = jnp.cos(angle), jnp.sin(angle)
        return q_ids, jnp.concatenate([cosine, cosine], -1), jnp.concatenate([-sine, sine], -1)

    count = wide // FEATS
    groups = [[i * crew + j for j in range(crew)] for i in range(heads)]
    if squared:

        def sides(value, name):
            return swap(value, "tp", tp, 1, f"side_{name}")

        def line(value, name):
            return swap(value, "seq", seq, 2, f"line_{name}")

        def core(value, name):
            return swap(value, "seq", seq, 1, f"core_{name}")

        depth = w_qkv.shape[0]
        w_sent = [jnp.concatenate([w, folded(c)], 0) for w, c in zip(w_cut[:3], caches)]
        w_own = w_cut[0][None]
        w_1, w_2 = across(w_sent[1], 1, "w"), across(w_sent[2], 2, "w")
        far, next_x = across(own, 2, "x_far"), across(own, 1, "x_next")
        own_line = line(w_own, "w0")
        own_side = sides(after(own, own_line), "own")
        w_some, w_line, cache_2 = unpack([w_own], [w_2], depth, fold)
        w_line = line(w_line, "w2")
        w_some, w_mid, cache_1 = unpack([w_some], [w_1], depth, fold)
        cache_mid = (cache_1, cache_2)
        late, late_cache, _ = lax.optimization_barrier((plane, caches[3], own))
        w_sent_3 = jnp.concatenate([w_cut[3], folded(late_cache)], 0)
        q_ids, cosine, sine = tables(late)
        ids = jnp.arange(count, dtype=jnp.int32)
        x_ids = jnp.concatenate([side * count + ids, (1 - side) * count + ids])
        order = ((0, 0), (2, 0), (1, 0), (0, 2), (2, 2), (1, 2), (3, 0), (3, 2))
        w_ids = [(late ^ k) * crew + (inner ^ turn ^ flip) for flip in (0, 1) for k, turn in order]
        w_ids = jnp.stack(w_ids).astype(jnp.int32)
        kv_ids = [(late ^ k) * crew + (inner ^ turn) for k in range(heads) for turn in (0, 2, 1, 3)]
        kv_ids = jnp.stack(kv_ids).astype(jnp.int32)
        numbers = (q_ids, cosine, sine, x_ids, w_ids, kv_ids)
        lines = (own_line, w_line)
        own, own_side, next_x, far, w_some, w_mid, cache_mid, w_3, lines, numbers = (
            lax.optimization_barrier(
                (own, own_side, next_x, far, w_some, w_mid, cache_mid, w_sent_3, lines, numbers)
            )
        )
        q_ids, cosine, sine, x_ids, w_ids, kv_ids = numbers
        next_side, far_side = sides(next_x, "next"), sides(far, "far")
        w_3 = across(w_3, 3, "w")
        last = across(far, 1, "x_last")
        w_mid_line = line(w_mid, "w1")
        w_last, _, cache_last = unpack([], [w_3], depth, fold)
        w_last_line = line(w_last, "w3")
        w_some = join([w_some, *lines, w_mid_line])
        w_some_core = core(w_some, "w")
        last_low, far_high = half(last, 0), half(far_side, 1)
        moved = (last, next_side, far_side, w_last, w_last_line, w_some)
        moved, w_some_core, last_low, far_high = lax.optimization_barrier(
            (moved, w_some_core, last_low, far_high)
        )
        last, next_side, far_side, w_last, w_last_line, w_some = moved
        caches = [caches[0], *cache_mid, cache_last]
        last_side = [sides(last_low, "last"), across(far_high, 1, "x_last_side")]
        w_parts = [w_some, w_last, w_last_line]
        w_parts += [w_some_core, core(w_last, "w3"), core(w_last_line, "w3_line")]
        x_chunks = [[own, own_side], [next_x, next_side], [far, far_side], [last, *last_side]]
    else:
        q_ids, cosine, sine = tables(plane)
        caches = [across(c, k) for k, c in enumerate(caches)]
        members = [
            [(i * crew + j) * tp + t for i in range(heads) for t in range(tp)] for j in range(crew)
        ]
        x_all = lax.all_gather(own, ("seq", "tp"), axis=0, tiled=True, axis_index_groups=members)
        x_chunks = [
            [lax.dynamic_slice_in_dim(x_all, (plane ^ k) * count * tp, count * tp)]
            for k in range(heads)
        ]
        x_ids = jnp.arange(count * tp, dtype=jnp.int32)
        gathered = [
            lax.all_gather(across(w, k), "seq", axis=0, tiled=True, axis_index_groups=groups)
            for k, w in enumerate(w_cut)
        ]
        per = gathered[0].shape[0] // FEATS
        w_parts = [g.reshape(per, FEATS, WIDTH) for g in gathered]
        w_ids = jnp.concatenate(
            [(plane ^ k) * per + jnp.arange(per, dtype=jnp.int32) for k in range(heads)]
        )

    def projected(kv, q, slots):
        chunks = [x_chunks[k] for k in slots]
        some = [caches[k] for k in slots]
        return project(kv, q, slots[0], chunks, x_ids, w_parts, w_ids, cosine, sine, some, tok, redo)

    if squared:
        kv_new = projected(True, False, (0, 1, 2))
        x_chunks[0][0] = after(own, kv_new[0])
        queries = projected(False, True, (0, 1, 2))
        x_chunks[3][0] = after(last, queries[0])
        kv_new = [*kv_new, *projected(True, False, (3,))]
        x_chunks[3][0] = after(x_chunks[3][0], kv_new[1])
        queries = [*queries, *projected(False, True, (3,))]
        first_queries = queries[1]
        queries = list(lax.optimization_barrier(tuple(queries)))
    else:
        kv_new, queries = [[value] for value in projected(True, True, tuple(range(heads)))]

    if squared:
        kv_parts, places = [], []
        fars = [swap(mine, "seq", seq, 2, "kv_line") for mine in kv_new]
        fars = lax.optimization_barrier((*fars, first_queries))
        for mine, far in zip(kv_new, fars):
            places += [(len(kv_parts) + n, i) for i in range(mine.shape[0]) for n in range(4)]
            kv_parts += [mine, far, core(mine, "kv"), core(far, "kv_line")]
    else:
        kv_parts = [
            lax.all_gather(kv_new[0][k : k + 1], "seq", axis=0, tiled=True, axis_index_groups=groups)
            for k in range(heads)
        ]
        places = [(k, i) for k in range(heads) for i in range(crew)]
        kv_ids = jnp.concatenate(
            [(plane ^ k) * crew + jnp.arange(crew, dtype=jnp.int32) for k in range(heads)]
        )

    back = [None] * heads
    for slots in ((3, 2), (1,), (0,)) if squared else tuple((k,) for k in range(heads)):
        some = [(queries[k // 3], k % 3) if squared else (queries[0], k) for k in slots]
        if squared and slots[0] < 3:
            earlier = back[3:] if slots == (0,) else []
            some = [(after(some[0][0], *mixed, *earlier), some[0][1])]
        mixed = attend(slots, prefix_len, some, q_ids, kv_parts, places, kv_ids, tok)
        for k, value in zip(slots, mixed):
            back[k] = across(value, k, "mixed")
    back = jnp.stack(back)
    columns = [lax.dynamic_index_in_dim(back, plane ^ h, 0, keepdims=False) for h in range(heads)]
    return jnp.concatenate(columns, 1)


def solution(mesh):
    placed = (
        P("seq", "tp"),
        P(),
        P("seq", "tp"),
        P(None, "seq", "tp"),
        P("seq", "tp"),
        P("seq"),
        P(),
    )
    return jax.shard_map(
        functools.partial(per_device, mesh.shape["seq"], mesh.shape["tp"]),
        mesh=mesh,
        in_specs=placed,
        out_specs=P("seq", "tp"),
        check_vma=False,
    )
```
